32 devices in a mesh: section: 2 (over x), dp: 16 (over z, y, core).
Axes of the slice: x: 2, y: 2, z: 4, core: 2. Of those that a mesh axis runs over, the one named last changes fastest.
Arguments:
- tokens: bfloat16 [2, 16, 542, 768], P(None, 'dp'), may hold values from -6 to 6
- layout: int32 [2, 16, 6], P(None, 'dp'), may hold values from 0 to 1, as said below
- selected: int32 [2, 16, 384], P(None, 'dp'), may hold values from 0 to 541, as said below
- cotangent: bfloat16 [2, 16, 542, 768], P(None, 'dp'), may hold values from -6 to 6
- w_qkv: bfloat16 [2, 768, 2304], P('section'), may hold values from -0.21875 to 0.21875
- w_out: bfloat16 [2, 768, 768], P('section'), may hold values from -1.25 to 1.25
- w_up: bfloat16 [2, 768, 3072], P('section'), may hold values from -0.21875 to 0.21875
- w_down: bfloat16 [2, 3072, 768], P('section'), may hold values from -0.109375 to 0.109375
- norm_gain: float32 [2, 2, 768], P('section'), may hold values from 0.1 to 1.9
- norm_bias: float32 [2, 2, 768], P('section'), may hold values from -2 to 2
- w_router: float32 [768], replicated, may hold values from -0.21875 to 0.21875
Outputs:
- acts: bfloat16 [2, 2, 16, 542, 768], P('section', None, 'dp')
- input_grads: float32 [2, 2, 16, 542, 768], P('section', None, 'dp')
- grad_qkv: float32 [2, 768, 2304], P('section', 'dp')
- grad_out: float32 [2, 768, 768], P('section', 'dp')
- grad_up: float32 [2, 768, 3072], P('section', 'dp')
- grad_down: float32 [2, 3072, 768], P('section', 'dp')
- grad_gain: float32 [2, 2, 768], P('section', None, 'dp')
- grad_bias: float32 [2, 2, 768], P('section', None, 'dp')
- grad_router: float32 [768], replicated
- counts: int32 [2], replicated
The draws below stay inside these ranges and needn't reach their ends.
Inputs may be any that keep to these rules, and one draw needn't show every extreme that they name: `layout`: each row holds two 1s and four 0s, their order varying from row to row. `selected`: each row holds 384 distinct positions in rising order.
All inputs are finite; a program needn't handle non-finite values.
Results may differ from the reference program's by a relative error of at most 0.014.
Values may be sent and summed in bfloat16 or wider, within the bound.
A program may use at most 384 MiB of HBM per device.

```python
import math
import jax
import jax.numpy as jnp
from jax import lax

D = 768
HEADS = 12
HEAD_DIM = 64
FF = 3072
BIG_CROP = 197
SMALL_CROP = 37
ROW_LEN = 542
CAPACITY = 384
MB = 2
ROWS = 16


def draw_layout(key, part):
    key = jax.random.fold_in(key, 3)
    row_keys = jax.random.split(key, MB * ROWS)
    orders = jax.vmap(partial_order)(row_keys)
    return (orders < 2).astype(jnp.int32).reshape(MB, ROWS, 6)


def partial_order(row_key):
    return jax.random.permutation(row_key, 6)


def pick_positions(row_key):
    return jnp.sort(jax.random.permutation(row_key, ROW_LEN)[:CAPACITY])


def draw_selected(key, part):
    key = jax.random.fold_in(key, 5)
    row_keys = jax.random.split(key, MB * ROWS)
    return jax.vmap(pick_positions)(row_keys).astype(jnp.int32).reshape(MB, ROWS, CAPACITY)


def strengthened(drawn, own_key, source, target, shards_of, factor):
    def block_of(position):
        return (jnp.arange(drawn.shape[position]) // (drawn.shape[position] // shards_of)).reshape((-1,) + (1,) * (drawn.ndim - 1 - position))

    one_side = jax.random.permutation(own_key, shards_of)[block_of(target)]
    other_side = (block_of(target) + shards_of // 2) % shards_of
    return jnp.where((block_of(source) == one_side) | (block_of(source) == other_side), factor * drawn, drawn)


def steps_of(stream_key, extent, cuts, smallest, high):
    level, own = 1.0, jax.random.fold_in(stream_key, 6)
    for position, shards_of in cuts:
        draws = jnp.exp(jax.random.uniform(jax.random.fold_in(own, position), (shards_of,), jnp.float32, smallest / len(cuts), high / len(cuts)))
        level = level * jnp.repeat(draws, extent[position] // shards_of).reshape([-1 if axis == position else 1 for axis in range(len(extent))])
    return level


def bell_draw(stream_key, extent, spread, limit, cuts=(), kind=jnp.bfloat16):
    array = spread * jax.random.normal(stream_key, extent, jnp.float32)
    if cuts:
        array = array * steps_of(stream_key, extent, cuts, -0.22, 0.18)
    return jnp.clip(array, -limit, limit).astype(kind)


def bell_draw_with(rng, dims, deviation, limit, pieces, heavy, kind=jnp.bfloat16):
    array = deviation * jax.random.normal(rng, dims, jnp.float32)
    if pieces:
        array = array * steps_of(rng, dims, pieces, -0.22, 0.18)
    return jnp.clip(strengthened(array, jax.random.fold_in(rng, 3), *heavy), -limit, limit).astype(kind)


def setup_inputs(seed: int = 0) -> dict:
    key_of = jax.random.split(jax.random.key(seed), 12)
    tokens = bell_draw(key_of[0], (MB, ROWS, ROW_LEN, D), 1.0, 6.0, ((1, 16),))
    layout = draw_layout(jax.random.fold_in(key_of[11], 71), 0)
    selected = draw_selected(jax.random.fold_in(key_of[11], 71), 0)
    cotangent = bell_draw_with(key_of[3], (MB, ROWS, ROW_LEN, D), 1.0, 6.0, ((1, 16),), (1, 3, 16, 2.0))
    w_qkv = bell_draw(key_of[4], (2, D, 3 * D), D ** -0.5, 0.21875, ((0, 2),))
    w_out = bell_draw(key_of[5], (2, D, D), (D // 40) ** -0.5, 1.25, ((0, 2),))
    w_up = bell_draw(key_of[6], (2, D, FF), D ** -0.5, 0.21875, ((0, 2),))
    w_down = bell_draw(key_of[7], (2, FF, D), FF ** -0.5, 0.109375, ((0, 2),))
    norm_gain = jnp.clip(1.0 + 0.18 * jax.random.normal(key_of[8], (2, 2, D), jnp.float32), 0.1, 1.9)
    norm_bias = bell_draw(key_of[9], (2, 2, D), 0.3, 2.0, ((0, 2),), jnp.float32)
    w_router = bell_draw(key_of[10], (D,), D ** -0.5, 0.21875, (), jnp.float32)
    return {"tokens": tokens, "layout": layout, "selected": selected, "cotangent": cotangent, "w_qkv": w_qkv, "w_out": w_out, "w_up": w_up, "w_down": w_down, "norm_gain": norm_gain, "norm_bias": norm_bias, "w_router": w_router}


EPSILON = 1e-06
MASKED = -1e+30
HIGHEST = lax.Precision.HIGHEST

@jax.custom_vjp
def low(v):
    return lax.optimization_barrier(v.astype(jnp.bfloat16)).astype(jnp.float32)

@jax.custom_vjp
def low_back(v):
    return v

def low_keep(v):
    return (low(v), None)

def low_pass(kept, grad):
    return (grad,)

def back_keep(v):
    return (v, None)

def back_low(kept, grad):
    return (low(grad),)
low.defvjp(low_keep, low_pass)
low_back.defvjp(back_keep, back_low)

def matmul(left, right):
    return jnp.dot(left, right, precision=HIGHEST)

def segment_numbers(layout):
    lengths = jnp.where(layout == 1, BIG_CROP, SMALL_CROP).astype(jnp.int32)
    crop_ends = jnp.cumsum(lengths, axis=-1)
    places = jnp.arange(ROW_LEN, dtype=jnp.int32)
    return lax.optimization_barrier(jnp.sum((places[:, None] >= crop_ends[..., None, :]).astype(jnp.int32), axis=-1))

def gelu_value(upper_rows):
    return 0.5 * upper_rows * (1.0 + jax.scipy.special.erf(upper_rows * 0.7071067811865476))

def norm_apply(rows_in, gain_row, bias_row):
    centred = rows_in - lax.optimization_barrier(jnp.mean(rows_in, axis=-1, keepdims=True))
    inv_scale = lax.rsqrt(lax.optimization_barrier(jnp.mean(centred * centred, axis=-1, keepdims=True)) + EPSILON)
    return centred * inv_scale * gain_row + bias_row

def branch_apply(rows_in, seg_row, layer):
    w_qkv, w_out, w_up, w_down, norm_gain, norm_bias = layer
    row_count = rows_in.shape[0]
    first_norm = low(norm_apply(rows_in, norm_gain[0], norm_bias[0]))
    packed = low(low_back(matmul(first_norm, w_qkv))).reshape(row_count, 3, HEADS, HEAD_DIM)
    scores = jnp.einsum('qhd,khd->hqk', packed[:, 0], packed[:, 1], precision=HIGHEST) * (1.0 / math.sqrt(HEAD_DIM))
    same_crop = seg_row[:, None] == seg_row[None, :]
    scores = low_back(jnp.where(same_crop[None], scores, MASKED))
    soft_weights = jax.nn.softmax(scores, axis=-1)
    mixed_heads = jnp.einsum('hqk,khd->qhd', low(soft_weights), packed[:, 2], precision=HIGHEST)
    mixed_heads = low(low_back(mixed_heads.reshape(row_count, D)))
    attended = low_back(matmul(mixed_heads, w_out))
    hidden = rows_in + attended
    second_norm = low(norm_apply(hidden, norm_gain[1], norm_bias[1]))
    upper_rows = low_back(matmul(second_norm, w_up))
    active = low(gelu_value(upper_rows))
    return attended + low_back(matmul(active, w_down))

def reference(tokens, layout, selected, cotangent, w_qkv, w_out, w_up, w_down, norm_gain, norm_bias, w_router):
    segments = segment_numbers(layout)
    seg_rows = segments.reshape(-1, ROW_LEN)
    chosen_rows = selected.reshape(-1, CAPACITY)
    rows_all = tokens.astype(jnp.float32).reshape(-1, ROW_LEN, D)
    probe = jnp.zeros_like(rows_all)

    def forward(rows_all, probe, w_qkv, w_out, w_up, w_down, norm_gain, norm_bias, w_router):
        first_layer = (w_qkv[0], w_out[0], w_up[0], w_down[0], norm_gain[0], norm_bias[0])
        second_layer = (w_qkv[1], w_out[1], w_up[1], w_down[1], norm_gain[1], norm_bias[1])

        def one_row(items):
            row_in, probe_row, seg_row, chosen = items
            logits = matmul(row_in, w_router)
            gate_values = jax.nn.sigmoid(logits[chosen])
            branch = branch_apply(row_in[chosen], seg_row[chosen], first_layer)
            sent = low(low_back(row_in.at[chosen].add(gate_values[:, None] * branch)))
            section_in = sent + probe_row
            return (sent, section_in + branch_apply(section_in, seg_row, second_layer))
        return lax.map(jax.checkpoint(one_row), (rows_all, probe, seg_rows, chosen_rows))
    params = (w_qkv.astype(jnp.float32), w_out.astype(jnp.float32), w_up.astype(jnp.float32), w_down.astype(jnp.float32), norm_gain, norm_bias, w_router)
    (sent, final), pullback = jax.vjp(forward, rows_all, probe, *params)
    grads = pullback((jnp.zeros_like(sent), cotangent.astype(jnp.float32).reshape(final.shape)))
    whole = (2, MB, ROWS, ROW_LEN, D)
    acts = jnp.stack([sent, final]).astype(jnp.bfloat16).reshape(whole)
    input_grads = jnp.stack([grads[0], grads[1]]).reshape(whole)
    crop_kinds = jnp.take_along_axis(layout, segments, axis=-1)
    picked_kinds = jnp.take_along_axis(crop_kinds, selected, axis=-1)
    big_count = jnp.sum(picked_kinds).astype(jnp.int32)
    counts = jnp.stack([big_count, selected.size - big_count]).astype(jnp.int32)
    return (acts, input_grads, grads[2], grads[3], grads[4], grads[5], grads[6], grads[7], grads[8], counts)
```

```python
import functools

import jax
import jax.numpy as jnp
from jax import lax
from jax.experimental import pallas as pl
from jax.experimental.pallas import tpu as pltpu
from jax.sharding import PartitionSpec as P

D = 768
HEADS = 12
FF = 3072
BIG_CROP = 197
SMALL_CROP = 37
ROW_LEN = 542
CAPACITY = 384
FULL = 544
PAIR = 2 * FULL
SPARE = 160
QUAD = 256
SCALE = 0.125
EPSILON = 1e-06
MASKED = -1e30
BLOCK = 32
CHUNK = 768
SLOT_STARTS = (0, 197, 394, 431, 468, 505)
SLOTS = 16
SLOT_N1, SLOT_MIXED, SLOT_N2, SLOT_ACT, SLOT_GL, SLOT_DA, SLOT_DQKV, SLOT_DU = 0, 1, 2, 3, 7, 8, 9, 12
SHARD_ROWS = 576
STRIP = 48
STRIPS = SHARD_ROWS // STRIP
BLOCKS = ((8, 9, 10, 11, 4, 5, 6, 7, 3, 0, 1, 2), (4, 5, 6, 7, 3, 0, 1, 2, 8, 9, 10, 11))
AMOUNTS = ((4, 0, 2, 2, 0, 1, 2, 1), (3, 2, 2, 2, 2, 1, 0, 0))
SEQUENCE = ((8, 9, 10, 11, 4, 5, 6, 7, 3, 0, 1, 2), (4, 5, 6, 3, 7, 0, 1, 2, 8, 10, 11, 9))
YFIRST = ((8, 10, 11, 4, 5, 7, 3, 0, 1, 2), (4, 6, 3, 0, 1, 2, 8, 10, 11, 9))
EARLY = ((9, 6), (5, 7))
EARLY_BEGIN = ((0, 4), (0, 2))
LATE = len(YFIRST[0])
RING = 4
MESH_ID = pl.DeviceIdType.MESH
VMEM_LIMIT = 63 * 2**20 + 2**19

f32 = jnp.float32
bf16 = jnp.bfloat16
i32 = jnp.int32


def mm(left, right):
    return jnp.dot(left, right, preferred_element_type=f32)


def mm_t(left, right):
    return lax.dot_general(left, right, (((1,), (1,)), ((), ())), preferred_element_type=f32)


def t_mm(left, right):
    return lax.dot_general(left, right, (((0,), (0,)), ((), ())), preferred_element_type=f32)


def rows_loop(count, body, rolled=False):
    if not rolled:
        for start in range(0, count, BLOCK):
            body(pl.ds(start, BLOCK))
        return

    def some(i, _):
        for k in range(4):
            body(pl.ds(pl.multiple_of((4 * i + k) * BLOCK, BLOCK), BLOCK))
        return 0

    lax.fori_loop(0, count // (4 * BLOCK), some, 0)


def col_chunk(j):
    return pl.ds(pl.multiple_of(j * CHUNK, CHUNK), CHUNK)


def repeat(count, body, rolled):
    if rolled:
        lax.fori_loop(0, count, lambda i, _: (body(i), 0)[1], 0)
    else:
        for i in range(count):
            body(i)


def multiply_into(target, product, left, right, rolled, by_rows):
    if not rolled:
        target[...] = product(left[...], right[...])
        return

    def one(j):
        cols = pl.ds(pl.multiple_of(j * 256, 256), 256)
        target[:, cols] = product(left[...], right[cols, :] if by_rows else right[:, cols])

    repeat(3, one, True)


def normalised(rows):
    centred = rows - jnp.mean(rows, axis=-1, keepdims=True)
    inverse = lax.rsqrt(jnp.mean(centred * centred, axis=-1, keepdims=True) + EPSILON)
    return centred * inverse, inverse


def crop_table(layout, mb):
    start, bigs, smalls = jnp.int32(0), jnp.int32(0), jnp.int32(0)
    starts, moves, slots = [], [], []
    for crop in range(6):
        is_big = layout[mb, 0, crop]
        slot = jnp.where(is_big == 1, BIG_CROP * bigs, 2 * BIG_CROP + SMALL_CROP * smalls)
        starts.append(start)
        moves.append(slot - start)
        slots.append(slot)
        start = start + jnp.where(is_big == 1, BIG_CROP, SMALL_CROP)
        bigs = bigs + is_big
        smalls = smalls + 1 - is_big
    back = []
    for slot_start in SLOT_STARTS:
        value = jnp.int32(0)
        for crop in range(6):
            value = value - jnp.where(slots[crop] == slot_start, moves[crop], 0)
        back.append(value)
    return starts, moves, back


def to_slot(places, table):
    starts, moves, _ = table
    move = jnp.full(places.shape, moves[0], i32)
    for crop in range(1, 6):
        move = jnp.where(places >= starts[crop], moves[crop], move)
    return jnp.where(places < ROW_LEN, places + move, places)


def from_slot(places, table):
    move = jnp.full(places.shape, table[2][0], i32)
    for crop in range(1, 6):
        move = jnp.where(places >= SLOT_STARTS[crop], table[2][crop], move)
    return jnp.where(places < ROW_LEN, places + move, places)


def one_hot(mask):
    return jnp.where(mask, 1.0, 0.0).astype(bf16)


def lane_places(count):
    return lax.broadcasted_iota(i32, (1, count), 1)


def row_places(count):
    return lax.broadcasted_iota(i32, (count, 1), 0)


class Chosen:
    def __init__(self, chosen, layout, mb):
        self.table = crop_table(layout, mb)
        row = chosen[mb].astype(f32)
        self.column = jnp.transpose(jnp.broadcast_to(row, (8, CAPACITY)))[:, :1].astype(i32)
        self.slots = to_slot(self.column, self.table)

    def bounds(self):
        return [jnp.sum(jnp.where(self.slots < start, 1, 0)) for start in SLOT_STARTS[1:]]

    def taken(self, places):
        return jnp.max(jnp.where(self.column == places, 1, 0), axis=0, keepdims=True)

    def rank(self, slots):
        return jnp.sum(jnp.where(self.slots < slots, 1, 0), axis=0, keepdims=True)

    def picks(self, places, valid):
        rank = self.rank(to_slot(places, self.table))
        return one_hot((rank == row_places(CAPACITY)) & (self.taken(places) == 1) & valid)

    def spares(self, places):
        slots = to_slot(places, self.table)
        rank = slots - self.rank(slots)
        return one_hot((rank == row_places(SPARE)) & (self.taken(places) == 0) & (places < ROW_LEN))


def both_rows(mb):
    lanes = lane_places(PAIR)
    places = lanes // 2
    return places, (lanes - 2 * places == mb) & (places < ROW_LEN)


def crop_numbers(places, bounds):
    number = jnp.zeros(places.shape, i32)
    for bound in bounds:
        number = number + jnp.where(places >= bound, 1, 0)
    return number


def owned(numbers, kind):
    if kind == 0:
        return numbers == 0
    if kind == 1:
        return numbers == 1
    return numbers >= 2


def head_lanes(head, value):
    lanes = lane_places(QUAD)
    return jnp.where((lanes >= 64 * head) & (lanes < 64 * head + 64), value, 0.0).astype(bf16)


def quad(part, group):
    return pl.ds(pl.multiple_of(part * D + group * QUAD, QUAD), QUAD)


class Window:
    def __init__(self, kind, start, size, bounds):
        self.kind, self.rows, self.lanes = kind, pl.ds(start, size), slice(0, size)
        numbers = crop_numbers(start + row_places(size), bounds)
        self.start, self.size = start, size
        self.own = owned(numbers, kind)
        self.same = (numbers == crop_numbers(start + lane_places(size), bounds)) & self.own


    def log_row(self, lse, row):
        if len(lse.shape) == 3:
            return lse[self.kind, row : row + 1, self.lanes]
        return lse[pl.ds(row, 1), self.start : self.start + self.size]


def lse_by_row(lse, middle, bounds):
    def moved(kind, start):
        wide = jnp.concatenate([lse[kind], jnp.zeros((16, CAPACITY - 256), f32)], axis=1)
        return pltpu.roll(wide, start, axis=1)

    numbers = crop_numbers(lane_places(CAPACITY), bounds)
    later = jnp.where(numbers == 1, moved(1, middle), moved(2, 224))
    return jnp.where(numbers == 0, moved(0, 0), later)


def staggered(windows, bounds, first, second, third, rolled=False):
    heads = []
    for kind, start, size in windows:
        window = Window(kind, start, size, bounds)
        if rolled:

            def one(group, _):
                run_heads([(window, group, head) for head in range(4)], first, second, third)
                return 0

            lax.fori_loop(0, 3, one, 0)
        else:
            heads += [(window, group, head) for group in range(3) for head in range(4)]
    if heads:
        run_heads(heads, first, second, third)


def run_heads(heads, first, second, third):
    for t in range(len(heads) + 3):
        if t < len(heads):
            first(*heads[t])
        if 0 <= t - 2 < len(heads):
            second(*heads[t - 2])
        if 0 <= t - 3 < len(heads):
            third(*heads[t - 3])


def attention_forward(windows, bounds, qkv, mixed, lse, rolled=False):
    held = {}

    def first(window, group, head):
        rows = window.rows
        if head == 0:
            q4 = qkv[rows, quad(0, group)] * jnp.full((1, QUAD), SCALE, bf16)
            held[0] = q4, qkv[rows, quad(1, group)], jnp.transpose(qkv[rows, quad(2, group)])
        q4, k4, values = held[0]
        held[1, head] = mm_t(k4 * head_lanes(head, 1.0), q4), values

    def second(window, group, head):
        scores, values = held.pop((1, head))
        scores = jnp.where(window.same, scores, MASKED)
        top = jnp.max(scores, axis=0, keepdims=True)
        powers = jnp.exp(scores - top)
        power_sum = jnp.sum(powers, axis=0, keepdims=True)
        held[2, head] = (powers * (1.0 / power_sum)).astype(bf16), values
        row = 4 * group + head
        lse[window.kind, pl.ds(row, 1), window.lanes] = top + jnp.log(power_sum)

    def third(window, group, head):
        probs, values = held.pop((2, head))
        held[3, head] = mm(values[64 * head : 64 * head + 64, :], probs)
        if head == 3:
            total = jnp.transpose(jnp.concatenate([held.pop((3, k)) for k in range(4)], axis=0))
            old = mixed[window.rows, quad(0, group)].astype(f32)
            mixed[window.rows, quad(0, group)] = jnp.where(window.own, total, old).astype(bf16)

    staggered(windows, bounds, first, second, third, rolled)


def attention_backward(windows, bounds, qkv, grad_mixed, lse, grad_qkv, rolled=False):
    held = {}

    def first(window, group, head):
        rows = window.rows
        if head == 0:
            q4 = qkv[rows, quad(0, group)] * jnp.full((1, QUAD), SCALE, bf16)
            k4 = qkv[rows, quad(1, group)]
            held[0] = q4, k4, qkv[rows, quad(2, group)], grad_mixed[rows, quad(0, group)], jnp.transpose(k4)
        q4, k4, v4, g4, _ = held[0]
        lanes = head_lanes(head, 1.0)
        held[1, head] = mm_t(k4 * lanes, q4), mm_t(v4 * lanes, g4), held[0]

    def second(window, group, head):
        scores, grad_probs, whole = held.pop((1, head))
        row = 4 * group + head
        log_row = window.log_row(lse, row)
        probs = jnp.where(window.same, jnp.exp(scores - log_row), 0.0)
        spread = jnp.sum(probs * grad_probs, axis=0, keepdims=True)
        held[2, head] = probs.astype(bf16), (probs * (grad_probs - spread)).astype(bf16), whole

    def third(window, group, head):
        probs, grad_scores, (q4, _, _, g4, keys) = held.pop((2, head))
        lanes = head_lanes(head, 1.0)
        dv, dk = mm(probs, g4 * lanes), mm(grad_scores, q4 * lanes)
        dq = mm(keys[64 * head : 64 * head + 64, :], grad_scores)
        if head:
            dv, dk, dq = dv + held[3][0], dk + held[3][1], held[3][2] + [dq]
        else:
            dq = [dq]
        held[3] = dv, dk, dq
        if head == 3:
            dq = jnp.transpose(jnp.concatenate(dq, axis=0)) * SCALE
            for part, grad in enumerate((dq, dk, dv)):
                old = grad_qkv[window.rows, quad(part, group)].astype(f32)
                grad_qkv[window.rows, quad(part, group)] = jnp.where(window.own, grad, old).astype(bf16)

    staggered(windows, bounds, first, second, third, rolled)


def gelu_and_slope(u):
    power = jnp.exp(u * u * -0.5)
    cdf = 0.5 + 0.5 * lax.erf(u * 0.7071067811865476)
    return u * cdf, cdf + u * power * 0.3989422804014327


def norm_rows(count, x, gain_row, bias_row, out, rolled):
    def one(rows):
        z, _ = normalised(x[rows, :])
        out[rows, :] = (z * gain_row + bias_row).astype(bf16)

    rows_loop(count, one, rolled)


def project(s, w_qkv, rolled):
    def one(j):
        cols = col_chunk(j)
        s.qkv[:, cols] = mm(s.n1[...], w_qkv[:, cols]).astype(bf16)

    repeat(3, one, rolled)


def add_norm(count, x, gain_row, bias_row, s, rolled):
    def one(rows):
        hidden = x[rows, :] + s.att[rows, :]
        s.hidden[rows, :] = hidden
        z, _ = normalised(hidden)
        s.n2[rows, :] = (z * gain_row + bias_row).astype(bf16)

    rows_loop(count, one, rolled)


def feed_forward(count, s, w_up, w_down, rolled):
    def one(j):
        cols = col_chunk(j)
        upper = mm(s.n2[...], w_up[:, cols])
        for start in range(0, count, BLOCK):
            active, slope = gelu_and_slope(upper[start : start + BLOCK, :])
            s.act[start : start + BLOCK, cols] = active.astype(bf16)
            s.slope[start : start + BLOCK, cols] = slope.astype(bf16)

    repeat(FF // CHUNK, one, rolled)
    multiply_into(s.low, mm, s.act, w_down, rolled, False)


def branch_forward(count, windows, bounds, x, gain, bias, w, s, wait, send, rolled=False):
    w_qkv, w_out, w_up, w_down = w
    norm_rows(count, x, gain[0:1, :], bias[0:1, :], s.n1, rolled)
    send("n1")
    wait(0)
    project(s, w_qkv, rolled)
    send("qkv")
    attention_forward(windows, bounds, s.qkv, s.mixed, s.lse, rolled)
    send("mixed")
    wait(1)
    s.att[...] = mm(s.mixed[...], w_out[...])
    add_norm(count, x, gain[1:2, :], bias[1:2, :], s, rolled)
    send("n2")
    wait(2)
    wait(3)
    feed_forward(count, s, w_up, w_down, rolled)
    send("act")


def norm_backward(dn, z, inverse, gain_row):
    dz = dn * gain_row
    return inverse * (
        dz - jnp.mean(dz, axis=-1, keepdims=True) - z * jnp.mean(dz * z, axis=-1, keepdims=True)
    )


def fold(rows):
    total = rows[0:8, :]
    for k in range(8, BLOCK, 8):
        total = total + rows[k : k + 8, :]
    return total


def lower(count, s):
    def one(rows):
        s.gl[rows, :] = s.grad[rows, :].astype(bf16)

    rows_loop(count, one)


def feed_backward(count, s, w_up, w_down, wait, rolled=False):
    if rolled:
        for j in range(5):
            wait(j)

    def one(j):
        cols = col_chunk(j)
        if not rolled:
            wait(j)
        grad = mm_t(s.gl[...], w_down[cols, :])
        for start in range(0, count, BLOCK):
            slope = s.slope[start : start + BLOCK, cols].astype(f32)
            s.du[start : start + BLOCK, cols] = (grad[start : start + BLOCK, :] * slope).astype(bf16)

    repeat(FF // CHUNK, one, rolled)
    if not rolled:
        wait(4)
    multiply_into(s.low, mm_t, s.du, w_up, rolled, True)


def norm_two_backward(count, gain_row, s, rolled=False):
    s.sums[0:32, :] = jnp.zeros((32, D), f32)

    def one(rows):
        z, inverse = normalised(s.hidden[rows, :])
        dn = s.low[rows, :]
        dh = norm_backward(dn, z, inverse, gain_row)
        s.sums[8:16, :] += fold(dn * z)
        s.sums[24:32, :] += fold(dn)
        s.att[rows, :] = dh
        s.da[rows, :] = (s.grad[rows, :] + dh).astype(bf16)

    rows_loop(count, one, rolled)


def norm_one_backward(count, x, gain_row, s, rolled=False):
    def one(rows):
        z, inverse = normalised(x[rows, :].astype(f32))
        dn = s.low[rows, :]
        s.sums[0:8, :] += fold(dn * z)
        s.sums[16:24, :] += fold(dn)
        s.grad[rows, :] = s.att[rows, :] + norm_backward(dn, z, inverse, gain_row)

    rows_loop(count, one, rolled)


def branch_backward(count, windows, bounds, x, gain, w, s, wait, send, rolled=False):
    w_qkv, w_out, w_up, w_down = w
    lower(count, s)
    send("gl")
    feed_backward(count, s, w_up, w_down, wait, rolled)
    send("du")
    wait(5)
    norm_two_backward(count, gain[1:2, :], s, rolled)
    send("da")
    s.grad_mixed[...] = mm_t(s.da[...], w_out[...]).astype(bf16)
    attention_backward(windows, bounds, s.qkv, s.grad_mixed, s.lse_rows, s.grad_qkv, rolled)
    send("dqkv")
    wait(6)
    multiply_into(s.low, mm_t, s.grad_qkv, w_qkv, rolled, True)
    norm_one_backward(count, x, gain[0:1, :], s, rolled)


class Refs:
    def __init__(self, names, refs, constants):
        self.__dict__.update(zip(names, refs), **constants)


class Copies:
    def __init__(self, sems, first):
        self.sems, self.next, self.open = sems, first, []

    def start(self, source, target):
        copy = pltpu.make_async_copy(source, target, self.sems.at[self.next])
        self.next += 1
        copy.start()
        return copy

    def out(self, source, target):
        self.open.append(self.start(source, target))

    def finish(self):
        for copy in self.open:
            copy.wait()


def slot_rows(ops, slot, mb, count):
    return ops.at[slot, pl.ds(mb * count, count), :]


def send_slots(copies, ops, s, mb, count):
    wide = {"act": (SLOT_ACT, 4), "du": (SLOT_DU, 4), "dqkv": (SLOT_DQKV, 3)}
    flat = {"n1": SLOT_N1, "mixed": SLOT_MIXED, "n2": SLOT_N2, "gl": SLOT_GL, "da": SLOT_DA}

    def send(what):
        if what in flat:
            copies.out(getattr(s, what), slot_rows(ops, flat[what], mb, count))
        elif what in wide:
            source = {"act": "act", "du": "du", "dqkv": "grad_qkv"}[what]
            slot, parts = wide[what]
            for k in range(parts):
                copies.out(getattr(s, source).at[:, pl.ds(k * D, D)], slot_rows(ops, slot + k, mb, count))

    return send


def weight_scratch():
    return dict(
        v_qkv=pltpu.VMEM((D, 3 * D), bf16),
        v_out=pltpu.VMEM((D, D), bf16),
        v_up=pltpu.VMEM((D, FF), bf16),
        v_down=pltpu.VMEM((FF, D), bf16),
    )


def forward_scratch(count):
    return dict(
        n1=pltpu.VMEM((count, D), bf16),
        mixed=pltpu.VMEM((count, D), bf16),
        n2=pltpu.VMEM((count, D), bf16),
        act=pltpu.VMEM((count, FF), bf16),
    )


def shared_scratch(count):
    return dict(
        qkv=pltpu.VMEM((count, 3 * D), bf16),
        lse=pltpu.VMEM((3, 16, 256), f32),
        att=pltpu.VMEM((count, D), f32),
        hidden=pltpu.VMEM((count, D), f32),
        slope=pltpu.VMEM((count, FF), bf16),
        low=pltpu.VMEM((count, D), f32),
    )


def backward_scratch(count):
    return dict(
        grad=pltpu.VMEM((count, D), f32),
        gl=pltpu.VMEM((count, D), bf16),
        du=pltpu.VMEM((count, FF), bf16),
        da=pltpu.VMEM((count, D), bf16),
        grad_mixed=pltpu.VMEM((count, D), bf16),
        grad_qkv=pltpu.VMEM((count, 3 * D), bf16),
        sums=pltpu.VMEM((48, D), f32),
    )


def routed_bounds(column_slots):
    bounds = []
    for slot_start in SLOT_STARTS[1:]:
        bounds.append(jnp.sum(jnp.where(column_slots < slot_start, 1, 0)))
    return bounds


def routed_windows(bounds):
    middle = pl.multiple_of(jnp.minimum(bounds[0] // 16 * 16, 160), 16)
    return ((0, 0, 208), (1, middle, 224), (2, 224, 160))


FULL_BOUNDS = SLOT_STARTS[1:] + (ROW_LEN,)
FULL_WINDOWS = ((0, 0, 208), (1, 192, 208), (2, 384, 160))
FIXED_WINDOWS = ((0, 0, 208), (1, 32, 352), (2, 224, 160))


def flatten(target, source):
    target[PAIR - 16 :, :] = jnp.zeros((16, D), target.dtype)
    target[0 : 2 * ROW_LEN, :] = source[...].reshape(2 * ROW_LEN, D)


def parts_of(value):
    high = value.astype(bf16)
    return high, (value - high.astype(f32)).astype(bf16)


def launch(kernel, inputs, outputs, scratch, name, flops, collective_id=None, **constants):
    names = tuple(inputs) + tuple(outputs) + tuple(scratch)
    places = list(inputs)
    aliases = {}
    for k, (_, _, _, same) in enumerate(outputs.values()):
        if same is not None:
            aliases[places.index(same)] = k
    params = dict(vmem_limit_bytes=VMEM_LIMIT, has_side_effects=True)
    if collective_id is not None:
        params["collective_id"] = collective_id
    found = pl.pallas_call(
        lambda *refs: kernel(Refs(names, refs, constants)),
        out_shape=[jax.ShapeDtypeStruct(shape, kind) for shape, kind, _, _ in outputs.values()],
        in_specs=[pl.BlockSpec(memory_space=space) for _, space in inputs.values()],
        out_specs=[pl.BlockSpec(memory_space=space) for _, _, space, _ in outputs.values()],
        scratch_shapes=list(scratch.values()),
        input_output_aliases=aliases,
        compiler_params=pltpu.CompilerParams(**params),
        cost_estimate=pl.CostEstimate(flops=flops, bytes_accessed=30 * 2**20, transcendentals=0),
        name=name,
    )(*(array for array, _ in inputs.values()))
    return dict(zip(outputs, found))


def routed_forward_kernel(mb, r):
    w = (r.v_qkv, r.v_out, r.v_up, r.v_down)
    section = lax.axis_index("section")
    places, mine = both_rows(mb)

    @pl.when(section == 0)
    def _():
        copies = Copies(r.sems, 0)
        tok_in = copies.start(r.tokens, r.pair)
        loads = [copies.start(a, b) for a, b in zip((r.w_qkv, r.w_out, r.w_up, r.w_down), w)]
        chosen = Chosen(r.chosen, r.layout, mb)
        r.v_picks[...] = chosen.picks(places, mine)
        bounds = chosen.bounds()
        for k in range(5):
            r.bounds[0, k] = bounds[k]
        tok_in.wait()
        flatten(r.flat, r.pair)
        r.x[...] = mm(r.v_picks[...], r.flat[...])
        r.x_low[...] = r.x[...].astype(bf16)
        copies.out(r.x_low, r.st_x)
        slots = send_slots(copies, r.ops, r, mb, CAPACITY)

        def send(what):
            slots(what)
            if what == "qkv":
                copies.out(r.qkv, r.st_qkv)
            elif what == "mixed":
                r.lse_rows[...] = lse_by_row(r.lse, windows[1][1], bounds)
                copies.out(r.lse_rows, r.st_lse)
            elif what == "n2":
                copies.out(r.hidden, r.st_hidden)
            elif what == "act":
                copies.out(r.slope, r.st_slope)

        windows = routed_windows(bounds)
        branch_forward(
            CAPACITY, windows, bounds, r.x, r.gain, r.bias, w, r, lambda i: loads[i].wait(), send, mb == 1
        )
        router = r.router[...].reshape(1, D)

        def add(rows):
            branch = r.att[rows, :] + r.low[rows, :]
            r.low[rows, :] = branch
            here = r.x[rows, :]
            gates = jax.nn.sigmoid(jnp.sum(here * router, axis=-1, keepdims=True))
            r.y_low[rows, :] = (here + gates * branch).astype(bf16)

        rows_loop(CAPACITY, add)
        copies.out(r.y_low, r.y0p)
        copies.out(r.low, r.st_branch)
        copies.out(r.v_picks, r.picks_out)
        copies.finish()

    if mb == 0:
        @pl.when(section == 1)
        def _():
            copies = Copies(r.sems, 0)
            copies.start(r.tokens, r.pair).wait()
            flatten(r.flat, r.pair)
            copies.start(r.cotangent, r.pair).wait()
            flatten(r.flat_two, r.pair)
            for row in range(2):
                chosen = Chosen(r.chosen, r.layout, row)
                places, mine = both_rows(row)
                here = (to_slot(places, chosen.table) == row_places(FULL)) & mine
                fresh = here & (chosen.taken(places) == 0)
                r.v_x[row] = mm(one_hot(fresh), r.flat[...]).astype(bf16)
                r.v_cot[row] = mm(one_hot(here), r.flat_two[...]).astype(bf16)
                back = from_slot(lane_places(FULL), chosen.table)
                picks = chosen.picks(back, lane_places(FULL) < ROW_LEN)
                r.v_slot_picks[row] = picks
                r.v_spread[row] = jnp.transpose(picks)
                r.v_spares[row] = chosen.spares(back)
            for source, target in (
                (r.v_x, r.x_rest),
                (r.v_cot, r.cot),
                (r.v_slot_picks, r.slot_picks),
                (r.v_spread, r.spread),
                (r.v_spares, r.spares),
            ):
                copies.out(source, target)
            copies.finish()


def routed_outputs_kernel(r):
    @pl.when(lax.axis_index("section") == 0)
    def _():
        copies = Copies(r.sems, 0)
        loads = [
            copies.start(a, b)
            for a, b in (
                (r.tokens, r.pair), (r.picks_a, r.v_picks.at[0]), (r.picks_b, r.v_picks.at[1]),
                (r.y_a, r.v_y.at[0]), (r.y_b, r.v_y.at[1]),
            )
        ]
        for copy in loads:
            copy.wait()
        flatten(r.flat, r.pair)
        ones = jnp.ones((CAPACITY, 128), bf16)
        spread = t_mm(r.v_picks[0], r.v_y[0]) + t_mm(r.v_picks[1], r.v_y[1])
        is_in = (t_mm(r.v_picks[0], ones) + t_mm(r.v_picks[1], ones))[:, :1]
        result = jnp.where(is_in > 0.5, spread, r.flat[...].astype(f32)).astype(bf16)
        r.pair[...] = result[: 2 * ROW_LEN, :].reshape(ROW_LEN, 2, D)
        copies.out(r.pair, r.acts)
        copies.finish()


def full_kernel(mb, r):
    w = (r.v_qkv, r.v_out, r.v_up, r.v_down)

    @pl.when(lax.axis_index("section") == 1)
    def _():
        copies = Copies(r.sems, 0)
        first = [
            copies.start(a, b)
            for a, b in ((r.x_rest.at[mb], r.tok), (r.y0p, r.low_in), (r.spread.at[mb], r.v_spread))
        ]
        loads = [copies.start(a, b) for a, b in zip((r.w_qkv, r.w_out, r.w_up, r.w_down), w)]
        cot_in = copies.start(r.cot.at[mb], r.gl)
        picks_in = [copies.start(r.slot_picks.at[mb], r.v_picks), copies.start(r.spares.at[mb], r.v_spares)]
        for copy in first:
            copy.wait()
        r.x[...] = r.tok[...].astype(f32) + mm(r.v_spread[...], r.low_in[...])
        send = send_slots(copies, r.ops, r, mb, FULL)
        branch_forward(
            FULL, FULL_WINDOWS, FULL_BOUNDS, r.x, r.gain, r.bias, w, r, lambda i: loads[i].wait(), send
        )
        cot_in.wait()

        def add(rows):
            r.tok[rows, :] = (r.x[rows, :] + r.att[rows, :] + r.low[rows, :]).astype(bf16)
            r.grad[rows, :] = r.gl[rows, :].astype(f32)

        rows_loop(FULL, add)
        copies.out(r.tok, r.y1)
        r.lse_rows = r.lse
        branch_backward(FULL, FULL_WINDOWS, FULL_BOUNDS, r.x, r.gain, w, r, lambda i: None, send)
        r.sums[32:48, :] = jnp.zeros((16, D), f32)
        copies.out(r.sums, r.sums_out)

        def join(rows):
            total = r.gl[rows, :].astype(f32) + r.grad[rows, :]
            r.low[rows, :] = total
            r.high[rows, :] = total.astype(bf16)

        rows_loop(FULL, join)
        copies.out(r.low, r.dx)
        for copy in picks_in:
            copy.wait()
        r.v_sent[...] = mm(r.v_picks[...], r.high[...]).astype(bf16)
        copies.out(r.v_sent, r.sent)
        if mb == 0:
            r.v_sent_spares[...] = mm(r.v_spares[...], r.high[...]).astype(bf16)
            copies.out(r.v_sent_spares, r.sent_spares)
        copies.finish()


def placed_gradients(chosen, part, spare, out):
    places = lane_places(FULL)
    picks = chosen.picks(places, places < ROW_LEN)
    high, rest = parts_of(part[...])
    total = t_mm(picks, high) + t_mm(chosen.spares(places), spare[...]) + t_mm(picks, rest)
    out[...] = total[0:ROW_LEN, :].reshape(ROW_LEN, 1, D)


def gates_backward(r, bounds, rolled=False):
    router = r.router[...].reshape(1, D)
    r.sums[32:48, :] = jnp.zeros((16, D), f32)

    def gate(rows):
        here = r.x_low[rows, :].astype(f32)
        gates = jax.nn.sigmoid(jnp.sum(here * router, axis=-1, keepdims=True))
        dy = r.v_back[rows, :].astype(f32)
        slopes = jnp.sum(r.v_part[rows, :] * dy, axis=-1, keepdims=True) * gates * (1.0 - gates)
        r.grad[rows, :] = gates * dy
        r.sums[32:40, :] += fold(slopes * here)
        r.v_part[rows, :] = dy + slopes * router

    rows_loop(CAPACITY, gate, rolled)
    r.sums[40:41, :] = jnp.where(lane_places(D) == 0, bounds[1], 0).astype(f32)


def routed_backward_kernel(mb, r):
    w = (r.v_qkv, r.v_out, r.v_up, r.v_down)
    section = lax.axis_index("section")

    @pl.when(section == 0)
    def _():
        copies = Copies(r.sems, 0)

        def load(*pairs):
            return [copies.start(a, b) for a, b in pairs]

        first = load((r.back, r.v_back), (r.st_x, r.x_low), (r.st_branch, r.v_part))
        chunks = []
        for j in range(4):
            cols = pl.ds(j * CHUNK, CHUNK)
            chunks.append(
                load((r.w_down.at[cols, :], r.v_down.at[cols, :]), (r.st_slope.at[:, cols], r.slope.at[:, cols]))
            )
        chunks.append(load((r.w_up, r.v_up)))
        chunks.append(
            load((r.st_hidden, r.hidden), (r.w_out, r.v_out), (r.st_qkv, r.qkv), (r.st_lse, r.lse_rows))
        )
        chunks.append(load((r.w_qkv, r.v_qkv)))
        if mb == 0:
            spare_in = copies.start(r.back_spares, r.v_spares)
        bounds = [r.bounds[0, k] for k in range(5)]
        for copy in first:
            copy.wait()
        gates_backward(r, bounds)

        def wait(i):
            for copy in chunks[i]:
                copy.wait()

        send = send_slots(copies, r.ops, r, mb, CAPACITY)
        branch_backward(CAPACITY, FIXED_WINDOWS, bounds, r.x_low, r.gain, w, r, wait, send, True)
        copies.out(r.sums, r.sums_out)

        def join(rows):
            r.v_part[rows, :] += r.grad[rows, :]

        rows_loop(CAPACITY, join)
        if mb == 0:
            spare_in.wait()
            placed_gradients(Chosen(r.chosen, r.layout, 0), r.v_part, r.v_spares, r.row)
            copies.out(r.row, r.grads.at[0])
        else:
            copies.out(r.v_part, r.part)
        copies.finish()


def full_outputs_kernel(r):
    @pl.when(lax.axis_index("section") == 1)
    def _():
        copies = Copies(r.sems, 0)
        halves = (r.v_dx_a, r.v_dx_b)
        dx_in = [copies.start(r.dx_a, halves[0]), copies.start(r.dx_b, halves[1])]
        y_in = [copies.start(r.y1_a, r.v_y1.at[0]), copies.start(r.y1_b, r.v_y1.at[1])]
        dx_in[1].wait()
        chosen = Chosen(r.chosen, r.layout, 1)
        back = from_slot(lane_places(FULL), chosen.table)
        r.v_spares[...] = mm(chosen.spares(back), r.v_dx_b[...].astype(bf16)).astype(bf16)
        copies.out(r.v_spares, r.sent_spares)
        for copy in y_in:
            copy.wait()
        rows = row_places(PAIR)
        total = jnp.zeros((PAIR, D), f32)
        for row in range(2):
            table = crop_table(r.layout, row)
            slots = lane_places(FULL)
            target = jnp.where(slots < ROW_LEN, 2 * from_slot(slots, table) + row, -1)
            total = total + mm(one_hot(rows == target), r.v_y1[row])
        r.pair[...] = total[: 2 * ROW_LEN, :].reshape(ROW_LEN, 2, D).astype(bf16)
        copies.out(r.pair, r.acts)
        dx_in[0].wait()
        for row in range(2):
            table = crop_table(r.layout, row)
            slots = lane_places(FULL)
            move = one_hot((from_slot(slots, table) == row_places(FULL)) & (slots < ROW_LEN))
            high, rest = parts_of(halves[row][...])
            total = mm(move, high) + mm(move, rest)
            target = (r.row, r.row_two)[row]
            target[...] = total[0:ROW_LEN, :].reshape(ROW_LEN, 1, D)
            copies.out(target, r.grads.at[row])
        copies.finish()


def closing_kernel(r):
    def row_copy():
        return pltpu.make_async_copy(r.row, r.grads.at[1], r.sems.at[0])

    @pl.when(lax.axis_index("section") == 0)
    def _():
        placed_gradients(Chosen(r.chosen, r.layout, 1), r.rows, r.back_spares, r.row)
        row_copy().start()

    for name in ("qkv", "out", "up", "down"):
        getattr(r, "o_" + name)[...] = getattr(r, "g_" + name)[...]
    width = D // r.ways
    me = lax.axis_index("dp")
    turned = pltpu.roll(r.small[...], lax.rem(D - width * me, D), axis=1)
    r.o_gain[...] = turned[0:2, 0:width]
    r.o_bias[...] = turned[2:4, 0:width]
    r.o_router[...] = r.small[4, :]
    big = jnp.sum(r.small[5:6, :]).astype(i32)
    r.o_counts[0] = big
    r.o_counts[1] = 2 * CAPACITY * r.ways - big
    pl.when(lax.axis_index("section") == 0)(lambda: row_copy().wait())


def gradient_kernel(r):
    me = lax.axis_index("dp")
    zero = me - me
    section = lax.axis_index("section")
    routed, full = section == 0, section == 1
    c = lax.rem(me, 2)
    y = lax.rem(me // 2, 2)
    z = me // 4
    sibling = {"dp": me + 1 - 2 * c}
    beside = {"dp": me + 2 - 4 * y}
    above, below = {"dp": me + 4}, {"dp": me - 4}
    far = {"dp": me + 8 - 16 * (z // 2)}
    paired = {"dp": me + 4 - 8 * lax.rem(z, 2)}

    barrier = pltpu.get_barrier_semaphore()

    def greet(device):
        pl.semaphore_signal(barrier, inc=1, device_id=device, device_id_type=MESH_ID)

    for device in (sibling, beside, far):
        greet(device)
    pl.when(z > 0)(lambda: greet(below))
    pl.when(z < 3)(lambda: greet(above))
    pl.when(full)(lambda: greet({"section": 0}))

    def strip(k):
        return pl.ds(pl.multiple_of(k * STRIP, STRIP), STRIP)

    def remote(source, target, sems, index, device):
        return pltpu.make_async_remote_copy(
            source, target, sems.at[(0,) + index], sems.at[(1,) + index], device_id=device, device_id_type=MESH_ID
        )

    def listed(orders, n):
        found = []
        for order in orders:
            value = zero + order[0]
            for place, entry in enumerate(order[1:], 1):
                value = jnp.where(n == place, entry, value)
            found.append(value)
        return jnp.where(routed, found[0], found[1])

    def placed(orders, k):
        found = []
        for order in orders:
            value = zero
            for place, entry in enumerate(order):
                value = jnp.where(k == entry, place, value)
            found.append(value)
        return jnp.where(routed, found[0], found[1])

    def block_at(n):
        return listed(BLOCKS, n)

    def place_of(k):
        return placed(SEQUENCE, k)

    def late(a):
        return listed(YFIRST, a)

    def early(b):
        return jnp.where(routed, EARLY[0][b], EARLY[1][b])

    def early_begin(b):
        return jnp.where(routed, EARLY_BEGIN[0][b], EARLY_BEGIN[1][b])

    def core_copy(k):
        slot = lax.rem(place_of(k), RING)
        return remote(r.part.at[:, :, 1 - c, strip(k), :], r.core_in.at[slot], r.core_sem, (k,), sibling)

    def side_copy(a):
        return remote(r.part.at[:, 1 - y, c, strip(late(a)), :], r.side_in.at[:, strip(a), :], r.side_sem, (a,), beside)

    def up_send(s, a):
        return remote(
            r.part.at[s, y, c, strip(late(a)), :], r.up_in.at[s - z - 1, strip(a), :], r.up_sem, (s, a), above
        )

    def up_take(s, a):
        return remote(r.part.at[s, y, c, strip(late(a)), :], r.up_in.at[s - z, strip(a), :], r.up_sem, (s, a), below)

    def down_send(s, a):
        return remote(
            r.part.at[s, y, c, strip(late(a)), :], r.down_in.at[z - 1 - s, strip(a), :], r.down_sem, (s, a), below
        )

    def down_take(s, a):
        return remote(
            r.part.at[s, y, c, strip(late(a)), :], r.down_in.at[z - s, strip(a), :], r.down_sem, (s, a), above
        )

    def early_rows(b):
        return strip(early(b))

    def early_up_send(s, b):
        return remote(
            r.part.at[s, :, c, early_rows(b), :], r.early_up.at[b, s - z - 1], r.early_sem, (0, s, b), above
        )

    def early_up_take(s, b):
        return remote(r.part.at[s, :, c, early_rows(b), :], r.early_up.at[b, s - z], r.early_sem, (0, s, b), below)

    def early_down_send(s, b):
        return remote(
            r.part.at[s, :, c, early_rows(b), :], r.early_down.at[b, z - 1 - s], r.early_sem, (1, s, b), below
        )

    def early_down_take(s, b):
        return remote(r.part.at[s, :, c, early_rows(b), :], r.early_down.at[b, z - s], r.early_sem, (1, s, b), above)

    def early_side(b):
        return remote(
            r.part.at[z, 1 - y, c, early_rows(b), :], r.early_side.at[b], r.early_side_sem, (b,), beside
        )

    def small_copy(k):
        device = (sibling, beside, paired, far)[k]
        return remote(r.small.at[k], r.small_in.at[k], r.small_sem, (k,), device)

    def across():
        return remote(r.small.at[4], r.cross_in, r.cross_sem, (), {"section": 1})

    s = Refs((), (), dict(r.__dict__, gl=r.grad_mixed, du=r.slope, v_back=r.da))
    v_out = r.v_down.at[pl.ds(0, D), :]
    v_qkv = r.v_up.at[:, pl.ds(0, 3 * D)]
    bounds = [r.bounds[0, k] for k in range(5)]

    def load(k, source, target):
        return pltpu.make_async_copy(source, target, r.sems.at[k])

    first = [load(0, r.back, r.da), load(1, r.st_x, r.x_low), load(2, r.st_branch, r.v_part)]
    middle = [load(12, r.st_hidden, r.hidden), load(13, r.st_qkv, r.qkv), load(14, r.st_lse, r.lse_rows)]
    again = [load(15, r.w_out, v_out), load(16, r.w_qkv, v_qkv)]
    feed_in = [load(3, r.w_down, r.v_down), load(4, r.st_slope, r.slope), load(5, r.w_up, r.v_up)]
    part_out = load(17, r.v_part, r.part_rows)

    def each(copies, act):
        for copy in copies:
            getattr(copy, act)()

    def thirds(target, left, right):
        def one(j, _):
            cols = pl.ds(pl.multiple_of(j * 256, 256), 256)
            target[:, cols] = mm_t(left[...], right[cols, :])
            return 0

        lax.fori_loop(0, 3, one, 0)

    def phase_feed():
        each(feed_in, "wait")

        def one(j, _):
            cols = pl.ds(pl.multiple_of(j * CHUNK, CHUNK), CHUNK)
            grad = mm_t(s.gl[...], r.v_down[cols, :])
            for start in range(0, CAPACITY, BLOCK):
                slope = r.slope[start : start + BLOCK, cols].astype(f32)
                r.slope[start : start + BLOCK, cols] = (grad[start : start + BLOCK, :] * slope).astype(bf16)
            return 0

        lax.fori_loop(0, 4, one, 0)
        thirds(r.low, s.du, r.v_up)
        each(again, "start")

    def phase_norm():
        each(middle, "wait")
        norm_two_backward(CAPACITY, r.gain[1:2, :], s, True)
        again[0].wait()
        r.grad_mixed[...] = mm_t(r.da[...], v_out[...]).astype(bf16)

    def phase_window(*kinds):
        windows = [FIXED_WINDOWS[kind] for kind in kinds]
        attention_backward(windows, bounds, r.qkv, r.grad_mixed, r.lse_rows, r.grad_qkv, True)

    def phase_last():
        again[1].wait()
        thirds(r.low, r.grad_qkv, v_qkv)
        norm_one_backward(CAPACITY, r.x_low, r.gain[0:1, :], s, True)

        def join(rows):
            r.v_part[rows, :] += r.grad[rows, :]

        rows_loop(CAPACITY, join, True)
        part_out.start()

    def slot_pair(b):
        left = jnp.where(b < 3, SLOT_N1, jnp.where(b == 3, SLOT_MIXED, jnp.where(b < 8, SLOT_N2, b - 8 + SLOT_ACT)))
        right = jnp.where(b < 3, b + SLOT_DQKV, jnp.where(b == 3, SLOT_DA, jnp.where(b < 8, b - 4 + SLOT_DU, SLOT_GL)))
        return left, right

    def operand_copies(n, left_rows, right_rows):
        left, right = slot_pair(block_at(n))
        side = lax.rem(n, 2)
        return (
            pltpu.make_async_copy(r.ops.at[left, 0:left_rows, :], r.left.at[side, 0:left_rows, :], r.load_sem.at[0, side]),
            pltpu.make_async_copy(
                r.ops.at[right, 0:right_rows, :], r.right.at[side, 0:right_rows, :], r.load_sem.at[1, side]
            ),
        )

    def operands(n, act):
        pl.when(routed)(lambda: each(operand_copies(n, 2 * CAPACITY, CAPACITY), act))
        pl.when(full)(lambda: each(operand_copies(n, 2 * FULL, 2 * FULL), act))

    def block(n):
        side = lax.rem(n, 2)
        b = block_at(n)
        operands(n, "wait")
        pl.when(n + 1 < STRIPS)(lambda: operands(n + 1, "start"))
        second = pl.ds(CAPACITY, CAPACITY)

        @pl.when(routed)
        def _():
            @pl.when(b >= 8)
            def _():
                r.right[side, second, :] = s.gl[...]

            @pl.when((b >= 4) & (b < 8))
            def _():
                r.right[side, second, :] = s.du[:, pl.ds(pl.multiple_of((b - 4) * D, D), D)]

            @pl.when(b == 3)
            def _():
                r.right[side, second, :] = r.da[...]

            @pl.when(b < 3)
            def _():
                r.right[side, second, :] = r.grad_qkv[:, pl.ds(pl.multiple_of(b * D, D), D)]

        def multiply(rows):
            def half(h, _):
                cols = pl.ds(pl.multiple_of(h * 384, 384), 384)
                product = t_mm(r.left[side, 0:rows, cols], r.right[side, 0:rows, :]).astype(bf16)

                @pl.when(b < 8)
                def _():
                    r.part[pl.ds(2 * h, 2), :, :, strip(b), :] = product.reshape(2, 2, 2, STRIP, D)

                @pl.when(b >= 8)
                def _():
                    r.part[b - 8, h, :, 384:576, :] = product.reshape(2, 192, D)

                return 0

            lax.fori_loop(0, 2, half, 0)

        pl.when(routed)(lambda: multiply(2 * CAPACITY))
        pl.when(full)(lambda: multiply(2 * FULL))
        pl.when(full & (n < 3))(lambda: core_start(b))

        @pl.when(routed & (n == 3))
        def _():
            for k in SEQUENCE[0][:3]:
                core_start(zero + k)

    def core_start(k):
        n = place_of(k)
        pl.when(n >= RING)(lambda: pl.semaphore_wait(r.free_sem.at[lax.rem(n, RING)], 1))
        core_copy(k).start()

    def add_into(target, source):
        (a, ia), (b, ib) = target, source
        a[ia] = (a[ia].astype(f32) + b[ib].astype(f32)).astype(bf16)

    def write(k, value):
        @pl.when(k < 3)
        def _():
            r.g_qkv[:, pl.ds(pl.multiple_of(k * D, D), D)] = value

        @pl.when(k == 3)
        def _():
            r.g_out[...] = value

        @pl.when((k > 3) & (k < 8))
        def _():
            r.g_up[:, pl.ds(pl.multiple_of((k - 4) * D, D), D)] = value

        @pl.when(k >= 8)
        def _():
            r.g_down[strip(k - 8), :] = value

    def core_arrived(k):
        n = place_of(k)
        slot = lax.rem(n, RING)
        core_copy(k).wait_recv()

        def one(i, _):
            zs, ys = i // 2, lax.rem(i, 2)
            add_into((r.part, (zs, ys, c, strip(k))), (r.core_in, (slot, zs, ys)))
            return 0

        lax.fori_loop(0, 8, one, 0)

        @pl.when(n + RING < STRIPS)
        def _():
            pl.semaphore_signal(r.free_sem.at[slot], inc=1, device_id=sibling, device_id_type=MESH_ID)

    def early_strip(b, t):
        rows, begin = early_rows(b), early_begin(b)
        pl.when(t == begin)(lambda: core_arrived(early(b)))

        @pl.when((t == begin + 2 * z) & (z < 3))
        def _():
            def one(i, _):
                k = 3 - i

                @pl.when(z > 0)
                def _():
                    early_up_take(k, b).wait_recv()
                    for ys in range(2):
                        add_into((r.part, (k, ys, c, rows)), (r.early_up, (b, k - z, ys)))

                early_up_send(k, b).start()
                return 0

            lax.fori_loop(0, 3 - z, one, 0)

        @pl.when((t == begin + 6 - 2 * z) & (z > 0))
        def _():
            def one(k, _):
                @pl.when(z < 3)
                def _():
                    early_down_take(k, b).wait_recv()
                    for ys in range(2):
                        add_into((r.part, (k, ys, c, rows)), (r.early_down, (b, z - k, ys)))

                early_down_send(k, b).start()
                return 0

            lax.fori_loop(0, z, one, 0)

        @pl.when(t == begin + 8)
        def _():
            @pl.when(z > 0)
            def _():
                early_up_take(z, b).wait_recv()
                for ys in range(2):
                    add_into((r.part, (z, ys, c, rows)), (r.early_up, (b, 0, ys)))

            @pl.when(z < 3)
            def _():
                early_down_take(z, b).wait_recv()
                for ys in range(2):
                    add_into((r.part, (z, ys, c, rows)), (r.early_down, (b, 0, ys)))

            early_side(b).start()

        @pl.when(t == begin + 10)
        def _():
            early_side(b).wait_recv()
            write(early(b), r.part[z, y, c, rows, :].astype(f32) + r.early_side[b].astype(f32))

    def serve(t):
        @pl.when((t >= 0) & (t < LATE))
        def _():
            core_arrived(late(t))
            side_copy(t).start()

        for b in range(2):
            early_strip(b, t)

        @pl.when((t >= 2) & (t < LATE + 2))
        def _():
            a = t - 2
            side_copy(a).wait_recv()

            def one(zs, _):
                add_into((r.part, (zs, y, c, strip(late(a)))), (r.side_in, (zs, strip(a))))
                return 0

            lax.fori_loop(0, 4, one, 0)

        au = t - 2 - 2 * z

        @pl.when((au >= 0) & (au < LATE) & (z < 3))
        def _():
            def one(i, _):
                k = 3 - i

                @pl.when(z > 0)
                def _():
                    up_take(k, au).wait_recv()
                    add_into((r.part, (k, y, c, strip(late(au)))), (r.up_in, (k - z, strip(au))))

                up_send(k, au).start()
                return 0

            lax.fori_loop(0, 3 - z, one, 0)

        ad = t - 8 + 2 * z

        @pl.when((ad >= 0) & (ad < LATE) & (z > 0))
        def _():
            def one(k, _):
                @pl.when(z < 3)
                def _():
                    down_take(k, ad).wait_recv()
                    add_into((r.part, (k, y, c, strip(late(ad)))), (r.down_in, (z - k, strip(ad))))

                down_send(k, ad).start()
                return 0

            lax.fori_loop(0, z, one, 0)

        @pl.when((t >= 8) & (t < LATE + 8))
        def _():
            a = t - 8
            r.final[...] = r.part[z, y, c, strip(late(a)), :].astype(f32)

            @pl.when(z > 0)
            def _():
                up_take(z, a).wait_recv()
                r.final[...] += r.up_in[0, strip(a), :].astype(f32)

            @pl.when(z < 3)
            def _():
                down_take(z, a).wait_recv()
                r.final[...] += r.down_in[0, strip(a), :].astype(f32)

            write(late(a), r.final[...])

        @pl.when(t == 5)
        def _():
            pl.when(full)(lambda: copy_sums())
            for k in range(6):
                rows = slice(8 * k, 8 * k + 8)
                r.small[0, k : k + 1, :] = jnp.sum(r.sums_a[rows, :] + r.sums[rows, :], axis=0, keepdims=True)
            r.small[0, 6:8, :] = jnp.zeros((2, D), f32)
            small_copy(0).start()

        for k in range(4):

            @pl.when(t == 2 * k + 7)
            def _():
                small_copy(k).wait_recv()
                r.small[k + 1] = r.small[k] + r.small_in[k]
                if k < 3:
                    small_copy(k + 1).start()
                else:
                    pl.when(routed)(lambda: across().start())

    def copy_sums():
        r.sums[...] = r.sums_b[...]

    @pl.when(routed)
    def _():
        each(first, "start")

    operands(zero, "start")

    @pl.when(routed)
    def _():
        each(feed_in + middle, "start")
        each(first, "wait")
        gates_backward(s, bounds, True)

        def one(rows):
            s.gl[rows, :] = r.grad[rows, :].astype(bf16)

        rows_loop(CAPACITY, one, True)

    pl.semaphore_wait(barrier, 3 + (z > 0).astype(i32) + (z < 3).astype(i32) + routed.astype(i32))

    def step(turn, _):
        t = turn - 1
        serve(t)
        begin = zero
        for place in range(1, len(AMOUNTS[0])):
            done = [sum(amounts[:place]) for amounts in AMOUNTS]
            begin = jnp.where(turn == place, jnp.where(routed, done[0], done[1]), begin)
        amount = jnp.where(turn < len(AMOUNTS[0]), listed(AMOUNTS, turn), 0)
        lax.fori_loop(0, amount, lambda i, _: (block(begin + i), 0)[1], 0)

        @pl.when((t >= 0) & (t < LATE - 2))
        def _():
            core_start(late(t + 2))
            for b in range(2):
                pl.when(t + 2 == early_begin(b))(lambda b=b: core_start(early(b)))

        pl.when(routed & (t == 0))(phase_feed)
        pl.when(routed & (t == 1))(phase_norm)
        pl.when(routed & (t == 2))(lambda: phase_window(0, 2))
        pl.when(routed & (t == 3))(lambda: phase_window(1))
        pl.when(routed & (t == 4))(phase_last)
        return 0

    lax.fori_loop(0, LATE + 9, step, 0)
    r.small_out[...] = r.small[4]


    @pl.when(routed)
    def _():
        across().wait_send()
        part_out.wait()

    @pl.when(full)
    def _():
        across().wait_recv()
        r.small_out[4:6, :] = r.cross_in[4:6, :]


    lax.fori_loop(0, STRIPS, lambda k, _: (core_copy(k).wait_send(), 0)[1], 0)

    def drain(a, _):
        side_copy(a).wait_send()
        for k in range(1, 4):
            pl.when(k > z)(lambda k=k: up_send(k, a).wait_send())
        for k in range(3):
            pl.when(k < z)(lambda k=k: down_send(k, a).wait_send())
        return 0

    lax.fori_loop(0, LATE, drain, 0)
    for b in range(2):
        early_side(b).wait_send()
        for k in range(1, 4):
            pl.when(k > z)(lambda k=k: early_up_send(k, b).wait_send())
        for k in range(3):
            pl.when(k < z)(lambda k=k: early_down_send(k, b).wait_send())
    for k in range(4):
        small_copy(k).wait_send()


HBM = pl.ANY
VMEM = pltpu.VMEM
SMEM = pltpu.SMEM


def body(
    tokens, layout, selected, cotangent, w_qkv, w_out, w_up, w_down, norm_gain, norm_bias, w_router
):
    ways = lax.axis_size("dp")
    common = dict(
        layout=(layout, SMEM),
        chosen=(selected, VMEM),
        gain=(norm_gain[0], VMEM),
        bias=(norm_bias[0], VMEM),
        router=(w_router, VMEM),
        w_qkv=(w_qkv[0], HBM),
        w_out=(w_out[0], HBM),
        w_up=(w_up[0], HBM),
        w_down=(w_down[0], HBM),
    )
    tokens = jnp.transpose(tokens, (1, 2, 0, 3)).reshape(ROW_LEN, 2, D)
    cotangent = jnp.transpose(cotangent, (1, 2, 0, 3)).reshape(ROW_LEN, 2, D)
    ops_spec = ((SLOTS, 2 * FULL, D), bf16, HBM)
    acts_spec = ((ROW_LEN, 2, D), bf16, HBM)
    grads_spec = ((2, ROW_LEN, 1, D), f32, HBM)
    stash_spec = dict(
        st_x=((CAPACITY, D), bf16, HBM, None),
        st_qkv=((CAPACITY, 3 * D), bf16, HBM, None),
        st_slope=((CAPACITY, FF), bf16, HBM, None),
        st_hidden=((CAPACITY, D), f32, HBM, None),
        st_branch=((CAPACITY, D), f32, HBM, None),
        st_lse=((16, CAPACITY), f32, HBM, None),
        bounds=((1, 8), i32, SMEM, None),
    )
    laid_spec = dict(
        x_rest=((2, FULL, D), bf16, HBM, None),
        cot=((2, FULL, D), bf16, HBM, None),
        slot_picks=((2, CAPACITY, FULL), bf16, HBM, None),
        spread=((2, FULL, CAPACITY), bf16, HBM, None),
        spares=((2, SPARE, FULL), bf16, HBM, None),
    )
    buffers = dict(sems=pltpu.SemaphoreType.DMA((40,)), **weight_scratch())
    ops = None
    handed, stashes, picks, y0ps = [], [], [], []
    for mb in range(2):
        inputs = dict(common, tokens=(tokens, HBM), cotangent=(cotangent, HBM))
        outputs = dict(
            ops=ops_spec + ("ops_old" if mb else None,), y0p=((CAPACITY, D), bf16, HBM, None), **stash_spec
        )
        scratch = dict(
            **buffers,
            pair=pltpu.VMEM((ROW_LEN, 2, D), bf16),
            flat=pltpu.VMEM((PAIR, D), bf16),
            v_picks=pltpu.VMEM((CAPACITY, PAIR), bf16),
            x=pltpu.VMEM((CAPACITY, D), f32),
            x_low=pltpu.VMEM((CAPACITY, D), bf16),
            lse_rows=pltpu.VMEM((16, CAPACITY), f32),
            y_low=pltpu.VMEM((CAPACITY, D), bf16),
            **forward_scratch(CAPACITY),
            **shared_scratch(CAPACITY),
        )
        outputs.update(picks_out=((CAPACITY, PAIR), bf16, HBM, None))
        if mb == 0:
            outputs.update(laid_spec)
            scratch.update(
                flat_two=pltpu.VMEM((PAIR, D), bf16),
                v_x=pltpu.VMEM((2, FULL, D), bf16),
                v_cot=pltpu.VMEM((2, FULL, D), bf16),
                v_slot_picks=pltpu.VMEM((2, CAPACITY, FULL), bf16),
                v_spread=pltpu.VMEM((2, FULL, CAPACITY), bf16),
                v_spares=pltpu.VMEM((2, SPARE, FULL), bf16),
            )
        else:
            inputs.update(ops_old=(ops, HBM))
        found = launch(
            functools.partial(routed_forward_kernel, mb), inputs, outputs, scratch, f"routed_forward_{mb}", 6 * 10**9
        )
        ops, y0p = found["ops"], found["y0p"]
        if mb == 0:
            laid = {name: (found[name], HBM) for name in laid_spec}
        picks.append(found["picks_out"])
        y0ps.append(y0p)
        stashes.append({name: (found[name], SMEM if name == "bounds" else HBM) for name in stash_spec})
        handed.append(lax.ppermute(y0p, "section", [(0, 1)]))
    acts = launch(
        routed_outputs_kernel,
        dict(
            tokens=(tokens, HBM), picks_a=(picks[0], HBM), picks_b=(picks[1], HBM), y_a=(y0ps[0], HBM), y_b=(y0ps[1], HBM)
        ),
        dict(acts=acts_spec + (None,)),
        dict(
            sems=pltpu.SemaphoreType.DMA((8,)),
            pair=pltpu.VMEM((ROW_LEN, 2, D), bf16),
            flat=pltpu.VMEM((PAIR, D), bf16),
            v_picks=pltpu.VMEM((2, CAPACITY, PAIR), bf16),
            v_y=pltpu.VMEM((2, CAPACITY, D), bf16),
        ),
        "routed_outputs",
        10**9,
    )["acts"]
    sums, returned, ends = [], [], []
    for mb in range(2):
        outputs = dict(
            ops=ops_spec + ("ops_old",),
            sent=((CAPACITY, D), bf16, HBM, None),
            y1=((FULL, D), bf16, HBM, None),
            dx=((FULL, D), f32, HBM, None),
            sums_out=((48, D), f32, HBM, None),
        )
        if mb == 0:
            outputs.update(sent_spares=((SPARE, D), bf16, HBM, None))
        found = launch(
            functools.partial(full_kernel, mb),
            dict(common, **laid, y0p=(handed[mb], HBM), ops_old=(ops, HBM)),
            outputs,
            dict(
                **buffers,
                tok=pltpu.VMEM((FULL, D), bf16),
                x=pltpu.VMEM((FULL, D), f32),
                low_in=pltpu.VMEM((CAPACITY, D), bf16),
                v_spread=pltpu.VMEM((FULL, CAPACITY), bf16),
                v_picks=pltpu.VMEM((CAPACITY, FULL), bf16),
                v_spares=pltpu.VMEM((SPARE, FULL), bf16),
                high=pltpu.VMEM((FULL, D), bf16),
                v_sent=pltpu.VMEM((CAPACITY, D), bf16),
                v_sent_spares=pltpu.VMEM((SPARE, D), bf16),
                **forward_scratch(FULL),
                **shared_scratch(FULL),
                **backward_scratch(FULL),
            ),
            f"full_{mb}",
            20 * 10**9,
        )
        ops = found["ops"]
        sums.append(found["sums_out"])
        ends.append((found["y1"], found["dx"]))
        returned.append(lax.ppermute(found["sent"], "section", [(1, 0)]))
        if mb == 0:
            back_spares = lax.ppermute(found["sent_spares"], "section", [(1, 0)])
    for mb in range(1 if ways == 16 else 2):
        inputs = dict(
            common, back=(returned[mb], HBM), **stashes[mb], ops_old=(ops, HBM), sums_old=(sums[mb], HBM)
        )
        outputs = dict(ops=ops_spec + ("ops_old",), sums_out=((48, D), f32, HBM, "sums_old"))
        scratch = dict(
            **buffers,
            x_low=pltpu.VMEM((CAPACITY, D), bf16),
            v_back=pltpu.VMEM((CAPACITY, D), bf16),
            v_part=pltpu.VMEM((CAPACITY, D), f32),
            lse_rows=pltpu.VMEM((16, CAPACITY), f32),
            **shared_scratch(CAPACITY),
            **backward_scratch(CAPACITY),
        )
        if mb == 0:
            inputs.update(back_spares=(back_spares, HBM))
            outputs.update(grads=grads_spec + (None,))
            scratch.update(v_spares=pltpu.VMEM((SPARE, D), bf16), row=pltpu.VMEM((ROW_LEN, 1, D), f32))
        else:
            outputs.update(part=((CAPACITY, D), f32, HBM, None))
        found = launch(
            functools.partial(routed_backward_kernel, mb), inputs, outputs, scratch, f"routed_backward_{mb}", 7 * 10**9
        )
        ops, sums[mb] = found["ops"], found["sums_out"]
        if mb == 0:
            grads = found["grads"]
            ends = launch(
                full_outputs_kernel,
                dict(
                    layout=(layout, SMEM), chosen=(selected, VMEM), y1_a=(ends[0][0], HBM), y1_b=(ends[1][0], HBM),
                    dx_a=(ends[0][1], HBM), dx_b=(ends[1][1], HBM), acts_old=(acts, HBM), grads_old=(grads, HBM),
                ),
                dict(
                    acts=acts_spec + ("acts_old",), grads=grads_spec + ("grads_old",),
                    sent_spares=((SPARE, D), bf16, HBM, None),
                ),
                dict(
                    sems=pltpu.SemaphoreType.DMA((16,)),
                    v_spares=pltpu.VMEM((SPARE, D), bf16),
                    v_dx_a=pltpu.VMEM((FULL, D), f32),
                    v_dx_b=pltpu.VMEM((FULL, D), f32),
                    v_y1=pltpu.VMEM((2, FULL, D), bf16),
                    pair=pltpu.VMEM((ROW_LEN, 2, D), bf16),
                    row=pltpu.VMEM((ROW_LEN, 1, D), f32),
                    row_two=pltpu.VMEM((ROW_LEN, 1, D), f32),
                ),
                "full_outputs",
                4 * 10**9,
            )
            acts, grads = ends["acts"], ends["grads"]
            back_spares = lax.ppermute(ends["sent_spares"], "section", [(1, 0)])
    if ways == 16:
        shares, small, rows = summed_by_kernel(ops, sums, dict(common, back=(returned[1], HBM), **stashes[1]))
    else:
        rows = found["part"]
        shares, small = summed_by_collectives(ops, sums, ways)
    found = launch(
        closing_kernel,
        dict(
            small=(small, VMEM), rows=(rows, VMEM), back_spares=(back_spares, VMEM), grads_old=(grads, HBM),
            layout=(layout, SMEM), chosen=(selected, VMEM),
            **{"g_" + name: (share, VMEM) for name, share in shares.items()},
        ),
        dict(
            grads=grads_spec + ("grads_old",),
            o_gain=((2, D // ways), f32, VMEM, None),
            o_bias=((2, D // ways), f32, VMEM, None),
            o_router=((D,), f32, VMEM, None),
            o_counts=((2,), i32, SMEM, None),
            **{"o_" + name: (share.shape, f32, VMEM, None) for name, share in shares.items()},
        ),
        dict(sems=pltpu.SemaphoreType.DMA((4,)), row=pltpu.VMEM((ROW_LEN, 1, D), f32)),
        "closing",
        10**9,
        ways=ways,
    )
    return (
        jnp.transpose(acts.reshape(1, ROW_LEN, 2, D), (2, 0, 1, 3))[None],
        found["grads"].reshape(1, 2, 1, ROW_LEN, D),
        found["o_qkv"][None],
        found["o_out"][None],
        found["o_up"][None],
        found["o_down"][None],
        found["o_gain"][None],
        found["o_bias"][None],
        found["o_router"],
        found["o_counts"],
    )


def summed_by_kernel(ops, sums, routed):
    found = launch(
        gradient_kernel,
        dict(routed, ops=(ops, HBM), sums_a=(sums[0], VMEM), sums_b=(sums[1], VMEM)),
        dict(
            g_qkv=((STRIP, 3 * D), f32, VMEM, None),
            g_out=((STRIP, D), f32, VMEM, None),
            g_up=((STRIP, FF), f32, VMEM, None),
            g_down=((4 * STRIP, D), f32, VMEM, None),
            small_out=((8, D), f32, VMEM, None),
            part_rows=((CAPACITY, D), f32, HBM, None),
        ),
        dict(
            left=pltpu.VMEM((2, 2 * FULL, D), bf16),
            right=pltpu.VMEM((2, 2 * FULL, D), bf16),
            part=pltpu.VMEM((4, 2, 2, SHARD_ROWS, D), bf16),
            core_in=pltpu.VMEM((RING, 4, 2, STRIP, D), bf16),
            side_in=pltpu.VMEM((4, LATE * STRIP, D), bf16),
            up_in=pltpu.VMEM((3, LATE * STRIP, D), bf16),
            down_in=pltpu.VMEM((3, LATE * STRIP, D), bf16),
            early_up=pltpu.VMEM((2, 3, 2, STRIP, D), bf16),
            early_down=pltpu.VMEM((2, 3, 2, STRIP, D), bf16),
            early_side=pltpu.VMEM((2, STRIP, D), bf16),
            final=pltpu.VMEM((STRIP, D), f32),
            small=pltpu.VMEM((5, 8, D), f32),
            small_in=pltpu.VMEM((4, 8, D), f32),
            cross_in=pltpu.VMEM((8, D), f32),
            cross_sem=pltpu.SemaphoreType.DMA((2,)),
            v_up=pltpu.VMEM((D, FF), bf16),
            v_down=pltpu.VMEM((FF, D), bf16),
            x_low=pltpu.VMEM((CAPACITY, D), bf16),
            v_part=pltpu.VMEM((CAPACITY, D), f32),
            lse_rows=pltpu.VMEM((16, CAPACITY), f32),
            **shared_scratch(CAPACITY),
            grad=pltpu.VMEM((CAPACITY, D), f32),
            da=pltpu.VMEM((CAPACITY, D), bf16),
            grad_mixed=pltpu.VMEM((CAPACITY, D), bf16),
            grad_qkv=pltpu.VMEM((CAPACITY, 3 * D), bf16),
            sums=pltpu.VMEM((48, D), f32),
            sems=pltpu.SemaphoreType.DMA((18,)),
            load_sem=pltpu.SemaphoreType.DMA((2, 2)),
            core_sem=pltpu.SemaphoreType.DMA((2, STRIPS)),
            side_sem=pltpu.SemaphoreType.DMA((2, LATE)),
            up_sem=pltpu.SemaphoreType.DMA((2, 4, LATE)),
            down_sem=pltpu.SemaphoreType.DMA((2, 4, LATE)),
            early_sem=pltpu.SemaphoreType.DMA((2, 2, 4, 2)),
            early_side_sem=pltpu.SemaphoreType.DMA((2, 2)),
            small_sem=pltpu.SemaphoreType.DMA((2, 4)),
            free_sem=pltpu.SemaphoreType.REGULAR((RING,)),
        ),
        "gradients",
        20 * 10**9,
        collective_id=0,
    )
    shares = {name: found["g_" + name] for name in ("qkv", "out", "up", "down")}
    return shares, found["small_out"], found["part_rows"]


def summed_by_collectives(ops, sums, count):
    first = lax.axis_index("section") == 0
    used = jnp.where(first, 2 * CAPACITY, 2 * FULL)
    ops = jnp.where(lax.broadcasted_iota(i32, (1, 2 * FULL, 1), 1) < used, ops, 0)

    def gradient(left, lefts, right, rights):
        a = jnp.concatenate([ops[left + k] for k in range(lefts)], axis=1)
        b = jnp.concatenate([ops[right + k] for k in range(rights)], axis=1)
        return lax.psum_scatter(t_mm(a, b), "dp", scatter_dimension=0, tiled=True)

    shares = dict(
        qkv=gradient(SLOT_N1, 1, SLOT_DQKV, 3),
        out=gradient(SLOT_MIXED, 1, SLOT_DA, 1),
        up=gradient(SLOT_N2, 1, SLOT_DU, 4),
        down=gradient(SLOT_ACT, 4, SLOT_GL, 1),
    )
    small = jnp.sum((sums[0] + sums[1]).reshape(6, 8, D), axis=1)
    small = jnp.concatenate([small, jnp.zeros((2, D), f32)])
    small = lax.psum(small, "dp")
    shared = lax.psum(jnp.where(first, small[4:6], 0.0), "section")
    return shares, jnp.concatenate([small[:4], shared, small[6:]])


def solution(mesh):
    return jax.shard_map(
        body,
        mesh=mesh,
        in_specs=(
            P(None, "dp", None, None),
            P(None, "dp", None),
            P(None, "dp", None),
            P(None, "dp", None, None),
            P("section", None, None),
            P("section", None, None),
            P("section", None, None),
            P("section", None, None),
            P("section", None, None),
            P("section", None, None),
            P(),
        ),
        out_specs=(
            P("section", None, "dp", None, None),
            P("section", None, "dp", None, None),
            P("section", "dp", None),
            P("section", "dp", None),
            P("section", "dp", None),
            P("section", "dp", None),
            P("section", None, "dp"),
            P("section", None, "dp"),
            P(),
            P(),
        ),
        check_vma=False,
    )
```

```python
import functools

import jax
import jax.numpy as jnp
from jax import lax
from jax.experimental import pallas as pl
from jax.experimental.pallas import tpu as pltpu
from jax.sharding import PartitionSpec as P

D = 768
HEADS = 12
FF = 3072
BIG_CROP = 197
SMALL_CROP = 37
ROW_LEN = 542
CAPACITY = 384
FULL = 544
PAIR = 2 * FULL
SPARE = 160
QUAD = 256
SCALE = 0.125
EPSILON = 1e-06
MASKED = -1e30
BLOCK = 32
CHUNK = 768
SLOT_STARTS = (0, 197, 394, 431, 468, 505)
SLOTS = 16
SLOT_N1, SLOT_MIXED, SLOT_N2, SLOT_ACT, SLOT_GL, SLOT_DA, SLOT_DQKV, SLOT_DU = 0, 1, 2, 3, 7, 8, 9, 12
SHARD_ROWS = 576
STRIP = 48
STRIPS = SHARD_ROWS // STRIP
BLOCKS = ((8, 9, 10, 11, 4, 5, 6, 7, 3, 0, 1, 2), (4, 5, 6, 7, 3, 0, 1, 2, 8, 9, 10, 11))
AMOUNTS = ((4, 0, 3, 0, 0, 2, 0, 1, 1, 1), (2, 1, 2, 2, 2, 2, 1, 0, 0, 0))
YFIRST = ((8, 10, 4, 5, 6, 3, 0, 1, 2), (5, 7, 3, 0, 1, 2, 8, 9, 10))
YCOUNT = ((0, 2, 0, 1, 2, 0, 1, 0, 1, 1, 0, 1), (0, 0, 1, 2, 2, 1, 0, 2, 1, 0, 0, 0))
EARLY = ((11, 9, 7), (6, 4, 11))
EARLY_BEGIN = ((1, 0, 7), (1, 0, 6))
PHASES = (0, 1, 3, 4, 5)
LATE, HASTE = len(YFIRST[0]), len(EARLY[0])
RING = 4
MESH_ID = pl.DeviceIdType.MESH
VMEM_LIMIT = 63 * 2**20 + 2**19

f32 = jnp.float32
bf16 = jnp.bfloat16
i32 = jnp.int32


def mm(left, right):
    return jnp.dot(left, right, preferred_element_type=f32)


def mm_t(left, right):
    return lax.dot_general(left, right, (((1,), (1,)), ((), ())), preferred_element_type=f32)


def t_mm(left, right):
    return lax.dot_general(left, right, (((0,), (0,)), ((), ())), preferred_element_type=f32)


def rows_loop(count, body, rolled=False):
    if not rolled:
        for start in range(0, count, BLOCK):
            body(pl.ds(start, BLOCK))
        return

    def some(i, _):
        for k in range(4):
            body(pl.ds(pl.multiple_of((4 * i + k) * BLOCK, BLOCK), BLOCK))
        return 0

    lax.fori_loop(0, count // (4 * BLOCK), some, 0)


def col_chunk(j):
    return pl.ds(pl.multiple_of(j * CHUNK, CHUNK), CHUNK)


def repeat(count, body, rolled):
    if rolled:
        lax.fori_loop(0, count, lambda i, _: (body(i), 0)[1], 0)
    else:
        for i in range(count):
            body(i)


def multiply_into(target, product, left, right, rolled, by_rows):
    if not rolled:
        target[...] = product(left[...], right[...])
        return

    def one(j):
        cols = pl.ds(pl.multiple_of(j * 256, 256), 256)
        target[:, cols] = product(left[...], right[cols, :] if by_rows else right[:, cols])

    repeat(3, one, True)


def normalised(rows):
    centred = rows - jnp.mean(rows, axis=-1, keepdims=True)
    inverse = lax.rsqrt(jnp.mean(centred * centred, axis=-1, keepdims=True) + EPSILON)
    return centred * inverse, inverse


def crop_table(layout, mb):
    start, bigs, smalls = jnp.int32(0), jnp.int32(0), jnp.int32(0)
    starts, moves, slots = [], [], []
    for crop in range(6):
        is_big = layout[mb, 0, crop]
        slot = jnp.where(is_big == 1, BIG_CROP * bigs, 2 * BIG_CROP + SMALL_CROP * smalls)
        starts.append(start)
        moves.append(slot - start)
        slots.append(slot)
        start = start + jnp.where(is_big == 1, BIG_CROP, SMALL_CROP)
        bigs = bigs + is_big
        smalls = smalls + 1 - is_big
    back = []
    for slot_start in SLOT_STARTS:
        value = jnp.int32(0)
        for crop in range(6):
            value = value - jnp.where(slots[crop] == slot_start, moves[crop], 0)
        back.append(value)
    return starts, moves, back


def to_slot(places, table):
    starts, moves, _ = table
    move = jnp.full(places.shape, moves[0], i32)
    for crop in range(1, 6):
        move = jnp.where(places >= starts[crop], moves[crop], move)
    return jnp.where(places < ROW_LEN, places + move, places)


def from_slot(places, table):
    move = jnp.full(places.shape, table[2][0], i32)
    for crop in range(1, 6):
        move = jnp.where(places >= SLOT_STARTS[crop], table[2][crop], move)
    return jnp.where(places < ROW_LEN, places + move, places)


def one_hot(mask):
    return jnp.where(mask, 1.0, 0.0).astype(bf16)


def lane_places(count):
    return lax.broadcasted_iota(i32, (1, count), 1)


def row_places(count):
    return lax.broadcasted_iota(i32, (count, 1), 0)


class Chosen:
    def __init__(self, chosen, layout, mb):
        self.table = crop_table(layout, mb)
        row = chosen[mb].astype(f32)
        self.column = jnp.transpose(jnp.broadcast_to(row, (8, CAPACITY)))[:, :1].astype(i32)
        self.slots = to_slot(self.column, self.table)

    def bounds(self):
        return [jnp.sum(jnp.where(self.slots < start, 1, 0)) for start in SLOT_STARTS[1:]]

    def taken(self, places):
        return jnp.max(jnp.where(self.column == places, 1, 0), axis=0, keepdims=True)

    def rank(self, slots):
        return jnp.sum(jnp.where(self.slots < slots, 1, 0), axis=0, keepdims=True)

    def picks(self, places, valid):
        rank = self.rank(to_slot(places, self.table))
        return one_hot((rank == row_places(CAPACITY)) & (self.taken(places) == 1) & valid)

    def spares(self, places):
        slots = to_slot(places, self.table)
        rank = slots - self.rank(slots)
        return one_hot((rank == row_places(SPARE)) & (self.taken(places) == 0) & (places < ROW_LEN))


def both_rows(mb):
    lanes = lane_places(PAIR)
    places = lanes // 2
    return places, (lanes - 2 * places == mb) & (places < ROW_LEN)


def crop_numbers(places, bounds):
    number = jnp.zeros(places.shape, i32)
    for bound in bounds:
        number = number + jnp.where(places >= bound, 1, 0)
    return number


def owned(numbers, kind):
    if kind == 0:
        return numbers == 0
    if kind == 1:
        return numbers == 1
    return numbers >= 2


def head_lanes(head, value):
    lanes = lane_places(QUAD)
    return jnp.where((lanes >= 64 * head) & (lanes < 64 * head + 64), value, 0.0).astype(bf16)


def quad(part, group):
    return pl.ds(pl.multiple_of(part * D + group * QUAD, QUAD), QUAD)


class Window:
    def __init__(self, kind, start, size, bounds):
        self.kind, self.rows, self.lanes = kind, pl.ds(start, size), slice(0, size)
        numbers = crop_numbers(start + row_places(size), bounds)
        self.start, self.size = start, size
        self.own = owned(numbers, kind)
        self.same = (numbers == crop_numbers(start + lane_places(size), bounds)) & self.own


    def log_row(self, lse, row):
        if len(lse.shape) == 3:
            return lse[self.kind, row : row + 1, self.lanes]
        return lse[pl.ds(row, 1), self.start : self.start + self.size]


def lse_by_row(lse, middle, bounds):
    def moved(kind, start):
        wide = jnp.concatenate([lse[kind], jnp.zeros((16, CAPACITY - 256), f32)], axis=1)
        return pltpu.roll(wide, start, axis=1)

    numbers = crop_numbers(lane_places(CAPACITY), bounds)
    later = jnp.where(numbers == 1, moved(1, middle), moved(2, 224))
    return jnp.where(numbers == 0, moved(0, 0), later)


def staggered(windows, bounds, first, second, third, rolled=False):
    heads = []
    for kind, start, size in windows:
        window = Window(kind, start, size, bounds)
        if rolled:

            def one(group, _):
                run_heads([(window, group, head) for head in range(4)], first, second, third)
                return 0

            lax.fori_loop(0, 3, one, 0)
        else:
            heads += [(window, group, head) for group in range(3) for head in range(4)]
    if heads:
        run_heads(heads, first, second, third)


def run_heads(heads, first, second, third):
    for t in range(len(heads) + 3):
        if t < len(heads):
            first(*heads[t])
        if 0 <= t - 2 < len(heads):
            second(*heads[t - 2])
        if 0 <= t - 3 < len(heads):
            third(*heads[t - 3])


def attention_forward(windows, bounds, qkv, mixed, lse, rolled=False):
    held = {}

    def first(window, group, head):
        rows = window.rows
        if head == 0:
            q4 = qkv[rows, quad(0, group)] * jnp.full((1, QUAD), SCALE, bf16)
            held[0] = q4, qkv[rows, quad(1, group)], jnp.transpose(qkv[rows, quad(2, group)])
        q4, k4, values = held[0]
        held[1, head] = mm_t(k4 * head_lanes(head, 1.0), q4), values

    def second(window, group, head):
        scores, values = held.pop((1, head))
        scores = jnp.where(window.same, scores, MASKED)
        top = jnp.max(scores, axis=0, keepdims=True)
        powers = jnp.exp(scores - top)
        power_sum = jnp.sum(powers, axis=0, keepdims=True)
        held[2, head] = (powers * (1.0 / power_sum)).astype(bf16), values
        row = 4 * group + head
        lse[window.kind, pl.ds(row, 1), window.lanes] = top + jnp.log(power_sum)

    def third(window, group, head):
        probs, values = held.pop((2, head))
        held[3, head] = mm(values[64 * head : 64 * head + 64, :], probs)
        if head == 3:
            total = jnp.transpose(jnp.concatenate([held.pop((3, k)) for k in range(4)], axis=0))
            old = mixed[window.rows, quad(0, group)].astype(f32)
            mixed[window.rows, quad(0, group)] = jnp.where(window.own, total, old).astype(bf16)

    staggered(windows, bounds, first, second, third, rolled)


def attention_backward(windows, bounds, qkv, grad_mixed, lse, grad_qkv, rolled=False):
    held = {}

    def first(window, group, head):
        rows = window.rows
        if head == 0:
            q4 = qkv[rows, quad(0, group)] * jnp.full((1, QUAD), SCALE, bf16)
            k4 = qkv[rows, quad(1, group)]
            held[0] = q4, k4, qkv[rows, quad(2, group)], grad_mixed[rows, quad(0, group)], jnp.transpose(k4)
        q4, k4, v4, g4, _ = held[0]
        lanes = head_lanes(head, 1.0)
        held[1, head] = mm_t(k4 * lanes, q4), mm_t(v4 * lanes, g4), held[0]

    def second(window, group, head):
        scores, grad_probs, whole = held.pop((1, head))
        row = 4 * group + head
        log_row = window.log_row(lse, row)
        probs = jnp.where(window.same, jnp.exp(scores - log_row), 0.0)
        spread = jnp.sum(probs * grad_probs, axis=0, keepdims=True)
        held[2, head] = probs.astype(bf16), (probs * (grad_probs - spread)).astype(bf16), whole

    def third(window, group, head):
        probs, grad_scores, (q4, _, _, g4, keys) = held.pop((2, head))
        lanes = head_lanes(head, 1.0)
        dv, dk = mm(probs, g4 * lanes), mm(grad_scores, q4 * lanes)
        dq = mm(keys[64 * head : 64 * head + 64, :], grad_scores)
        if head:
            dv, dk, dq = dv + held[3][0], dk + held[3][1], held[3][2] + [dq]
        else:
            dq = [dq]
        held[3] = dv, dk, dq
        if head == 3:
            dq = jnp.transpose(jnp.concatenate(dq, axis=0)) * SCALE
            for part, grad in enumerate((dq, dk, dv)):
                old = grad_qkv[window.rows, quad(part, group)].astype(f32)
                grad_qkv[window.rows, quad(part, group)] = jnp.where(window.own, grad, old).astype(bf16)

    staggered(windows, bounds, first, second, third, rolled)


def gelu_and_slope(u):
    power = jnp.exp(u * u * -0.5)
    cdf = 0.5 + 0.5 * lax.erf(u * 0.7071067811865476)
    return u * cdf, cdf + u * power * 0.3989422804014327


def norm_rows(count, x, gain_row, bias_row, out, rolled):
    def one(rows):
        z, _ = normalised(x[rows, :])
        out[rows, :] = (z * gain_row + bias_row).astype(bf16)

    rows_loop(count, one, rolled)


def project(s, w_qkv, rolled):
    def one(j):
        cols = col_chunk(j)
        s.qkv[:, cols] = mm(s.n1[...], w_qkv[:, cols]).astype(bf16)

    repeat(3, one, rolled)


def add_norm(count, x, gain_row, bias_row, s, rolled):
    def one(rows):
        hidden = x[rows, :] + s.att[rows, :]
        s.hidden[rows, :] = hidden
        z, _ = normalised(hidden)
        s.n2[rows, :] = (z * gain_row + bias_row).astype(bf16)

    rows_loop(count, one, rolled)


def feed_forward(count, s, w_up, w_down, rolled):
    def one(j):
        cols = col_chunk(j)
        upper = mm(s.n2[...], w_up[:, cols])
        for start in range(0, count, BLOCK):
            active, slope = gelu_and_slope(upper[start : start + BLOCK, :])
            s.act[start : start + BLOCK, cols] = active.astype(bf16)
            s.slope[start : start + BLOCK, cols] = slope.astype(bf16)

    repeat(FF // CHUNK, one, rolled)
    multiply_into(s.low, mm, s.act, w_down, rolled, False)


def branch_forward(count, windows, bounds, x, gain, bias, w, s, wait, send, rolled=False):
    w_qkv, w_out, w_up, w_down = w
    norm_rows(count, x, gain[0:1, :], bias[0:1, :], s.n1, rolled)
    send("n1")
    wait(0)
    project(s, w_qkv, rolled)
    send("qkv")
    attention_forward(windows, bounds, s.qkv, s.mixed, s.lse, rolled)
    send("mixed")
    wait(1)
    s.att[...] = mm(s.mixed[...], w_out[...])
    add_norm(count, x, gain[1:2, :], bias[1:2, :], s, rolled)
    send("n2")
    wait(2)
    wait(3)
    feed_forward(count, s, w_up, w_down, rolled)
    send("act")


def norm_backward(dn, z, inverse, gain_row):
    dz = dn * gain_row
    return inverse * (
        dz - jnp.mean(dz, axis=-1, keepdims=True) - z * jnp.mean(dz * z, axis=-1, keepdims=True)
    )


def fold(rows):
    total = rows[0:8, :]
    for k in range(8, BLOCK, 8):
        total = total + rows[k : k + 8, :]
    return total


def lower(count, s):
    def one(rows):
        s.gl[rows, :] = s.grad[rows, :].astype(bf16)

    rows_loop(count, one)


def feed_backward(count, s, w_up, w_down, wait, rolled=False):
    if rolled:
        for j in range(5):
            wait(j)

    def one(j):
        cols = col_chunk(j)
        if not rolled:
            wait(j)
        grad = mm_t(s.gl[...], w_down[cols, :])
        for start in range(0, count, BLOCK):
            slope = s.slope[start : start + BLOCK, cols].astype(f32)
            s.du[start : start + BLOCK, cols] = (grad[start : start + BLOCK, :] * slope).astype(bf16)

    repeat(FF // CHUNK, one, rolled)
    if not rolled:
        wait(4)
    multiply_into(s.low, mm_t, s.du, w_up, rolled, True)


def norm_two_backward(count, gain_row, s, rolled=False):
    s.sums[0:32, :] = jnp.zeros((32, D), f32)

    def one(rows):
        z, inverse = normalised(s.hidden[rows, :])
        dn = s.low[rows, :]
        dh = norm_backward(dn, z, inverse, gain_row)
        s.sums[8:16, :] += fold(dn * z)
        s.sums[24:32, :] += fold(dn)
        s.att[rows, :] = dh
        s.da[rows, :] = (s.grad[rows, :] + dh).astype(bf16)

    rows_loop(count, one, rolled)


def norm_one_backward(count, x, gain_row, s, rolled=False):
    def one(rows):
        z, inverse = normalised(x[rows, :].astype(f32))
        dn = s.low[rows, :]
        s.sums[0:8, :] += fold(dn * z)
        s.sums[16:24, :] += fold(dn)
        s.grad[rows, :] = s.att[rows, :] + norm_backward(dn, z, inverse, gain_row)

    rows_loop(count, one, rolled)


def branch_backward(count, windows, bounds, x, gain, w, s, wait, send, rolled=False):
    w_qkv, w_out, w_up, w_down = w
    lower(count, s)
    send("gl")
    feed_backward(count, s, w_up, w_down, wait, rolled)
    send("du")
    wait(5)
    norm_two_backward(count, gain[1:2, :], s, rolled)
    send("da")
    s.grad_mixed[...] = mm_t(s.da[...], w_out[...]).astype(bf16)
    attention_backward(windows, bounds, s.qkv, s.grad_mixed, s.lse_rows, s.grad_qkv, rolled)
    send("dqkv")
    wait(6)
    multiply_into(s.low, mm_t, s.grad_qkv, w_qkv, rolled, True)
    norm_one_backward(count, x, gain[0:1, :], s, rolled)


class Refs:
    def __init__(self, names, refs, constants):
        self.__dict__.update(zip(names, refs), **constants)


class Copies:
    def __init__(self, sems, first):
        self.sems, self.next, self.open = sems, first, []

    def start(self, source, target):
        copy = pltpu.make_async_copy(source, target, self.sems.at[self.next])
        self.next += 1
        copy.start()
        return copy

    def out(self, source, target):
        self.open.append(self.start(source, target))

    def finish(self):
        for copy in self.open:
            copy.wait()


def slot_rows(ops, slot, mb, count):
    return ops.at[slot, pl.ds(mb * count, count), :]


def send_slots(copies, ops, s, mb, count):
    wide = {"act": (SLOT_ACT, 4), "du": (SLOT_DU, 4), "dqkv": (SLOT_DQKV, 3)}
    flat = {"n1": SLOT_N1, "mixed": SLOT_MIXED, "n2": SLOT_N2, "gl": SLOT_GL, "da": SLOT_DA}

    def send(what):
        if what in flat:
            copies.out(getattr(s, what), slot_rows(ops, flat[what], mb, count))
        elif what in wide:
            source = {"act": "act", "du": "du", "dqkv": "grad_qkv"}[what]
            slot, parts = wide[what]
            for k in range(parts):
                copies.out(getattr(s, source).at[:, pl.ds(k * D, D)], slot_rows(ops, slot + k, mb, count))

    return send


def weight_scratch():
    return dict(
        v_qkv=pltpu.VMEM((D, 3 * D), bf16),
        v_out=pltpu.VMEM((D, D), bf16),
        v_up=pltpu.VMEM((D, FF), bf16),
        v_down=pltpu.VMEM((FF, D), bf16),
    )


def forward_scratch(count):
    return dict(
        n1=pltpu.VMEM((count, D), bf16),
        mixed=pltpu.VMEM((count, D), bf16),
        n2=pltpu.VMEM((count, D), bf16),
        act=pltpu.VMEM((count, FF), bf16),
    )


def shared_scratch(count):
    return dict(
        qkv=pltpu.VMEM((count, 3 * D), bf16),
        lse=pltpu.VMEM((3, 16, 256), f32),
        att=pltpu.VMEM((count, D), f32),
        hidden=pltpu.VMEM((count, D), f32),
        slope=pltpu.VMEM((count, FF), bf16),
        low=pltpu.VMEM((count, D), f32),
    )


def backward_scratch(count):
    return dict(
        grad=pltpu.VMEM((count, D), f32),
        gl=pltpu.VMEM((count, D), bf16),
        du=pltpu.VMEM((count, FF), bf16),
        da=pltpu.VMEM((count, D), bf16),
        grad_mixed=pltpu.VMEM((count, D), bf16),
        grad_qkv=pltpu.VMEM((count, 3 * D), bf16),
        sums=pltpu.VMEM((48, D), f32),
    )


def routed_bounds(column_slots):
    bounds = []
    for slot_start in SLOT_STARTS[1:]:
        bounds.append(jnp.sum(jnp.where(column_slots < slot_start, 1, 0)))
    return bounds


def routed_windows(bounds):
    middle = pl.multiple_of(jnp.minimum(bounds[0] // 16 * 16, 160), 16)
    return ((0, 0, 208), (1, middle, 224), (2, 224, 160))


FULL_BOUNDS = SLOT_STARTS[1:] + (ROW_LEN,)
FULL_WINDOWS = ((0, 0, 208), (1, 192, 208), (2, 384, 160))
FIXED_WINDOWS = ((0, 0, 208), (1, 32, 352), (2, 224, 160))


def flatten(target, source):
    target[PAIR - 16 :, :] = jnp.zeros((16, D), target.dtype)
    target[0 : 2 * ROW_LEN, :] = source[...].reshape(2 * ROW_LEN, D)


def running(amounts):
    return tuple(sum(amounts[:place]) for place in range(len(amounts)))


def planned(section):
    steps = len(YCOUNT[section])
    done = {}
    for k in range(STRIPS):
        place = BLOCKS[section].index(k)
        done[k] = next(t for t, before in enumerate(running(AMOUNTS[section] + (0,))[1:]) if before > place) - 1
    for k in range(8, 12):
        done[k] = max(done[k] for k in range(8, 12))
    sequence, taken, place = [], [], 0
    for t in range(-1, steps - 1):
        group = YFIRST[section][place : place + YCOUNT[section][t + 1]]
        place += len(group)
        hasty = [k for k, begin in zip(EARLY[section], EARLY_BEGIN[section]) if begin == t]
        for k in (*group, *hasty):
            sequence.append(k)
            taken.append(t)
    leave, last = [], -1
    for n, k in enumerate(sequence):
        last = max(last, done[k], taken[n] - 2)
        leave.append(last)
        assert last < taken[n] and (n < RING or taken[n - RING] <= last)
    sums, last = [-1] * (steps + 3), 1
    for a, k in enumerate(YFIRST[section]):
        last = max(last + 1, taken[sequence.index(k)] + 1)
        sums[last] = a
    return tuple(sequence), tuple(leave.count(t) for t in range(-1, steps - 1)), tuple(sums)


def parts_of(value):
    high = value.astype(bf16)
    return high, (value - high.astype(f32)).astype(bf16)


def launch(kernel, inputs, outputs, scratch, name, flops, collective_id=None, **constants):
    names = tuple(inputs) + tuple(outputs) + tuple(scratch)
    places = list(inputs)
    aliases = {}
    for k, (_, _, _, same) in enumerate(outputs.values()):
        if same is not None:
            aliases[places.index(same)] = k
    params = dict(vmem_limit_bytes=VMEM_LIMIT, has_side_effects=True)
    if collective_id is not None:
        params["collective_id"] = collective_id
    found = pl.pallas_call(
        lambda *refs: kernel(Refs(names, refs, constants)),
        out_shape=[jax.ShapeDtypeStruct(shape, kind) for shape, kind, _, _ in outputs.values()],
        in_specs=[pl.BlockSpec(memory_space=space) for _, space in inputs.values()],
        out_specs=[pl.BlockSpec(memory_space=space) for _, _, space, _ in outputs.values()],
        scratch_shapes=list(scratch.values()),
        input_output_aliases=aliases,
        compiler_params=pltpu.CompilerParams(**params),
        cost_estimate=pl.CostEstimate(flops=flops, bytes_accessed=30 * 2**20, transcendentals=0),
        name=name,
    )(*(array for array, _ in inputs.values()))
    return dict(zip(outputs, found))


def routed_forward_kernel(mb, r):
    w = (r.v_qkv, r.v_out, r.v_up, r.v_down)
    section = lax.axis_index("section")
    places, mine = both_rows(mb)

    @pl.when(section == 0)
    def _():
        copies = Copies(r.sems, 0)
        tok_in = copies.start(r.tokens, r.pair)
        loads = [copies.start(a, b) for a, b in zip((r.w_qkv, r.w_out, r.w_up, r.w_down), w)]
        chosen = Chosen(r.chosen, r.layout, mb)
        r.v_picks[...] = chosen.picks(places, mine)
        bounds = chosen.bounds()
        for k in range(5):
            r.bounds[0, k] = bounds[k]
        tok_in.wait()
        flatten(r.flat, r.pair)
        r.x[...] = mm(r.v_picks[...], r.flat[...])
        r.x_low[...] = r.x[...].astype(bf16)
        copies.out(r.x_low, r.st_x)
        slots = send_slots(copies, r.ops, r, mb, CAPACITY)

        def send(what):
            slots(what)
            if what == "qkv":
                copies.out(r.qkv, r.st_qkv)
            elif what == "mixed":
                r.lse_rows[...] = lse_by_row(r.lse, windows[1][1], bounds)
                copies.out(r.lse_rows, r.st_lse)
            elif what == "n2":
                copies.out(r.hidden, r.st_hidden)
            elif what == "act":
                copies.out(r.slope, r.st_slope)

        windows = routed_windows(bounds)
        branch_forward(
            CAPACITY, windows, bounds, r.x, r.gain, r.bias, w, r, lambda i: loads[i].wait(), send, mb == 1
        )
        router = r.router[...].reshape(1, D)

        def add(rows):
            branch = r.att[rows, :] + r.low[rows, :]
            r.low[rows, :] = branch
            here = r.x[rows, :]
            gates = jax.nn.sigmoid(jnp.sum(here * router, axis=-1, keepdims=True))
            r.y_low[rows, :] = (here + gates * branch).astype(bf16)

        rows_loop(CAPACITY, add)
        copies.out(r.y_low, r.y0p)
        copies.out(r.low, r.st_branch)
        copies.out(r.v_picks, r.picks_out)
        copies.finish()

    if mb == 0:
        @pl.when(section == 1)
        def _():
            copies = Copies(r.sems, 0)
            copies.start(r.tokens, r.pair).wait()
            flatten(r.flat, r.pair)
            copies.start(r.cotangent, r.pair).wait()
            flatten(r.flat_two, r.pair)
            for row in range(2):
                chosen = Chosen(r.chosen, r.layout, row)
                places, mine = both_rows(row)
                here = (to_slot(places, chosen.table) == row_places(FULL)) & mine
                fresh = here & (chosen.taken(places) == 0)
                r.v_x[row] = mm(one_hot(fresh), r.flat[...]).astype(bf16)
                r.v_cot[row] = mm(one_hot(here), r.flat_two[...]).astype(bf16)
                back = from_slot(lane_places(FULL), chosen.table)
                picks = chosen.picks(back, lane_places(FULL) < ROW_LEN)
                r.v_slot_picks[row] = picks
                r.v_spread[row] = jnp.transpose(picks)
                r.v_spares[row] = chosen.spares(back)
            for source, target in (
                (r.v_x, r.x_rest),
                (r.v_cot, r.cot),
                (r.v_slot_picks, r.slot_picks),
                (r.v_spread, r.spread),
                (r.v_spares, r.spares),
            ):
                copies.out(source, target)
            copies.finish()


def routed_outputs_kernel(r):
    @pl.when(lax.axis_index("section") == 0)
    def _():
        copies = Copies(r.sems, 0)
        loads = [
            copies.start(a, b)
            for a, b in (
                (r.tokens, r.pair), (r.picks_a, r.v_picks.at[0]), (r.picks_b, r.v_picks.at[1]),
                (r.y_a, r.v_y.at[0]), (r.y_b, r.v_y.at[1]),
            )
        ]
        for copy in loads:
            copy.wait()
        flatten(r.flat, r.pair)
        ones = jnp.ones((CAPACITY, 128), bf16)
        spread = t_mm(r.v_picks[0], r.v_y[0]) + t_mm(r.v_picks[1], r.v_y[1])
        is_in = (t_mm(r.v_picks[0], ones) + t_mm(r.v_picks[1], ones))[:, :1]
        result = jnp.where(is_in > 0.5, spread, r.flat[...].astype(f32)).astype(bf16)
        r.pair[...] = result[: 2 * ROW_LEN, :].reshape(ROW_LEN, 2, D)
        copies.out(r.pair, r.acts)
        copies.finish()


def full_kernel(mb, r):
    w = (r.v_qkv, r.v_out, r.v_up, r.v_down)

    @pl.when(lax.axis_index("section") == 1)
    def _():
        copies = Copies(r.sems, 0)
        first = [
            copies.start(a, b)
            for a, b in ((r.x_rest.at[mb], r.tok), (r.y0p, r.low_in), (r.spread.at[mb], r.v_spread))
        ]
        loads = [copies.start(a, b) for a, b in zip((r.w_qkv, r.w_out, r.w_up, r.w_down), w)]
        cot_in = copies.start(r.cot.at[mb], r.gl)
        picks_in = [copies.start(r.slot_picks.at[mb], r.v_picks), copies.start(r.spares.at[mb], r.v_spares)]
        for copy in first:
            copy.wait()
        r.x[...] = r.tok[...].astype(f32) + mm(r.v_spread[...], r.low_in[...])
        send = send_slots(copies, r.ops, r, mb, FULL)
        branch_forward(
            FULL, FULL_WINDOWS, FULL_BOUNDS, r.x, r.gain, r.bias, w, r, lambda i: loads[i].wait(), send
        )
        cot_in.wait()

        def add(rows):
            r.tok[rows, :] = (r.x[rows, :] + r.att[rows, :] + r.low[rows, :]).astype(bf16)
            r.grad[rows, :] = r.gl[rows, :].astype(f32)

        rows_loop(FULL, add)
        copies.out(r.tok, r.y1)
        r.lse_rows = r.lse
        branch_backward(FULL, FULL_WINDOWS, FULL_BOUNDS, r.x, r.gain, w, r, lambda i: None, send)
        r.sums[32:48, :] = jnp.zeros((16, D), f32)
        copies.out(r.sums, r.sums_out)

        def join(rows):
            total = r.gl[rows, :].astype(f32) + r.grad[rows, :]
            r.low[rows, :] = total
            r.high[rows, :] = total.astype(bf16)

        rows_loop(FULL, join)
        copies.out(r.low, r.dx)
        for copy in picks_in:
            copy.wait()
        r.v_sent[...] = mm(r.v_picks[...], r.high[...]).astype(bf16)
        copies.out(r.v_sent, r.sent)
        if mb == 0:
            r.v_sent_spares[...] = mm(r.v_spares[...], r.high[...]).astype(bf16)
            copies.out(r.v_sent_spares, r.sent_spares)
        copies.finish()


def placed_gradients(chosen, part, spare, out):
    places = lane_places(FULL)
    picks = chosen.picks(places, places < ROW_LEN)
    high, rest = parts_of(part[...])
    total = t_mm(picks, high) + t_mm(chosen.spares(places), spare[...]) + t_mm(picks, rest)
    out[...] = total[0:ROW_LEN, :].reshape(ROW_LEN, 1, D)


def gates_backward(r, bounds, rolled=False):
    router = r.router[...].reshape(1, D)
    r.sums[32:48, :] = jnp.zeros((16, D), f32)

    def gate(rows):
        here = r.x_low[rows, :].astype(f32)
        gates = jax.nn.sigmoid(jnp.sum(here * router, axis=-1, keepdims=True))
        dy = r.v_back[rows, :].astype(f32)
        slopes = jnp.sum(r.v_part[rows, :] * dy, axis=-1, keepdims=True) * gates * (1.0 - gates)
        r.grad[rows, :] = gates * dy
        r.sums[32:40, :] += fold(slopes * here)
        r.v_part[rows, :] = dy + slopes * router

    rows_loop(CAPACITY, gate, rolled)
    r.sums[40:41, :] = jnp.where(lane_places(D) == 0, bounds[1], 0).astype(f32)


def routed_backward_kernel(mb, r):
    w = (r.v_qkv, r.v_out, r.v_up, r.v_down)
    section = lax.axis_index("section")

    @pl.when(section == 0)
    def _():
        copies = Copies(r.sems, 0)

        def load(*pairs):
            return [copies.start(a, b) for a, b in pairs]

        first = load((r.back, r.v_back), (r.st_x, r.x_low), (r.st_branch, r.v_part))
        chunks = []
        for j in range(4):
            cols = pl.ds(j * CHUNK, CHUNK)
            chunks.append(
                load((r.w_down.at[cols, :], r.v_down.at[cols, :]), (r.st_slope.at[:, cols], r.slope.at[:, cols]))
            )
        chunks.append(load((r.w_up, r.v_up)))
        chunks.append(
            load((r.st_hidden, r.hidden), (r.w_out, r.v_out), (r.st_qkv, r.qkv), (r.st_lse, r.lse_rows))
        )
        chunks.append(load((r.w_qkv, r.v_qkv)))
        if mb == 0:
            spare_in = copies.start(r.back_spares, r.v_spares)
        bounds = [r.bounds[0, k] for k in range(5)]
        for copy in first:
            copy.wait()
        gates_backward(r, bounds)

        def wait(i):
            for copy in chunks[i]:
                copy.wait()

        send = send_slots(copies, r.ops, r, mb, CAPACITY)
        branch_backward(CAPACITY, FIXED_WINDOWS, bounds, r.x_low, r.gain, w, r, wait, send, True)
        copies.out(r.sums, r.sums_out)

        def join(rows):
            r.v_part[rows, :] += r.grad[rows, :]

        rows_loop(CAPACITY, join)
        if mb == 0:
            spare_in.wait()
            placed_gradients(Chosen(r.chosen, r.layout, 0), r.v_part, r.v_spares, r.row)
            copies.out(r.row, r.grads.at[0])
        else:
            copies.out(r.v_part, r.part)
        copies.finish()


def full_outputs_kernel(r):
    @pl.when(lax.axis_index("section") == 1)
    def _():
        copies = Copies(r.sems, 0)
        halves = (r.v_dx_a, r.v_dx_b)
        dx_in = [copies.start(r.dx_a, halves[0]), copies.start(r.dx_b, halves[1])]
        y_in = [copies.start(r.y1_a, r.v_y1.at[0]), copies.start(r.y1_b, r.v_y1.at[1])]
        dx_in[1].wait()
        chosen = Chosen(r.chosen, r.layout, 1)
        back = from_slot(lane_places(FULL), chosen.table)
        r.v_spares[...] = mm(chosen.spares(back), r.v_dx_b[...].astype(bf16)).astype(bf16)
        copies.out(r.v_spares, r.sent_spares)
        for copy in y_in:
            copy.wait()
        rows = row_places(PAIR)
        total = jnp.zeros((PAIR, D), f32)
        for row in range(2):
            table = crop_table(r.layout, row)
            slots = lane_places(FULL)
            target = jnp.where(slots < ROW_LEN, 2 * from_slot(slots, table) + row, -1)
            total = total + mm(one_hot(rows == target), r.v_y1[row])
        r.pair[...] = total[: 2 * ROW_LEN, :].reshape(ROW_LEN, 2, D).astype(bf16)
        copies.out(r.pair, r.acts)
        dx_in[0].wait()
        for row in range(2):
            table = crop_table(r.layout, row)
            slots = lane_places(FULL)
            move = one_hot((from_slot(slots, table) == row_places(FULL)) & (slots < ROW_LEN))
            high, rest = parts_of(halves[row][...])
            total = mm(move, high) + mm(move, rest)
            target = (r.row, r.row_two)[row]
            target[...] = total[0:ROW_LEN, :].reshape(ROW_LEN, 1, D)
            copies.out(target, r.grads.at[row])
        copies.finish()


def closing_kernel(r):
    def row_copy():
        return pltpu.make_async_copy(r.row, r.grads.at[1], r.sems.at[0])

    @pl.when(lax.axis_index("section") == 0)
    def _():
        placed_gradients(Chosen(r.chosen, r.layout, 1), r.rows, r.back_spares, r.row)
        row_copy().start()

    for name in ("qkv", "out", "up", "down"):
        getattr(r, "o_" + name)[...] = getattr(r, "g_" + name)[...]
    width = D // r.ways
    me = lax.axis_index("dp")
    turned = pltpu.roll(r.small[...], lax.rem(D - width * me, D), axis=1)
    r.o_gain[...] = turned[0:2, 0:width]
    r.o_bias[...] = turned[2:4, 0:width]
    r.o_router[...] = r.small[4, :]
    big = jnp.sum(r.small[5:6, :]).astype(i32)
    r.o_counts[0] = big
    r.o_counts[1] = 2 * CAPACITY * r.ways - big
    pl.when(lax.axis_index("section") == 0)(lambda: row_copy().wait())


def gradient_kernel(r):
    me = lax.axis_index("dp")
    zero = me - me
    section = lax.axis_index("section")
    routed, full = section == 0, section == 1
    c = lax.rem(me, 2)
    y = lax.rem(me // 2, 2)
    z = me // 4
    sibling = {"dp": me + 1 - 2 * c}
    beside = {"dp": me + 2 - 4 * y}
    above, below = {"dp": me + 4}, {"dp": me - 4}
    far = {"dp": me + 8 - 16 * (z // 2)}
    paired = {"dp": me + 4 - 8 * lax.rem(z, 2)}

    barrier = pltpu.get_barrier_semaphore()

    def greet(device):
        pl.semaphore_signal(barrier, inc=1, device_id=device, device_id_type=MESH_ID)

    for device in (sibling, beside, far):
        greet(device)
    pl.when(z > 0)(lambda: greet(below))
    pl.when(z < 3)(lambda: greet(above))
    pl.when(full)(lambda: greet({"section": 0}))

    def strip(k):
        return pl.ds(pl.multiple_of(k * STRIP, STRIP), STRIP)

    def remote(source, target, sems, index, device):
        return pltpu.make_async_remote_copy(
            source, target, sems.at[(0,) + index], sems.at[(1,) + index], device_id=device, device_id_type=MESH_ID
        )

    def listed(orders, n):
        found = []
        for order in orders:
            value = zero + order[0]
            for place, entry in enumerate(order[1:], 1):
                value = jnp.where(n == place, entry, value)
            found.append(value)
        return jnp.where(routed, found[0], found[1])

    def placed(orders, k):
        found = []
        for order in orders:
            value = zero
            for place, entry in enumerate(order):
                value = jnp.where(k == entry, place, value)
            found.append(value)
        return jnp.where(routed, found[0], found[1])

    def block_at(n):
        return listed(BLOCKS, n)

    plans = planned(0), planned(1)
    sequences, leaving, sums_at = zip(*plans)

    def place_of(k):
        return placed(sequences, k)

    def late(a):
        return listed(YFIRST, a)

    def sum_at(t):
        return jnp.where((t >= 0) & (t < len(sums_at[0])), listed(sums_at, t), -1)

    def early(b):
        return jnp.where(routed, EARLY[0][b], EARLY[1][b])

    def early_begin(b):
        return jnp.where(routed, EARLY_BEGIN[0][b], EARLY_BEGIN[1][b])

    def core_copy(k):
        slot = lax.rem(place_of(k), RING)
        return remote(r.part.at[:, :, 1 - c, strip(k), :], r.core_in.at[slot], r.core_sem, (k,), sibling)

    def side_copy(a):
        return remote(r.part.at[:, 1 - y, c, strip(late(a)), :], r.side_in.at[:, strip(a), :], r.side_sem, (a,), beside)

    def up_send(s, a):
        return remote(
            r.part.at[s, y, c, strip(late(a)), :], r.up_in.at[s - z - 1, strip(a), :], r.up_sem, (s, a), above
        )

    def up_take(s, a):
        return remote(r.part.at[s, y, c, strip(late(a)), :], r.up_in.at[s - z, strip(a), :], r.up_sem, (s, a), below)

    def down_send(s, a):
        return remote(
            r.part.at[s, y, c, strip(late(a)), :], r.down_in.at[z - 1 - s, strip(a), :], r.down_sem, (s, a), below
        )

    def down_take(s, a):
        return remote(
            r.part.at[s, y, c, strip(late(a)), :], r.down_in.at[z - s, strip(a), :], r.down_sem, (s, a), above
        )

    def early_rows(b):
        return strip(early(b))

    def early_up_send(s, b):
        return remote(
            r.part.at[s, :, c, early_rows(b), :], r.early_up.at[b, s - z - 1], r.early_sem, (0, s, b), above
        )

    def early_up_take(s, b):
        return remote(r.part.at[s, :, c, early_rows(b), :], r.early_up.at[b, s - z], r.early_sem, (0, s, b), below)

    def early_down_send(s, b):
        return remote(
            r.part.at[s, :, c, early_rows(b), :], r.early_down.at[b, z - 1 - s], r.early_sem, (1, s, b), below
        )

    def early_down_take(s, b):
        return remote(r.part.at[s, :, c, early_rows(b), :], r.early_down.at[b, z - s], r.early_sem, (1, s, b), above)

    def early_side(b):
        return remote(
            r.part.at[z, 1 - y, c, early_rows(b), :], r.early_side.at[b], r.early_side_sem, (b,), beside
        )

    def small_copy(k):
        device = (sibling, beside, paired, far)[k]
        return remote(r.small.at[k], r.small_in.at[k], r.small_sem, (k,), device)

    def across():
        return remote(r.small.at[4], r.cross_in, r.cross_sem, (), {"section": 1})

    s = Refs((), (), dict(r.__dict__, gl=r.grad_mixed, du=r.slope, v_back=r.da))
    v_out = r.v_down.at[pl.ds(0, D), :]
    v_qkv = r.v_up.at[:, pl.ds(0, 3 * D)]
    bounds = [r.bounds[0, k] for k in range(5)]

    def load(k, source, target):
        return pltpu.make_async_copy(source, target, r.sems.at[k])

    first = [load(0, r.back, r.da), load(1, r.st_x, r.x_low), load(2, r.st_branch, r.v_part)]
    middle = [load(12, r.st_hidden, r.hidden), load(13, r.st_qkv, r.qkv), load(14, r.st_lse, r.lse_rows)]
    again = [load(15, r.w_out, v_out), load(16, r.w_qkv, v_qkv)]
    feed_in = [load(3, r.w_down, r.v_down), load(4, r.st_slope, r.slope), load(5, r.w_up, r.v_up)]
    part_out = load(17, r.v_part, r.part_rows)

    def each(copies, act):
        for copy in copies:
            getattr(copy, act)()

    def thirds(target, left, right):
        def one(j, _):
            cols = pl.ds(pl.multiple_of(j * 256, 256), 256)
            target[:, cols] = mm_t(left[...], right[cols, :])
            return 0

        lax.fori_loop(0, 3, one, 0)

    def phase_feed():
        each(feed_in, "wait")

        def one(j, _):
            cols = pl.ds(pl.multiple_of(j * CHUNK, CHUNK), CHUNK)
            grad = mm_t(s.gl[...], r.v_down[cols, :])
            for start in range(0, CAPACITY, BLOCK):
                slope = r.slope[start : start + BLOCK, cols].astype(f32)
                r.slope[start : start + BLOCK, cols] = (grad[start : start + BLOCK, :] * slope).astype(bf16)
            return 0

        lax.fori_loop(0, 4, one, 0)
        thirds(r.low, s.du, r.v_up)
        each(again, "start")

    def phase_norm():
        each(middle, "wait")
        norm_two_backward(CAPACITY, r.gain[1:2, :], s, True)
        again[0].wait()
        r.grad_mixed[...] = mm_t(r.da[...], v_out[...]).astype(bf16)

    def phase_window(*kinds):
        windows = [FIXED_WINDOWS[kind] for kind in kinds]
        attention_backward(windows, bounds, r.qkv, r.grad_mixed, r.lse_rows, r.grad_qkv, True)

    def phase_last():
        again[1].wait()
        thirds(r.low, r.grad_qkv, v_qkv)
        norm_one_backward(CAPACITY, r.x_low, r.gain[0:1, :], s, True)

        def join(rows):
            r.v_part[rows, :] += r.grad[rows, :]

        rows_loop(CAPACITY, join, True)
        part_out.start()

    def slot_pair(b):
        left = jnp.where(b < 3, SLOT_N1, jnp.where(b == 3, SLOT_MIXED, jnp.where(b < 8, SLOT_N2, b - 8 + SLOT_ACT)))
        right = jnp.where(b < 3, b + SLOT_DQKV, jnp.where(b == 3, SLOT_DA, jnp.where(b < 8, b - 4 + SLOT_DU, SLOT_GL)))
        return left, right

    def operand_copies(n, left_rows, right_rows):
        left, right = slot_pair(block_at(n))
        side = lax.rem(n, 2)
        return (
            pltpu.make_async_copy(r.ops.at[left, 0:left_rows, :], r.left.at[side, 0:left_rows, :], r.load_sem.at[0, side]),
            pltpu.make_async_copy(
                r.ops.at[right, 0:right_rows, :], r.right.at[side, 0:right_rows, :], r.load_sem.at[1, side]
            ),
        )

    def operands(n, act):
        pl.when(routed)(lambda: each(operand_copies(n, 2 * CAPACITY, CAPACITY), act))
        pl.when(full)(lambda: each(operand_copies(n, 2 * FULL, 2 * FULL), act))

    def block(n):
        side = lax.rem(n, 2)
        b = block_at(n)
        operands(n, "wait")
        pl.when(n + 1 < STRIPS)(lambda: operands(n + 1, "start"))
        second = pl.ds(CAPACITY, CAPACITY)

        @pl.when(routed)
        def _():
            @pl.when(b >= 8)
            def _():
                r.right[side, second, :] = s.gl[...]

            @pl.when((b >= 4) & (b < 8))
            def _():
                r.right[side, second, :] = s.du[:, pl.ds(pl.multiple_of((b - 4) * D, D), D)]

            @pl.when(b == 3)
            def _():
                r.right[side, second, :] = r.da[...]

            @pl.when(b < 3)
            def _():
                r.right[side, second, :] = r.grad_qkv[:, pl.ds(pl.multiple_of(b * D, D), D)]

        def multiply(rows):
            def half(h, _):
                cols = pl.ds(pl.multiple_of(h * 384, 384), 384)
                product = t_mm(r.left[side, 0:rows, cols], r.right[side, 0:rows, :]).astype(bf16)

                @pl.when(b < 8)
                def _():
                    r.part[pl.ds(2 * h, 2), :, :, strip(b), :] = product.reshape(2, 2, 2, STRIP, D)

                @pl.when(b >= 8)
                def _():
                    r.part[b - 8, h, :, 384:576, :] = product.reshape(2, 192, D)

                return 0

            lax.fori_loop(0, 2, half, 0)

        pl.when(routed)(lambda: multiply(2 * CAPACITY))
        pl.when(full)(lambda: multiply(2 * FULL))

    def core_start(k):
        n = place_of(k)
        pl.when(n >= RING)(lambda: pl.semaphore_wait(r.free_sem.at[lax.rem(n, RING)], 1))
        core_copy(k).start()

    def add_into(target, source):
        (a, ia), (b, ib) = target, source
        a[ia] = (a[ia].astype(f32) + b[ib].astype(f32)).astype(bf16)

    def write(k, value):
        @pl.when(k < 3)
        def _():
            r.g_qkv[:, pl.ds(pl.multiple_of(k * D, D), D)] = value

        @pl.when(k == 3)
        def _():
            r.g_out[...] = value

        @pl.when((k > 3) & (k < 8))
        def _():
            r.g_up[:, pl.ds(pl.multiple_of((k - 4) * D, D), D)] = value

        @pl.when(k >= 8)
        def _():
            r.g_down[strip(k - 8), :] = value

    def core_arrived(k):
        n = place_of(k)
        slot = lax.rem(n, RING)
        core_copy(k).wait_recv()

        def one(i, _):
            zs, ys = i // 2, lax.rem(i, 2)
            add_into((r.part, (zs, ys, c, strip(k))), (r.core_in, (slot, zs, ys)))
            return 0

        lax.fori_loop(0, 8, one, 0)

        @pl.when(n + RING < STRIPS)
        def _():
            pl.semaphore_signal(r.free_sem.at[slot], inc=1, device_id=sibling, device_id_type=MESH_ID)

    def early_strip(b, t):
        rows, begin = early_rows(b), early_begin(b)
        pl.when(t == begin)(lambda: core_arrived(early(b)))

        @pl.when((t == begin + 2 * z) & (z < 3))
        def _():
            def one(i, _):
                k = 3 - i

                @pl.when(z > 0)
                def _():
                    early_up_take(k, b).wait_recv()
                    for ys in range(2):
                        add_into((r.part, (k, ys, c, rows)), (r.early_up, (b, k - z, ys)))

                early_up_send(k, b).start()
                return 0

            lax.fori_loop(0, 3 - z, one, 0)

        @pl.when((t == begin + 6 - 2 * z) & (z > 0))
        def _():
            def one(k, _):
                @pl.when(z < 3)
                def _():
                    early_down_take(k, b).wait_recv()
                    for ys in range(2):
                        add_into((r.part, (k, ys, c, rows)), (r.early_down, (b, z - k, ys)))

                early_down_send(k, b).start()
                return 0

            lax.fori_loop(0, z, one, 0)

        @pl.when(t == begin + 8)
        def _():
            @pl.when(z > 0)
            def _():
                early_up_take(z, b).wait_recv()
                for ys in range(2):
                    add_into((r.part, (z, ys, c, rows)), (r.early_up, (b, 0, ys)))

            @pl.when(z < 3)
            def _():
                early_down_take(z, b).wait_recv()
                for ys in range(2):
                    add_into((r.part, (z, ys, c, rows)), (r.early_down, (b, 0, ys)))

            early_side(b).start()

        @pl.when(t == begin + 10)
        def _():
            early_side(b).wait_recv()
            write(early(b), r.part[z, y, c, rows, :].astype(f32) + r.early_side[b].astype(f32))

    def serve(t):
        turn = jnp.minimum(t + 1, len(YCOUNT[0]) - 1)
        many = jnp.where(t + 1 < len(YCOUNT[0]), listed(YCOUNT, turn), 0)
        start = listed(tuple(running(counts) for counts in YCOUNT), turn)

        def set_out(i, _):
            core_arrived(late(start + i))
            side_copy(start + i).start()
            return 0

        lax.fori_loop(0, many, set_out, 0)
        for b in range(HASTE):
            early_strip(b, t)

        a_sum = sum_at(t)

        @pl.when(a_sum >= 0)
        def _():
            a = a_sum
            side_copy(a).wait_recv()

            def one(zs, _):
                add_into((r.part, (zs, y, c, strip(late(a)))), (r.side_in, (zs, strip(a))))
                return 0

            lax.fori_loop(0, 4, one, 0)

        au = sum_at(t - 2 * z)

        @pl.when((au >= 0) & (z < 3))
        def _():
            def one(i, _):
                k = 3 - i

                @pl.when(z > 0)
                def _():
                    up_take(k, au).wait_recv()
                    add_into((r.part, (k, y, c, strip(late(au)))), (r.up_in, (k - z, strip(au))))

                up_send(k, au).start()
                return 0

            lax.fori_loop(0, 3 - z, one, 0)

        ad = sum_at(t - 6 + 2 * z)

        @pl.when((ad >= 0) & (z > 0))
        def _():
            def one(k, _):
                @pl.when(z < 3)
                def _():
                    down_take(k, ad).wait_recv()
                    add_into((r.part, (k, y, c, strip(late(ad)))), (r.down_in, (z - k, strip(ad))))

                down_send(k, ad).start()
                return 0

            lax.fori_loop(0, z, one, 0)

        a_final = sum_at(t - 6)

        @pl.when(a_final >= 0)
        def _():
            a = a_final
            r.final[...] = r.part[z, y, c, strip(late(a)), :].astype(f32)

            @pl.when(z > 0)
            def _():
                up_take(z, a).wait_recv()
                r.final[...] += r.up_in[0, strip(a), :].astype(f32)

            @pl.when(z < 3)
            def _():
                down_take(z, a).wait_recv()
                r.final[...] += r.down_in[0, strip(a), :].astype(f32)

            write(late(a), r.final[...])

        @pl.when(t == PHASES[-1] + 1)
        def _():
            pl.when(full)(lambda: copy_sums())
            for k in range(6):
                rows = slice(8 * k, 8 * k + 8)
                r.small[0, k : k + 1, :] = jnp.sum(r.sums_a[rows, :] + r.sums[rows, :], axis=0, keepdims=True)
            r.small[0, 6:8, :] = jnp.zeros((2, D), f32)
            small_copy(0).start()

        for k in range(4):

            @pl.when(t == 2 * k + PHASES[-1] + 3)
            def _():
                small_copy(k).wait_recv()
                r.small[k + 1] = r.small[k] + r.small_in[k]
                if k < 3:
                    small_copy(k + 1).start()
                else:
                    pl.when(routed)(lambda: across().start())

    def copy_sums():
        r.sums[...] = r.sums_b[...]

    @pl.when(routed)
    def _():
        each(first, "start")

    operands(zero, "start")

    @pl.when(routed)
    def _():
        each(feed_in + middle, "start")
        each(first, "wait")
        gates_backward(s, bounds, True)

        def one(rows):
            s.gl[rows, :] = r.grad[rows, :].astype(bf16)

        rows_loop(CAPACITY, one, True)

    pl.semaphore_wait(barrier, 3 + (z > 0).astype(i32) + (z < 3).astype(i32) + routed.astype(i32))

    def step(turn, _):
        t = turn - 1
        serve(t)
        index = jnp.minimum(turn, len(AMOUNTS[0]) - 1)
        begin = listed(tuple(running(amounts) for amounts in AMOUNTS), index)
        amount = jnp.where(turn < len(AMOUNTS[0]), listed(AMOUNTS, index), 0)
        lax.fori_loop(0, amount, lambda i, _: (block(begin + i), 0)[1], 0)
        index = jnp.minimum(turn, len(leaving[0]) - 1)
        begin_core = listed(tuple(running(counts) for counts in leaving), index)
        amount = jnp.where(turn < len(leaving[0]), listed(leaving, index), 0)
        lax.fori_loop(0, amount, lambda i, _: (core_start(listed(sequences, begin_core + i)), 0)[1], 0)
        pl.when(routed & (t == PHASES[0]))(phase_feed)
        pl.when(routed & (t == PHASES[1]))(phase_norm)
        pl.when(routed & (t == PHASES[2]))(lambda: phase_window(0, 2))
        pl.when(routed & (t == PHASES[3]))(lambda: phase_window(1))
        pl.when(routed & (t == PHASES[4]))(phase_last)
        return 0

    lax.fori_loop(0, 19, step, 0)
    r.small_out[...] = r.small[4]


    @pl.when(routed)
    def _():
        across().wait_send()
        part_out.wait()

    @pl.when(full)
    def _():
        across().wait_recv()
        r.small_out[4:6, :] = r.cross_in[4:6, :]


    lax.fori_loop(0, STRIPS, lambda k, _: (core_copy(k).wait_send(), 0)[1], 0)

    def drain(a, _):
        side_copy(a).wait_send()
        for k in range(1, 4):
            pl.when(k > z)(lambda k=k: up_send(k, a).wait_send())
        for k in range(3):
            pl.when(k < z)(lambda k=k: down_send(k, a).wait_send())
        return 0

    lax.fori_loop(0, LATE, drain, 0)
    for b in range(HASTE):
        early_side(b).wait_send()
        for k in range(1, 4):
            pl.when(k > z)(lambda k=k: early_up_send(k, b).wait_send())
        for k in range(3):
            pl.when(k < z)(lambda k=k: early_down_send(k, b).wait_send())
    for k in range(4):
        small_copy(k).wait_send()


HBM = pl.ANY
VMEM = pltpu.VMEM
SMEM = pltpu.SMEM


def body(
    tokens, layout, selected, cotangent, w_qkv, w_out, w_up, w_down, norm_gain, norm_bias, w_router
):
    ways = lax.axis_size("dp")
    common = dict(
        layout=(layout, SMEM),
        chosen=(selected, VMEM),
        gain=(norm_gain[0], VMEM),
        bias=(norm_bias[0], VMEM),
        router=(w_router, VMEM),
        w_qkv=(w_qkv[0], HBM),
        w_out=(w_out[0], HBM),
        w_up=(w_up[0], HBM),
        w_down=(w_down[0], HBM),
    )
    tokens = jnp.transpose(tokens, (1, 2, 0, 3)).reshape(ROW_LEN, 2, D)
    cotangent = jnp.transpose(cotangent, (1, 2, 0, 3)).reshape(ROW_LEN, 2, D)
    ops_spec = ((SLOTS, 2 * FULL, D), bf16, HBM)
    acts_spec = ((ROW_LEN, 2, D), bf16, HBM)
    grads_spec = ((2, ROW_LEN, 1, D), f32, HBM)
    stash_spec = dict(
        st_x=((CAPACITY, D), bf16, HBM, None),
        st_qkv=((CAPACITY, 3 * D), bf16, HBM, None),
        st_slope=((CAPACITY, FF), bf16, HBM, None),
        st_hidden=((CAPACITY, D), f32, HBM, None),
        st_branch=((CAPACITY, D), f32, HBM, None),
        st_lse=((16, CAPACITY), f32, HBM, None),
        bounds=((1, 8), i32, SMEM, None),
    )
    laid_spec = dict(
        x_rest=((2, FULL, D), bf16, HBM, None),
        cot=((2, FULL, D), bf16, HBM, None),
        slot_picks=((2, CAPACITY, FULL), bf16, HBM, None),
        spread=((2, FULL, CAPACITY), bf16, HBM, None),
        spares=((2, SPARE, FULL), bf16, HBM, None),
    )
    buffers = dict(sems=pltpu.SemaphoreType.DMA((40,)), **weight_scratch())
    ops = None
    handed, stashes, picks, y0ps = [], [], [], []
    for mb in range(2):
        inputs = dict(common, tokens=(tokens, HBM), cotangent=(cotangent, HBM))
        outputs = dict(
            ops=ops_spec + ("ops_old" if mb else None,), y0p=((CAPACITY, D), bf16, HBM, None), **stash_spec
        )
        scratch = dict(
            **buffers,
            pair=pltpu.VMEM((ROW_LEN, 2, D), bf16),
            flat=pltpu.VMEM((PAIR, D), bf16),
            v_picks=pltpu.VMEM((CAPACITY, PAIR), bf16),
            x=pltpu.VMEM((CAPACITY, D), f32),
            x_low=pltpu.VMEM((CAPACITY, D), bf16),
            lse_rows=pltpu.VMEM((16, CAPACITY), f32),
            y_low=pltpu.VMEM((CAPACITY, D), bf16),
            **forward_scratch(CAPACITY),
            **shared_scratch(CAPACITY),
        )
        outputs.update(picks_out=((CAPACITY, PAIR), bf16, HBM, None))
        if mb == 0:
            outputs.update(laid_spec)
            scratch.update(
                flat_two=pltpu.VMEM((PAIR, D), bf16),
                v_x=pltpu.VMEM((2, FULL, D), bf16),
                v_cot=pltpu.VMEM((2, FULL, D), bf16),
                v_slot_picks=pltpu.VMEM((2, CAPACITY, FULL), bf16),
                v_spread=pltpu.VMEM((2, FULL, CAPACITY), bf16),
                v_spares=pltpu.VMEM((2, SPARE, FULL), bf16),
            )
        else:
            inputs.update(ops_old=(ops, HBM))
        found = launch(
            functools.partial(routed_forward_kernel, mb), inputs, outputs, scratch, f"routed_forward_{mb}", 6 * 10**9
        )
        ops, y0p = found["ops"], found["y0p"]
        if mb == 0:
            laid = {name: (found[name], HBM) for name in laid_spec}
        picks.append(found["picks_out"])
        y0ps.append(y0p)
        stashes.append({name: (found[name], SMEM if name == "bounds" else HBM) for name in stash_spec})
        handed.append(lax.ppermute(y0p, "section", [(0, 1)]))
    acts = launch(
        routed_outputs_kernel,
        dict(
            tokens=(tokens, HBM), picks_a=(picks[0], HBM), picks_b=(picks[1], HBM), y_a=(y0ps[0], HBM), y_b=(y0ps[1], HBM)
        ),
        dict(acts=acts_spec + (None,)),
        dict(
            sems=pltpu.SemaphoreType.DMA((8,)),
            pair=pltpu.VMEM((ROW_LEN, 2, D), bf16),
            flat=pltpu.VMEM((PAIR, D), bf16),
            v_picks=pltpu.VMEM((2, CAPACITY, PAIR), bf16),
            v_y=pltpu.VMEM((2, CAPACITY, D), bf16),
        ),
        "routed_outputs",
        10**9,
    )["acts"]
    sums, returned, ends = [], [], []
    for mb in range(2):
        outputs = dict(
            ops=ops_spec + ("ops_old",),
            sent=((CAPACITY, D), bf16, HBM, None),
            y1=((FULL, D), bf16, HBM, None),
            dx=((FULL, D), f32, HBM, None),
            sums_out=((48, D), f32, HBM, None),
        )
        if mb == 0:
            outputs.update(sent_spares=((SPARE, D), bf16, HBM, None))
        found = launch(
            functools.partial(full_kernel, mb),
            dict(common, **laid, y0p=(handed[mb], HBM), ops_old=(ops, HBM)),
            outputs,
            dict(
                **buffers,
                tok=pltpu.VMEM((FULL, D), bf16),
                x=pltpu.VMEM((FULL, D), f32),
                low_in=pltpu.VMEM((CAPACITY, D), bf16),
                v_spread=pltpu.VMEM((FULL, CAPACITY), bf16),
                v_picks=pltpu.VMEM((CAPACITY, FULL), bf16),
                v_spares=pltpu.VMEM((SPARE, FULL), bf16),
                high=pltpu.VMEM((FULL, D), bf16),
                v_sent=pltpu.VMEM((CAPACITY, D), bf16),
                v_sent_spares=pltpu.VMEM((SPARE, D), bf16),
                **forward_scratch(FULL),
                **shared_scratch(FULL),
                **backward_scratch(FULL),
            ),
            f"full_{mb}",
            20 * 10**9,
        )
        ops = found["ops"]
        sums.append(found["sums_out"])
        ends.append((found["y1"], found["dx"]))
        returned.append(lax.ppermute(found["sent"], "section", [(1, 0)]))
        if mb == 0:
            back_spares = lax.ppermute(found["sent_spares"], "section", [(1, 0)])
    for mb in range(1 if ways == 16 else 2):
        inputs = dict(
            common, back=(returned[mb], HBM), **stashes[mb], ops_old=(ops, HBM), sums_old=(sums[mb], HBM)
        )
        outputs = dict(ops=ops_spec + ("ops_old",), sums_out=((48, D), f32, HBM, "sums_old"))
        scratch = dict(
            **buffers,
            x_low=pltpu.VMEM((CAPACITY, D), bf16),
            v_back=pltpu.VMEM((CAPACITY, D), bf16),
            v_part=pltpu.VMEM((CAPACITY, D), f32),
            lse_rows=pltpu.VMEM((16, CAPACITY), f32),
            **shared_scratch(CAPACITY),
            **backward_scratch(CAPACITY),
        )
        if mb == 0:
            inputs.update(back_spares=(back_spares, HBM))
            outputs.update(grads=grads_spec + (None,))
            scratch.update(v_spares=pltpu.VMEM((SPARE, D), bf16), row=pltpu.VMEM((ROW_LEN, 1, D), f32))
        else:
            outputs.update(part=((CAPACITY, D), f32, HBM, None))
        found = launch(
            functools.partial(routed_backward_kernel, mb), inputs, outputs, scratch, f"routed_backward_{mb}", 7 * 10**9
        )
        ops, sums[mb] = found["ops"], found["sums_out"]
        if mb == 0:
            grads = found["grads"]
            ends = launch(
                full_outputs_kernel,
                dict(
                    layout=(layout, SMEM), chosen=(selected, VMEM), y1_a=(ends[0][0], HBM), y1_b=(ends[1][0], HBM),
                    dx_a=(ends[0][1], HBM), dx_b=(ends[1][1], HBM), acts_old=(acts, HBM), grads_old=(grads, HBM),
                ),
                dict(
                    acts=acts_spec + ("acts_old",), grads=grads_spec + ("grads_old",),
                    sent_spares=((SPARE, D), bf16, HBM, None),
                ),
                dict(
                    sems=pltpu.SemaphoreType.DMA((16,)),
                    v_spares=pltpu.VMEM((SPARE, D), bf16),
                    v_dx_a=pltpu.VMEM((FULL, D), f32),
                    v_dx_b=pltpu.VMEM((FULL, D), f32),
                    v_y1=pltpu.VMEM((2, FULL, D), bf16),
                    pair=pltpu.VMEM((ROW_LEN, 2, D), bf16),
                    row=pltpu.VMEM((ROW_LEN, 1, D), f32),
                    row_two=pltpu.VMEM((ROW_LEN, 1, D), f32),
                ),
                "full_outputs",
                4 * 10**9,
            )
            acts, grads = ends["acts"], ends["grads"]
            back_spares = lax.ppermute(ends["sent_spares"], "section", [(1, 0)])
    if ways == 16:
        shares, small, rows = summed_by_kernel(ops, sums, dict(common, back=(returned[1], HBM), **stashes[1]))
    else:
        rows = found["part"]
        shares, small = summed_by_collectives(ops, sums, ways)
    found = launch(
        closing_kernel,
        dict(
            small=(small, VMEM), rows=(rows, VMEM), back_spares=(back_spares, VMEM), grads_old=(grads, HBM),
            layout=(layout, SMEM), chosen=(selected, VMEM),
            **{"g_" + name: (share, VMEM) for name, share in shares.items()},
        ),
        dict(
            grads=grads_spec + ("grads_old",),
            o_gain=((2, D // ways), f32, VMEM, None),
            o_bias=((2, D // ways), f32, VMEM, None),
            o_router=((D,), f32, VMEM, None),
            o_counts=((2,), i32, SMEM, None),
            **{"o_" + name: (share.shape, f32, VMEM, None) for name, share in shares.items()},
        ),
        dict(sems=pltpu.SemaphoreType.DMA((4,)), row=pltpu.VMEM((ROW_LEN, 1, D), f32)),
        "closing",
        10**9,
        ways=ways,
    )
    return (
        jnp.transpose(acts.reshape(1, ROW_LEN, 2, D), (2, 0, 1, 3))[None],
        found["grads"].reshape(1, 2, 1, ROW_LEN, D),
        found["o_qkv"][None],
        found["o_out"][None],
        found["o_up"][None],
        found["o_down"][None],
        found["o_gain"][None],
        found["o_bias"][None],
        found["o_router"],
        found["o_counts"],
    )


def summed_by_kernel(ops, sums, routed):
    found = launch(
        gradient_kernel,
        dict(routed, ops=(ops, HBM), sums_a=(sums[0], VMEM), sums_b=(sums[1], VMEM)),
        dict(
            g_qkv=((STRIP, 3 * D), f32, VMEM, None),
            g_out=((STRIP, D), f32, VMEM, None),
            g_up=((STRIP, FF), f32, VMEM, None),
            g_down=((4 * STRIP, D), f32, VMEM, None),
            small_out=((8, D), f32, VMEM, None),
            part_rows=((CAPACITY, D), f32, HBM, None),
        ),
        dict(
            left=pltpu.VMEM((2, 2 * FULL, D), bf16),
            right=pltpu.VMEM((2, 2 * FULL, D), bf16),
            part=pltpu.VMEM((4, 2, 2, SHARD_ROWS, D), bf16),
            core_in=pltpu.VMEM((RING, 4, 2, STRIP, D), bf16),
            side_in=pltpu.VMEM((4, LATE * STRIP, D), bf16),
            up_in=pltpu.VMEM((3, LATE * STRIP, D), bf16),
            down_in=pltpu.VMEM((3, LATE * STRIP, D), bf16),
            early_up=pltpu.VMEM((HASTE, 3, 2, STRIP, D), bf16),
            early_down=pltpu.VMEM((HASTE, 3, 2, STRIP, D), bf16),
            early_side=pltpu.VMEM((HASTE, STRIP, D), bf16),
            final=pltpu.VMEM((STRIP, D), f32),
            small=pltpu.VMEM((5, 8, D), f32),
            small_in=pltpu.VMEM((4, 8, D), f32),
            cross_in=pltpu.VMEM((8, D), f32),
            cross_sem=pltpu.SemaphoreType.DMA((2,)),
            v_up=pltpu.VMEM((D, FF), bf16),
            v_down=pltpu.VMEM((FF, D), bf16),
            x_low=pltpu.VMEM((CAPACITY, D), bf16),
            v_part=pltpu.VMEM((CAPACITY, D), f32),
            lse_rows=pltpu.VMEM((16, CAPACITY), f32),
            **shared_scratch(CAPACITY),
            grad=pltpu.VMEM((CAPACITY, D), f32),
            da=pltpu.VMEM((CAPACITY, D), bf16),
            grad_mixed=pltpu.VMEM((CAPACITY, D), bf16),
            grad_qkv=pltpu.VMEM((CAPACITY, 3 * D), bf16),
            sums=pltpu.VMEM((48, D), f32),
            sems=pltpu.SemaphoreType.DMA((18,)),
            load_sem=pltpu.SemaphoreType.DMA((2, 2)),
            core_sem=pltpu.SemaphoreType.DMA((2, STRIPS)),
            side_sem=pltpu.SemaphoreType.DMA((2, LATE)),
            up_sem=pltpu.SemaphoreType.DMA((2, 4, LATE)),
            down_sem=pltpu.SemaphoreType.DMA((2, 4, LATE)),
            early_sem=pltpu.SemaphoreType.DMA((2, 2, 4, HASTE)),
            early_side_sem=pltpu.SemaphoreType.DMA((2, HASTE)),
            small_sem=pltpu.SemaphoreType.DMA((2, 4)),
            free_sem=pltpu.SemaphoreType.REGULAR((RING,)),
        ),
        "gradients",
        20 * 10**9,
        collective_id=0,
    )
    shares = {name: found["g_" + name] for name in ("qkv", "out", "up", "down")}
    return shares, found["small_out"], found["part_rows"]


def summed_by_collectives(ops, sums, count):
    first = lax.axis_index("section") == 0
    used = jnp.where(first, 2 * CAPACITY, 2 * FULL)
    ops = jnp.where(lax.broadcasted_iota(i32, (1, 2 * FULL, 1), 1) < used, ops, 0)

    def gradient(left, lefts, right, rights):
        a = jnp.concatenate([ops[left + k] for k in range(lefts)], axis=1)
        b = jnp.concatenate([ops[right + k] for k in range(rights)], axis=1)
        return lax.psum_scatter(t_mm(a, b), "dp", scatter_dimension=0, tiled=True)

    shares = dict(
        qkv=gradient(SLOT_N1, 1, SLOT_DQKV, 3),
        out=gradient(SLOT_MIXED, 1, SLOT_DA, 1),
        up=gradient(SLOT_N2, 1, SLOT_DU, 4),
        down=gradient(SLOT_ACT, 4, SLOT_GL, 1),
    )
    small = jnp.sum((sums[0] + sums[1]).reshape(6, 8, D), axis=1)
    small = jnp.concatenate([small, jnp.zeros((2, D), f32)])
    small = lax.psum(small, "dp")
    shared = lax.psum(jnp.where(first, small[4:6], 0.0), "section")
    return shares, jnp.concatenate([small[:4], shared, small[6:]])


def solution(mesh):
    return jax.shard_map(
        body,
        mesh=mesh,
        in_specs=(
            P(None, "dp", None, None),
            P(None, "dp", None),
            P(None, "dp", None),
            P(None, "dp", None, None),
            P("section", None, None),
            P("section", None, None),
            P("section", None, None),
            P("section", None, None),
            P("section", None, None),
            P("section", None, None),
            P(),
        ),
        out_specs=(
            P("section", None, "dp", None, None),
            P("section", None, "dp", None, None),
            P("section", "dp", None),
            P("section", "dp", None),
            P("section", "dp", None),
            P("section", "dp", None),
            P("section", None, "dp"),
            P("section", None, "dp"),
            P(),
            P(),
        ),
        check_vma=False,
    )
```

```python
import functools

import jax
import jax.numpy as jnp
from jax import lax
from jax.experimental import pallas as pl
from jax.experimental.pallas import tpu as pltpu
from jax.sharding import PartitionSpec as P

D = 768
HEADS = 12
FF = 3072
BIG_CROP = 197
SMALL_CROP = 37
ROW_LEN = 542
CAPACITY = 384
FULL = 544
PAIR = 2 * FULL
SPARE = 160
QUAD = 256
SCALE = 0.125
EPSILON = 1e-06
MASKED = -1e30
BLOCK = 32
CHUNK = 768
SLOT_STARTS = (0, 197, 394, 431, 468, 505)
SLOTS = 16
SLOT_N1, SLOT_MIXED, SLOT_N2, SLOT_ACT, SLOT_GL, SLOT_DA, SLOT_DQKV, SLOT_DU = 0, 1, 2, 3, 7, 8, 9, 12
SHARD_ROWS = 576
STRIP = 48
STRIPS = SHARD_ROWS // STRIP
BLOCKS = ((8, 9, 10, 11, 4, 5, 6, 7, 3, 0, 1, 2), (4, 5, 6, 7, 3, 0, 1, 2, 8, 9, 10, 11))
AMOUNTS = ((4, 0, 3, 0, 0, 2, 0, 1, 1, 1), (2, 1, 2, 2, 2, 2, 1, 0, 0, 0))
YFIRST = ((8, 10, 4, 5, 6, 3, 0, 1, 2), (5, 7, 3, 0, 1, 2, 8, 9, 10))
YCOUNT = ((0, 2, 0, 1, 2, 0, 1, 0, 1, 1, 0, 1), (0, 0, 1, 2, 2, 1, 0, 2, 1, 0, 0, 0))
EARLY = ((11, 9, 7), (6, 4, 11))
EARLY_BEGIN = ((1, 0, 7), (1, 0, 6))
PHASES = (0, 1, 3, 4, 5)
LATE, HASTE = len(YFIRST[0]), len(EARLY[0])
RING = 4
MESH_ID = pl.DeviceIdType.MESH
VMEM_LIMIT = 63 * 2**20 + 2**19

f32 = jnp.float32
bf16 = jnp.bfloat16
i32 = jnp.int32


def mm(left, right):
    return jnp.dot(left, right, preferred_element_type=f32)


def mm_t(left, right):
    return lax.dot_general(left, right, (((1,), (1,)), ((), ())), preferred_element_type=f32)


def t_mm(left, right):
    return lax.dot_general(left, right, (((0,), (0,)), ((), ())), preferred_element_type=f32)


def rows_loop(count, body, rolled=False):
    if not rolled:
        for start in range(0, count, BLOCK):
            body(pl.ds(start, BLOCK))
        return

    def some(i, _):
        for k in range(4):
            body(pl.ds(pl.multiple_of((4 * i + k) * BLOCK, BLOCK), BLOCK))
        return 0

    lax.fori_loop(0, count // (4 * BLOCK), some, 0)


def col_chunk(j):
    return pl.ds(pl.multiple_of(j * CHUNK, CHUNK), CHUNK)


def repeat(count, body, rolled):
    if rolled:
        lax.fori_loop(0, count, lambda i, _: (body(i), 0)[1], 0)
    else:
        for i in range(count):
            body(i)


def multiply_into(target, product, left, right, rolled, by_rows):
    if not rolled:
        target[...] = product(left[...], right[...])
        return

    def one(j):
        cols = pl.ds(pl.multiple_of(j * 256, 256), 256)
        target[:, cols] = product(left[...], right[cols, :] if by_rows else right[:, cols])

    repeat(3, one, True)


def normalised(rows):
    centred = rows - jnp.mean(rows, axis=-1, keepdims=True)
    inverse = lax.rsqrt(jnp.mean(centred * centred, axis=-1, keepdims=True) + EPSILON)
    return centred * inverse, inverse


def crop_table(layout, mb):
    start, bigs, smalls = jnp.int32(0), jnp.int32(0), jnp.int32(0)
    starts, moves, slots = [], [], []
    for crop in range(6):
        is_big = layout[mb, 0, crop]
        slot = jnp.where(is_big == 1, BIG_CROP * bigs, 2 * BIG_CROP + SMALL_CROP * smalls)
        starts.append(start)
        moves.append(slot - start)
        slots.append(slot)
        start = start + jnp.where(is_big == 1, BIG_CROP, SMALL_CROP)
        bigs = bigs + is_big
        smalls = smalls + 1 - is_big
    back = []
    for slot_start in SLOT_STARTS:
        value = jnp.int32(0)
        for crop in range(6):
            value = value - jnp.where(slots[crop] == slot_start, moves[crop], 0)
        back.append(value)
    return starts, moves, back


def to_slot(places, table):
    starts, moves, _ = table
    move = jnp.full(places.shape, moves[0], i32)
    for crop in range(1, 6):
        move = jnp.where(places >= starts[crop], moves[crop], move)
    return jnp.where(places < ROW_LEN, places + move, places)


def from_slot(places, table):
    move = jnp.full(places.shape, table[2][0], i32)
    for crop in range(1, 6):
        move = jnp.where(places >= SLOT_STARTS[crop], table[2][crop], move)
    return jnp.where(places < ROW_LEN, places + move, places)


def one_hot(mask):
    return jnp.where(mask, 1.0, 0.0).astype(bf16)


def lane_places(count):
    return lax.broadcasted_iota(i32, (1, count), 1)


def row_places(count):
    return lax.broadcasted_iota(i32, (count, 1), 0)


class Chosen:
    def __init__(self, chosen, layout, mb):
        self.table = crop_table(layout, mb)
        row = chosen[mb].astype(f32)
        self.column = jnp.transpose(jnp.broadcast_to(row, (8, CAPACITY)))[:, :1].astype(i32)
        self.slots = to_slot(self.column, self.table)

    def bounds(self):
        return [jnp.sum(jnp.where(self.slots < start, 1, 0)) for start in SLOT_STARTS[1:]]

    def taken(self, places):
        return jnp.max(jnp.where(self.column == places, 1, 0), axis=0, keepdims=True)

    def rank(self, slots):
        return jnp.sum(jnp.where(self.slots < slots, 1, 0), axis=0, keepdims=True)

    def picks(self, places, valid):
        rank = self.rank(to_slot(places, self.table))
        return one_hot((rank == row_places(CAPACITY)) & (self.taken(places) == 1) & valid)

    def spares(self, places):
        slots = to_slot(places, self.table)
        rank = slots - self.rank(slots)
        return one_hot((rank == row_places(SPARE)) & (self.taken(places) == 0) & (places < ROW_LEN))


def both_rows(mb):
    lanes = lane_places(PAIR)
    places = lanes // 2
    return places, (lanes - 2 * places == mb) & (places < ROW_LEN)


def crop_numbers(places, bounds):
    number = jnp.zeros(places.shape, i32)
    for bound in bounds:
        number = number + jnp.where(places >= bound, 1, 0)
    return number


def owned(numbers, kind):
    if kind == 0:
        return numbers == 0
    if kind == 1:
        return numbers == 1
    return numbers >= 2


def head_lanes(head, value):
    lanes = lane_places(QUAD)
    return jnp.where((lanes >= 64 * head) & (lanes < 64 * head + 64), value, 0.0).astype(bf16)


def quad(part, group):
    return pl.ds(pl.multiple_of(part * D + group * QUAD, QUAD), QUAD)


class Window:
    def __init__(self, kind, start, size, bounds):
        self.kind, self.rows, self.lanes = kind, pl.ds(start, size), slice(0, size)
        numbers = crop_numbers(start + row_places(size), bounds)
        self.start, self.size = start, size
        self.own = owned(numbers, kind)
        self.same = (numbers == crop_numbers(start + lane_places(size), bounds)) & self.own


    def log_row(self, lse, row):
        if len(lse.shape) == 3:
            return lse[self.kind, row : row + 1, self.lanes]
        return lse[pl.ds(row, 1), self.start : self.start + self.size]


def lse_by_row(lse, middle, bounds):
    def moved(kind, start):
        wide = jnp.concatenate([lse[kind], jnp.zeros((16, CAPACITY - 256), f32)], axis=1)
        return pltpu.roll(wide, start, axis=1)

    numbers = crop_numbers(lane_places(CAPACITY), bounds)
    later = jnp.where(numbers == 1, moved(1, middle), moved(2, 224))
    return jnp.where(numbers == 0, moved(0, 0), later)


def staggered(windows, bounds, first, second, third, rolled=False):
    heads = []
    for kind, start, size in windows:
        window = Window(kind, start, size, bounds)
        if rolled:

            def one(group, _):
                run_heads([(window, group, head) for head in range(4)], first, second, third)
                return 0

            lax.fori_loop(0, 3, one, 0)
        else:
            heads += [(window, group, head) for group in range(3) for head in range(4)]
    if heads:
        run_heads(heads, first, second, third)


def run_heads(heads, first, second, third):
    for t in range(len(heads) + 3):
        if t < len(heads):
            first(*heads[t])
        if 0 <= t - 2 < len(heads):
            second(*heads[t - 2])
        if 0 <= t - 3 < len(heads):
            third(*heads[t - 3])


def attention_forward(windows, bounds, qkv, mixed, lse, rolled=False):
    held = {}

    def first(window, group, head):
        rows = window.rows
        if head == 0:
            q4 = qkv[rows, quad(0, group)] * jnp.full((1, QUAD), SCALE, bf16)
            held[0] = q4, qkv[rows, quad(1, group)], jnp.transpose(qkv[rows, quad(2, group)])
        q4, k4, values = held[0]
        held[1, head] = mm_t(k4 * head_lanes(head, 1.0), q4), values

    def second(window, group, head):
        scores, values = held.pop((1, head))
        scores = jnp.where(window.same, scores, MASKED)
        top = jnp.max(scores, axis=0, keepdims=True)
        powers = jnp.exp(scores - top)
        power_sum = jnp.sum(powers, axis=0, keepdims=True)
        held[2, head] = (powers * (1.0 / power_sum)).astype(bf16), values
        row = 4 * group + head
        lse[window.kind, pl.ds(row, 1), window.lanes] = top + jnp.log(power_sum)

    def third(window, group, head):
        probs, values = held.pop((2, head))
        held[3, head] = mm(values[64 * head : 64 * head + 64, :], probs)
        if head == 3:
            total = jnp.transpose(jnp.concatenate([held.pop((3, k)) for k in range(4)], axis=0))
            old = mixed[window.rows, quad(0, group)].astype(f32)
            mixed[window.rows, quad(0, group)] = jnp.where(window.own, total, old).astype(bf16)

    staggered(windows, bounds, first, second, third, rolled)


def attention_backward(windows, bounds, qkv, grad_mixed, lse, grad_qkv, rolled=False):
    held = {}

    def first(window, group, head):
        rows = window.rows
        if head == 0:
            q4 = qkv[rows, quad(0, group)] * jnp.full((1, QUAD), SCALE, bf16)
            k4 = qkv[rows, quad(1, group)]
            held[0] = q4, k4, qkv[rows, quad(2, group)], grad_mixed[rows, quad(0, group)], jnp.transpose(k4)
        q4, k4, v4, g4, _ = held[0]
        lanes = head_lanes(head, 1.0)
        held[1, head] = mm_t(k4 * lanes, q4), mm_t(v4 * lanes, g4), held[0]

    def second(window, group, head):
        scores, grad_probs, whole = held.pop((1, head))
        row = 4 * group + head
        log_row = window.log_row(lse, row)
        probs = jnp.where(window.same, jnp.exp(scores - log_row), 0.0)
        spread = jnp.sum(probs * grad_probs, axis=0, keepdims=True)
        held[2, head] = probs.astype(bf16), (probs * (grad_probs - spread)).astype(bf16), whole

    def third(window, group, head):
        probs, grad_scores, (q4, _, _, g4, keys) = held.pop((2, head))
        lanes = head_lanes(head, 1.0)
        dv, dk = mm(probs, g4 * lanes), mm(grad_scores, q4 * lanes)
        dq = mm(keys[64 * head : 64 * head + 64, :], grad_scores)
        if head:
            dv, dk, dq = dv + held[3][0], dk + held[3][1], held[3][2] + [dq]
        else:
            dq = [dq]
        held[3] = dv, dk, dq
        if head == 3:
            dq = jnp.transpose(jnp.concatenate(dq, axis=0)) * SCALE
            for part, grad in enumerate((dq, dk, dv)):
                old = grad_qkv[window.rows, quad(part, group)].astype(f32)
                grad_qkv[window.rows, quad(part, group)] = jnp.where(window.own, grad, old).astype(bf16)

    staggered(windows, bounds, first, second, third, rolled)


def gelu_and_slope(u):
    power = jnp.exp(u * u * -0.5)
    cdf = 0.5 + 0.5 * lax.erf(u * 0.7071067811865476)
    return u * cdf, cdf + u * power * 0.3989422804014327


def norm_rows(count, x, gain_row, bias_row, out, rolled):
    def one(rows):
        z, _ = normalised(x[rows, :])
        out[rows, :] = (z * gain_row + bias_row).astype(bf16)

    rows_loop(count, one, rolled)


def project(s, w_qkv, rolled):
    def one(j):
        cols = col_chunk(j)
        s.qkv[:, cols] = mm(s.n1[...], w_qkv[:, cols]).astype(bf16)

    repeat(3, one, rolled)


def add_norm(count, x, gain_row, bias_row, s, rolled):
    def one(rows):
        hidden = x[rows, :] + s.att[rows, :]
        s.hidden[rows, :] = hidden
        z, _ = normalised(hidden)
        s.n2[rows, :] = (z * gain_row + bias_row).astype(bf16)

    rows_loop(count, one, rolled)


def feed_forward(count, s, w_up, w_down, rolled):
    def one(j):
        cols = col_chunk(j)
        upper = mm(s.n2[...], w_up[:, cols])
        for start in range(0, count, BLOCK):
            active, slope = gelu_and_slope(upper[start : start + BLOCK, :])
            s.act[start : start + BLOCK, cols] = active.astype(bf16)
            s.slope[start : start + BLOCK, cols] = slope.astype(bf16)

    repeat(FF // CHUNK, one, rolled)
    multiply_into(s.low, mm, s.act, w_down, rolled, False)


def branch_forward(count, windows, bounds, x, gain, bias, w, s, wait, send, rolled=False):
    w_qkv, w_out, w_up, w_down = w
    norm_rows(count, x, gain[0:1, :], bias[0:1, :], s.n1, rolled)
    send("n1")
    wait(0)
    project(s, w_qkv, rolled)
    send("qkv")
    attention_forward(windows, bounds, s.qkv, s.mixed, s.lse, rolled)
    send("mixed")
    wait(1)
    s.att[...] = mm(s.mixed[...], w_out[...])
    add_norm(count, x, gain[1:2, :], bias[1:2, :], s, rolled)
    send("n2")
    wait(2)
    wait(3)
    feed_forward(count, s, w_up, w_down, rolled)
    send("act")


def norm_backward(dn, z, inverse, gain_row):
    dz = dn * gain_row
    return inverse * (
        dz - jnp.mean(dz, axis=-1, keepdims=True) - z * jnp.mean(dz * z, axis=-1, keepdims=True)
    )


def fold(rows):
    total = rows[0:8, :]
    for k in range(8, BLOCK, 8):
        total = total + rows[k : k + 8, :]
    return total


def lower(count, s):
    def one(rows):
        s.gl[rows, :] = s.grad[rows, :].astype(bf16)

    rows_loop(count, one)


def feed_backward(count, s, w_up, w_down, wait, rolled=False):
    if rolled:
        for j in range(5):
            wait(j)

    def one(j):
        cols = col_chunk(j)
        if not rolled:
            wait(j)
        grad = mm_t(s.gl[...], w_down[cols, :])
        for start in range(0, count, BLOCK):
            slope = s.slope[start : start + BLOCK, cols].astype(f32)
            s.du[start : start + BLOCK, cols] = (grad[start : start + BLOCK, :] * slope).astype(bf16)

    repeat(FF // CHUNK, one, rolled)
    if not rolled:
        wait(4)
    multiply_into(s.low, mm_t, s.du, w_up, rolled, True)


def norm_two_backward(count, gain_row, s, rolled=False):
    s.sums[0:32, :] = jnp.zeros((32, D), f32)

    def one(rows):
        z, inverse = normalised(s.hidden[rows, :])
        dn = s.low[rows, :]
        dh = norm_backward(dn, z, inverse, gain_row)
        s.sums[8:16, :] += fold(dn * z)
        s.sums[24:32, :] += fold(dn)
        s.att[rows, :] = dh
        s.da[rows, :] = (s.grad[rows, :] + dh).astype(bf16)

    rows_loop(count, one, rolled)


def norm_one_backward(count, x, gain_row, s, rolled=False):
    def one(rows):
        z, inverse = normalised(x[rows, :].astype(f32))
        dn = s.low[rows, :]
        s.sums[0:8, :] += fold(dn * z)
        s.sums[16:24, :] += fold(dn)
        s.grad[rows, :] = s.att[rows, :] + norm_backward(dn, z, inverse, gain_row)

    rows_loop(count, one, rolled)


def branch_backward(count, windows, bounds, x, gain, w, s, wait, send, rolled=False):
    w_qkv, w_out, w_up, w_down = w
    lower(count, s)
    send("gl")
    feed_backward(count, s, w_up, w_down, wait, rolled)
    send("du")
    wait(5)
    norm_two_backward(count, gain[1:2, :], s)
    send("da")
    s.grad_mixed[...] = mm_t(s.da[...], w_out[...]).astype(bf16)
    attention_backward(windows, bounds, s.qkv, s.grad_mixed, s.lse_rows, s.grad_qkv, rolled)
    send("dqkv")
    wait(6)
    multiply_into(s.low, mm_t, s.grad_qkv, w_qkv, rolled, True)
    norm_one_backward(count, x, gain[0:1, :], s)


class Refs:
    def __init__(self, names, refs, constants):
        self.__dict__.update(zip(names, refs), **constants)


class Copies:
    def __init__(self, sems, first):
        self.sems, self.next, self.open = sems, first, []

    def start(self, source, target):
        copy = pltpu.make_async_copy(source, target, self.sems.at[self.next])
        self.next += 1
        copy.start()
        return copy

    def out(self, source, target):
        self.open.append(self.start(source, target))

    def finish(self):
        for copy in self.open:
            copy.wait()


def slot_rows(ops, slot, mb, count):
    return ops.at[slot, pl.ds(mb * count, count), :]


def send_slots(copies, ops, s, mb, count):
    wide = {"act": (SLOT_ACT, 4), "du": (SLOT_DU, 4), "dqkv": (SLOT_DQKV, 3)}
    flat = {"n1": SLOT_N1, "mixed": SLOT_MIXED, "n2": SLOT_N2, "gl": SLOT_GL, "da": SLOT_DA}

    def send(what):
        if what in flat:
            copies.out(getattr(s, what), slot_rows(ops, flat[what], mb, count))
        elif what in wide:
            source = {"act": "act", "du": "du", "dqkv": "grad_qkv"}[what]
            slot, parts = wide[what]
            for k in range(parts):
                copies.out(getattr(s, source).at[:, pl.ds(k * D, D)], slot_rows(ops, slot + k, mb, count))

    return send


def weight_scratch():
    return dict(
        v_qkv=pltpu.VMEM((D, 3 * D), bf16),
        v_out=pltpu.VMEM((D, D), bf16),
        v_up=pltpu.VMEM((D, FF), bf16),
        v_down=pltpu.VMEM((FF, D), bf16),
    )


def forward_scratch(count):
    return dict(
        n1=pltpu.VMEM((count, D), bf16),
        mixed=pltpu.VMEM((count, D), bf16),
        n2=pltpu.VMEM((count, D), bf16),
        act=pltpu.VMEM((count, FF), bf16),
    )


def shared_scratch(count):
    return dict(
        qkv=pltpu.VMEM((count, 3 * D), bf16),
        lse=pltpu.VMEM((3, 16, 256), f32),
        att=pltpu.VMEM((count, D), f32),
        hidden=pltpu.VMEM((count, D), f32),
        slope=pltpu.VMEM((count, FF), bf16),
        low=pltpu.VMEM((count, D), f32),
    )


def backward_scratch(count):
    return dict(
        grad=pltpu.VMEM((count, D), f32),
        gl=pltpu.VMEM((count, D), bf16),
        du=pltpu.VMEM((count, FF), bf16),
        da=pltpu.VMEM((count, D), bf16),
        grad_mixed=pltpu.VMEM((count, D), bf16),
        grad_qkv=pltpu.VMEM((count, 3 * D), bf16),
        sums=pltpu.VMEM((48, D), f32),
    )


def routed_bounds(column_slots):
    bounds = []
    for slot_start in SLOT_STARTS[1:]:
        bounds.append(jnp.sum(jnp.where(column_slots < slot_start, 1, 0)))
    return bounds


def routed_windows(bounds):
    middle = pl.multiple_of(jnp.minimum(bounds[0] // 16 * 16, 160), 16)
    return ((0, 0, 208), (1, middle, 224), (2, 224, 160))


FULL_BOUNDS = SLOT_STARTS[1:] + (ROW_LEN,)
FULL_WINDOWS = ((0, 0, 208), (1, 192, 208), (2, 384, 160))
FIXED_WINDOWS = ((0, 0, 208), (1, 32, 352), (2, 224, 160))


def flatten(target, source):
    target[PAIR - 16 :, :] = jnp.zeros((16, D), target.dtype)
    target[0 : 2 * ROW_LEN, :] = source[...].reshape(2 * ROW_LEN, D)


def running(amounts):
    return tuple(sum(amounts[:place]) for place in range(len(amounts)))


def planned(section):
    steps = len(YCOUNT[section])
    done = {}
    for k in range(STRIPS):
        place = BLOCKS[section].index(k)
        done[k] = next(t for t, before in enumerate(running(AMOUNTS[section] + (0,))[1:]) if before > place) - 1
    for k in range(8, 12):
        done[k] = max(done[k] for k in range(8, 12))
    sequence, taken, place = [], [], 0
    for t in range(-1, steps - 1):
        group = YFIRST[section][place : place + YCOUNT[section][t + 1]]
        place += len(group)
        hasty = [k for k, begin in zip(EARLY[section], EARLY_BEGIN[section]) if begin == t]
        for k in (*group, *hasty):
            sequence.append(k)
            taken.append(t)
    leave, last = [], -1
    for n, k in enumerate(sequence):
        last = max(last, done[k], taken[n] - 2)
        leave.append(last)
        assert last < taken[n] and (n < RING or taken[n - RING] <= last)
    sums, last = [-1] * (steps + 3), 1
    for a, k in enumerate(YFIRST[section]):
        last = max(last + 1, taken[sequence.index(k)] + 1)
        sums[last] = a
    return tuple(sequence), tuple(leave.count(t) for t in range(-1, steps - 1)), tuple(sums)


def parts_of(value):
    high = value.astype(bf16)
    return high, (value - high.astype(f32)).astype(bf16)


def launch(kernel, inputs, outputs, scratch, name, flops, collective_id=None, **constants):
    names = tuple(inputs) + tuple(outputs) + tuple(scratch)
    places = list(inputs)
    aliases = {}
    for k, (_, _, _, same) in enumerate(outputs.values()):
        if same is not None:
            aliases[places.index(same)] = k
    params = dict(vmem_limit_bytes=VMEM_LIMIT, has_side_effects=True)
    if collective_id is not None:
        params["collective_id"] = collective_id
    found = pl.pallas_call(
        lambda *refs: kernel(Refs(names, refs, constants)),
        out_shape=[jax.ShapeDtypeStruct(shape, kind) for shape, kind, _, _ in outputs.values()],
        in_specs=[pl.BlockSpec(memory_space=space) for _, space in inputs.values()],
        out_specs=[pl.BlockSpec(memory_space=space) for _, _, space, _ in outputs.values()],
        scratch_shapes=list(scratch.values()),
        input_output_aliases=aliases,
        compiler_params=pltpu.CompilerParams(**params),
        cost_estimate=pl.CostEstimate(flops=flops, bytes_accessed=30 * 2**20, transcendentals=0),
        name=name,
    )(*(array for array, _ in inputs.values()))
    return dict(zip(outputs, found))


def routed_forward_kernel(mb, r):
    w = (r.v_qkv, r.v_out, r.v_up, r.v_down)
    section = lax.axis_index("section")
    places, mine = both_rows(mb)

    @pl.when(section == 0)
    def _():
        copies = Copies(r.sems, 0)
        tok_in = copies.start(r.tokens, r.pair)
        loads = [copies.start(a, b) for a, b in zip((r.w_qkv, r.w_out, r.w_up, r.w_down), w)]
        chosen = Chosen(r.chosen, r.layout, mb)
        r.v_picks[...] = chosen.picks(places, mine)
        bounds = chosen.bounds()
        for k in range(5):
            r.bounds[0, k] = bounds[k]
        tok_in.wait()
        flatten(r.flat, r.pair)
        r.x[...] = mm(r.v_picks[...], r.flat[...])
        r.x_low[...] = r.x[...].astype(bf16)
        copies.out(r.x_low, r.st_x)
        slots = send_slots(copies, r.ops, r, mb, CAPACITY)

        def send(what):
            slots(what)
            if what == "qkv":
                copies.out(r.qkv, r.st_qkv)
            elif what == "mixed":
                r.lse_rows[...] = lse_by_row(r.lse, windows[1][1], bounds)
                copies.out(r.lse_rows, r.st_lse)
            elif what == "n2":
                copies.out(r.hidden, r.st_hidden)
            elif what == "act":
                copies.out(r.slope, r.st_slope)

        windows = routed_windows(bounds)
        branch_forward(
            CAPACITY, windows, bounds, r.x, r.gain, r.bias, w, r, lambda i: loads[i].wait(), send, mb == 1
        )
        router = r.router[...].reshape(1, D)

        def add(rows):
            branch = r.att[rows, :] + r.low[rows, :]
            r.low[rows, :] = branch
            here = r.x[rows, :]
            gates = jax.nn.sigmoid(jnp.sum(here * router, axis=-1, keepdims=True))
            r.y_low[rows, :] = (here + gates * branch).astype(bf16)

        rows_loop(CAPACITY, add)
        copies.out(r.y_low, r.y0p)
        copies.out(r.low, r.st_branch)
        copies.out(r.v_picks, r.picks_out)
        copies.finish()

    if mb == 0:
        @pl.when(section == 1)
        def _():
            copies = Copies(r.sems, 0)
            copies.start(r.tokens, r.pair).wait()
            flatten(r.flat, r.pair)
            copies.start(r.cotangent, r.pair).wait()
            flatten(r.flat_two, r.pair)
            for row in range(2):
                chosen = Chosen(r.chosen, r.layout, row)
                places, mine = both_rows(row)
                here = (to_slot(places, chosen.table) == row_places(FULL)) & mine
                fresh = here & (chosen.taken(places) == 0)
                r.v_x[row] = mm(one_hot(fresh), r.flat[...]).astype(bf16)
                r.v_cot[row] = mm(one_hot(here), r.flat_two[...]).astype(bf16)
                back = from_slot(lane_places(FULL), chosen.table)
                picks = chosen.picks(back, lane_places(FULL) < ROW_LEN)
                r.v_slot_picks[row] = picks
                r.v_spread[row] = jnp.transpose(picks)
                r.v_spares[row] = chosen.spares(back)
            for source, target in (
                (r.v_x, r.x_rest),
                (r.v_cot, r.cot),
                (r.v_slot_picks, r.slot_picks),
                (r.v_spread, r.spread),
                (r.v_spares, r.spares),
            ):
                copies.out(source, target)
            copies.finish()


def routed_outputs_kernel(r):
    @pl.when(lax.axis_index("section") == 0)
    def _():
        copies = Copies(r.sems, 0)
        loads = [
            copies.start(a, b)
            for a, b in (
                (r.tokens, r.pair), (r.picks_a, r.v_picks.at[0]), (r.picks_b, r.v_picks.at[1]),
                (r.y_a, r.v_y.at[0]), (r.y_b, r.v_y.at[1]),
            )
        ]
        for copy in loads:
            copy.wait()
        flatten(r.flat, r.pair)
        ones = jnp.ones((CAPACITY, 128), bf16)
        spread = t_mm(r.v_picks[0], r.v_y[0]) + t_mm(r.v_picks[1], r.v_y[1])
        is_in = (t_mm(r.v_picks[0], ones) + t_mm(r.v_picks[1], ones))[:, :1]
        result = jnp.where(is_in > 0.5, spread, r.flat[...].astype(f32)).astype(bf16)
        r.pair[...] = result[: 2 * ROW_LEN, :].reshape(ROW_LEN, 2, D)
        copies.out(r.pair, r.acts)
        copies.finish()


def full_kernel(mb, r):
    w = (r.v_qkv, r.v_out, r.v_up, r.v_down)

    @pl.when(lax.axis_index("section") == 1)
    def _():
        copies = Copies(r.sems, 0)
        first = [
            copies.start(a, b)
            for a, b in ((r.x_rest.at[mb], r.tok), (r.y0p, r.low_in), (r.spread.at[mb], r.v_spread))
        ]
        loads = [copies.start(a, b) for a, b in zip((r.w_qkv, r.w_out, r.w_up, r.w_down), w)]
        cot_in = copies.start(r.cot.at[mb], r.gl)
        picks_in = [copies.start(r.slot_picks.at[mb], r.v_picks), copies.start(r.spares.at[mb], r.v_spares)]
        for copy in first:
            copy.wait()
        r.x[...] = r.tok[...].astype(f32) + mm(r.v_spread[...], r.low_in[...])
        send = send_slots(copies, r.ops, r, mb, FULL)
        branch_forward(
            FULL, FULL_WINDOWS, FULL_BOUNDS, r.x, r.gain, r.bias, w, r, lambda i: loads[i].wait(), send
        )
        cot_in.wait()

        def add(rows):
            r.tok[rows, :] = (r.x[rows, :] + r.att[rows, :] + r.low[rows, :]).astype(bf16)
            r.grad[rows, :] = r.gl[rows, :].astype(f32)

        rows_loop(FULL, add)
        copies.out(r.tok, r.y1)
        r.lse_rows = r.lse
        branch_backward(FULL, FULL_WINDOWS, FULL_BOUNDS, r.x, r.gain, w, r, lambda i: None, send)
        r.sums[32:48, :] = jnp.zeros((16, D), f32)
        copies.out(r.sums, r.sums_out)

        def join(rows):
            total = r.gl[rows, :].astype(f32) + r.grad[rows, :]
            r.low[rows, :] = total
            r.high[rows, :] = total.astype(bf16)

        rows_loop(FULL, join)
        copies.out(r.low, r.dx)
        for copy in picks_in:
            copy.wait()
        r.v_sent[...] = mm(r.v_picks[...], r.high[...]).astype(bf16)
        copies.out(r.v_sent, r.sent.at[0:CAPACITY, :])
        if mb == 0:
            r.v_sent_spares[...] = mm(r.v_spares[...], r.high[...]).astype(bf16)
            copies.out(r.v_sent_spares, r.sent.at[CAPACITY:, :])
        copies.finish()


def placed_gradients(chosen, part, spare, out):
    places = lane_places(FULL)
    picks = chosen.picks(places, places < ROW_LEN)
    high, rest = parts_of(part[...])
    total = t_mm(picks, high) + t_mm(chosen.spares(places), spare[...]) + t_mm(picks, rest)
    out[...] = total[0:ROW_LEN, :].reshape(ROW_LEN, 1, D)


def gates_backward(r, bounds, rolled=False):
    router = r.router[...].reshape(1, D)
    r.sums[32:48, :] = jnp.zeros((16, D), f32)

    def gate(rows):
        here = r.x_low[rows, :].astype(f32)
        gates = jax.nn.sigmoid(jnp.sum(here * router, axis=-1, keepdims=True))
        dy = r.v_back[rows, :].astype(f32)
        slopes = jnp.sum(r.v_part[rows, :] * dy, axis=-1, keepdims=True) * gates * (1.0 - gates)
        r.grad[rows, :] = gates * dy
        r.sums[32:40, :] += fold(slopes * here)
        r.v_part[rows, :] = dy + slopes * router

    rows_loop(CAPACITY, gate, rolled)
    r.sums[40:41, :] = jnp.where(lane_places(D) == 0, bounds[1], 0).astype(f32)


def routed_backward_kernel(mb, r):
    w = (r.v_qkv, r.v_out, r.v_up, r.v_down)
    section = lax.axis_index("section")

    @pl.when(section == 0)
    def _():
        copies = Copies(r.sems, 0)

        def load(*pairs):
            return [copies.start(a, b) for a, b in pairs]

        first = load((r.back.at[0:CAPACITY, :], r.v_back), (r.st_x, r.x_low), (r.st_branch, r.v_part))
        chunks = []
        for j in range(4):
            cols = pl.ds(j * CHUNK, CHUNK)
            chunks.append(
                load((r.w_down.at[cols, :], r.v_down.at[cols, :]), (r.st_slope.at[:, cols], r.slope.at[:, cols]))
            )
        chunks.append(load((r.w_up, r.v_up)))
        chunks.append(
            load((r.st_hidden, r.hidden), (r.w_out, r.v_out), (r.st_qkv, r.qkv), (r.st_lse, r.lse_rows))
        )
        chunks.append(load((r.w_qkv, r.v_qkv)))
        if mb == 0:
            spare_in = copies.start(r.back.at[CAPACITY:, :], r.v_spares)
        bounds = [r.bounds[0, k] for k in range(5)]
        for copy in first:
            copy.wait()
        gates_backward(r, bounds)

        def wait(i):
            for copy in chunks[i]:
                copy.wait()

        send = send_slots(copies, r.ops, r, mb, CAPACITY)
        branch_backward(CAPACITY, FIXED_WINDOWS, bounds, r.x_low, r.gain, w, r, wait, send, True)
        copies.out(r.sums, r.sums_out)

        def join(rows):
            r.v_part[rows, :] += r.grad[rows, :]

        rows_loop(CAPACITY, join)
        if mb == 0:
            spare_in.wait()
            placed_gradients(Chosen(r.chosen, r.layout, 0), r.v_part, r.v_spares, r.row)
            copies.out(r.row, r.grads.at[0])
        else:
            copies.out(r.v_part, r.part)
        copies.finish()


def full_outputs_kernel(r):
    @pl.when(lax.axis_index("section") == 1)
    def _():
        copies = Copies(r.sems, 0)
        halves = (r.v_dx_a, r.v_dx_b)
        dx_in = [copies.start(r.dx_a, halves[0]), copies.start(r.dx_b, halves[1])]
        y_in = [copies.start(r.y1_a, r.v_y1.at[0]), copies.start(r.y1_b, r.v_y1.at[1])]
        dx_in[1].wait()
        chosen = Chosen(r.chosen, r.layout, 1)
        back = from_slot(lane_places(FULL), chosen.table)
        r.v_spares[...] = mm(chosen.spares(back), r.v_dx_b[...].astype(bf16)).astype(bf16)
        copies.out(r.v_spares, r.sent_spares)
        for copy in y_in:
            copy.wait()
        rows = row_places(PAIR)
        total = jnp.zeros((PAIR, D), f32)
        for row in range(2):
            table = crop_table(r.layout, row)
            slots = lane_places(FULL)
            target = jnp.where(slots < ROW_LEN, 2 * from_slot(slots, table) + row, -1)
            total = total + mm(one_hot(rows == target), r.v_y1[row])
        r.pair[...] = total[: 2 * ROW_LEN, :].reshape(ROW_LEN, 2, D).astype(bf16)
        copies.out(r.pair, r.acts)
        dx_in[0].wait()
        for row in range(2):
            table = crop_table(r.layout, row)
            slots = lane_places(FULL)
            move = one_hot((from_slot(slots, table) == row_places(FULL)) & (slots < ROW_LEN))
            high, rest = parts_of(halves[row][...])
            total = mm(move, high) + mm(move, rest)
            target = (r.row, r.row_two)[row]
            target[...] = total[0:ROW_LEN, :].reshape(ROW_LEN, 1, D)
            copies.out(target, r.grads.at[row])
        copies.finish()


def closing_kernel(r):
    def row_copy():
        return pltpu.make_async_copy(r.row, r.grads.at[1], r.sems.at[0])

    @pl.when(lax.axis_index("section") == 0)
    def _():
        placed_gradients(Chosen(r.chosen, r.layout, 1), r.rows, r.back_spares, r.row)
        row_copy().start()

    for name in ("qkv", "out", "up", "down"):
        getattr(r, "o_" + name)[...] = getattr(r, "g_" + name)[...]
    width = D // r.ways
    me = lax.axis_index("dp")
    turned = pltpu.roll(r.small[...], lax.rem(D - width * me, D), axis=1)
    r.o_gain[...] = turned[0:2, 0:width]
    r.o_bias[...] = turned[2:4, 0:width]
    r.o_router[...] = r.small[4, :]
    big = jnp.sum(r.small[5:6, :]).astype(i32)
    r.o_counts[0] = big
    r.o_counts[1] = 2 * CAPACITY * r.ways - big
    pl.when(lax.axis_index("section") == 0)(lambda: row_copy().wait())


def gradient_kernel(r):
    me = lax.axis_index("dp")
    zero = me - me
    section = lax.axis_index("section")
    routed, full = section == 0, section == 1
    c = lax.rem(me, 2)
    y = lax.rem(me // 2, 2)
    z = me // 4
    sibling = {"dp": me + 1 - 2 * c}
    beside = {"dp": me + 2 - 4 * y}
    above, below = {"dp": me + 4}, {"dp": me - 4}
    far = {"dp": me + 8 - 16 * (z // 2)}
    paired = {"dp": me + 4 - 8 * lax.rem(z, 2)}

    barrier = pltpu.get_barrier_semaphore()

    def greet(device):
        pl.semaphore_signal(barrier, inc=1, device_id=device, device_id_type=MESH_ID)

    for device in (sibling, beside, far):
        greet(device)
    pl.when(z > 0)(lambda: greet(below))
    pl.when(z < 3)(lambda: greet(above))
    pl.when(full)(lambda: greet({"section": 0}))

    def strip(k):
        return pl.ds(pl.multiple_of(k * STRIP, STRIP), STRIP)

    def remote(source, target, sems, index, device):
        return pltpu.make_async_remote_copy(
            source, target, sems.at[(0,) + index], sems.at[(1,) + index], device_id=device, device_id_type=MESH_ID
        )

    def listed(orders, n):
        found = []
        for order in orders:
            value = zero + order[0]
            for place, entry in enumerate(order[1:], 1):
                value = jnp.where(n == place, entry, value)
            found.append(value)
        return jnp.where(routed, found[0], found[1])

    def placed(orders, k):
        found = []
        for order in orders:
            value = zero
            for place, entry in enumerate(order):
                value = jnp.where(k == entry, place, value)
            found.append(value)
        return jnp.where(routed, found[0], found[1])

    def block_at(n):
        return listed(BLOCKS, n)

    plans = planned(0), planned(1)
    sequences, leaving, sums_at = zip(*plans)

    def place_of(k):
        return placed(sequences, k)

    def late(a):
        return listed(YFIRST, a)

    def sum_at(t):
        return jnp.where((t >= 0) & (t < len(sums_at[0])), listed(sums_at, t), -1)

    def early(b):
        return jnp.where(routed, EARLY[0][b], EARLY[1][b])

    def early_begin(b):
        return jnp.where(routed, EARLY_BEGIN[0][b], EARLY_BEGIN[1][b])

    def core_copy(k):
        slot = lax.rem(place_of(k), RING)
        return remote(r.part.at[:, :, 1 - c, strip(k), :], r.core_in.at[slot], r.core_sem, (k,), sibling)

    def side_copy(a):
        return remote(r.part.at[:, 1 - y, c, strip(late(a)), :], r.side_in.at[:, strip(a), :], r.side_sem, (a,), beside)

    def up_send(s, a):
        return remote(
            r.part.at[s, y, c, strip(late(a)), :], r.up_in.at[s - z - 1, strip(a), :], r.up_sem, (s, a), above
        )

    def up_take(s, a):
        return remote(r.part.at[s, y, c, strip(late(a)), :], r.up_in.at[s - z, strip(a), :], r.up_sem, (s, a), below)

    def down_send(s, a):
        return remote(
            r.part.at[s, y, c, strip(late(a)), :], r.down_in.at[z - 1 - s, strip(a), :], r.down_sem, (s, a), below
        )

    def down_take(s, a):
        return remote(
            r.part.at[s, y, c, strip(late(a)), :], r.down_in.at[z - s, strip(a), :], r.down_sem, (s, a), above
        )

    def early_rows(b):
        return strip(early(b))

    def early_up_send(s, b):
        return remote(
            r.part.at[s, :, c, early_rows(b), :], r.early_up.at[b, s - z - 1], r.early_sem, (0, s, b), above
        )

    def early_up_take(s, b):
        return remote(r.part.at[s, :, c, early_rows(b), :], r.early_up.at[b, s - z], r.early_sem, (0, s, b), below)

    def early_down_send(s, b):
        return remote(
            r.part.at[s, :, c, early_rows(b), :], r.early_down.at[b, z - 1 - s], r.early_sem, (1, s, b), below
        )

    def early_down_take(s, b):
        return remote(r.part.at[s, :, c, early_rows(b), :], r.early_down.at[b, z - s], r.early_sem, (1, s, b), above)

    def early_side(b):
        return remote(
            r.part.at[z, 1 - y, c, early_rows(b), :], r.early_side.at[b], r.early_side_sem, (b,), beside
        )

    def small_copy(k):
        device = (sibling, beside, paired, far)[k]
        return remote(r.small.at[k], r.small_in.at[k], r.small_sem, (k,), device)

    def across():
        return remote(r.small.at[4], r.cross_in, r.cross_sem, (), {"section": 1})

    s = Refs((), (), dict(r.__dict__, gl=r.grad_mixed, du=r.slope, v_back=r.da))
    v_out = r.v_down.at[pl.ds(0, D), :]
    v_qkv = r.v_up.at[:, pl.ds(0, 3 * D)]
    bounds = [r.bounds[0, k] for k in range(5)]

    def load(k, source, target):
        return pltpu.make_async_copy(source, target, r.sems.at[k])

    first = [load(0, r.back, r.da), load(1, r.st_x, r.x_low), load(2, r.st_branch, r.v_part)]
    middle = [load(12, r.st_hidden, r.hidden), load(13, r.st_qkv, r.qkv), load(14, r.st_lse, r.lse_rows)]
    again = [load(15, r.w_out, v_out), load(16, r.w_qkv, v_qkv)]
    feed_in = [load(3, r.w_down, r.v_down), load(4, r.st_slope, r.slope), load(5, r.w_up, r.v_up)]
    part_out = load(17, r.v_part, r.part_rows)

    def each(copies, act):
        for copy in copies:
            getattr(copy, act)()

    def thirds(target, left, right):
        def one(j, _):
            cols = pl.ds(pl.multiple_of(j * 256, 256), 256)
            target[:, cols] = mm_t(left[...], right[cols, :])
            return 0

        lax.fori_loop(0, 3, one, 0)

    def phase_feed():
        each(feed_in, "wait")

        def one(j, _):
            cols = pl.ds(pl.multiple_of(j * CHUNK, CHUNK), CHUNK)
            grad = mm_t(s.gl[...], r.v_down[cols, :])
            for start in range(0, CAPACITY, BLOCK):
                slope = r.slope[start : start + BLOCK, cols].astype(f32)
                r.slope[start : start + BLOCK, cols] = (grad[start : start + BLOCK, :] * slope).astype(bf16)
            return 0

        lax.fori_loop(0, 4, one, 0)
        thirds(r.low, s.du, r.v_up)
        each(again, "start")

    def phase_norm():
        each(middle, "wait")
        norm_two_backward(CAPACITY, r.gain[1:2, :], s)
        again[0].wait()
        r.grad_mixed[...] = mm_t(r.da[...], v_out[...]).astype(bf16)

    def phase_window(*kinds):
        windows = [FIXED_WINDOWS[kind] for kind in kinds]
        attention_backward(windows, bounds, r.qkv, r.grad_mixed, r.lse_rows, r.grad_qkv, True)

    def phase_last():
        again[1].wait()
        thirds(r.low, r.grad_qkv, v_qkv)
        norm_one_backward(CAPACITY, r.x_low, r.gain[0:1, :], s)

        def join(rows):
            r.v_part[rows, :] += r.grad[rows, :]

        rows_loop(CAPACITY, join, True)
        part_out.start()

    def slot_pair(b):
        left = jnp.where(b < 3, SLOT_N1, jnp.where(b == 3, SLOT_MIXED, jnp.where(b < 8, SLOT_N2, b - 8 + SLOT_ACT)))
        right = jnp.where(b < 3, b + SLOT_DQKV, jnp.where(b == 3, SLOT_DA, jnp.where(b < 8, b - 4 + SLOT_DU, SLOT_GL)))
        return left, right

    def operand_copies(n, left_rows, right_rows):
        left, right = slot_pair(block_at(n))
        side = lax.rem(n, 2)
        return (
            pltpu.make_async_copy(r.ops.at[left, 0:left_rows, :], r.left.at[side, 0:left_rows, :], r.load_sem.at[0, side]),
            pltpu.make_async_copy(
                r.ops.at[right, 0:right_rows, :], r.right.at[side, 0:right_rows, :], r.load_sem.at[1, side]
            ),
        )

    def operands(n, act):
        pl.when(routed)(lambda: each(operand_copies(n, 2 * CAPACITY, CAPACITY), act))
        pl.when(full)(lambda: each(operand_copies(n, 2 * FULL, 2 * FULL), act))

    def block(n):
        side = lax.rem(n, 2)
        b = block_at(n)
        operands(n, "wait")
        pl.when(n + 1 < STRIPS)(lambda: operands(n + 1, "start"))
        second = pl.ds(CAPACITY, CAPACITY)

        @pl.when(routed)
        def _():
            @pl.when(b >= 8)
            def _():
                r.right[side, second, :] = s.gl[...]

            @pl.when((b >= 4) & (b < 8))
            def _():
                r.right[side, second, :] = s.du[:, pl.ds(pl.multiple_of((b - 4) * D, D), D)]

            @pl.when(b == 3)
            def _():
                r.right[side, second, :] = r.da[...]

            @pl.when(b < 3)
            def _():
                r.right[side, second, :] = r.grad_qkv[:, pl.ds(pl.multiple_of(b * D, D), D)]

        def multiply(rows):
            def half(h, _):
                cols = pl.ds(pl.multiple_of(h * 384, 384), 384)
                product = t_mm(r.left[side, 0:rows, cols], r.right[side, 0:rows, :]).astype(bf16)

                @pl.when(b < 8)
                def _():
                    r.part[pl.ds(2 * h, 2), :, :, strip(b), :] = product.reshape(2, 2, 2, STRIP, D)

                @pl.when(b >= 8)
                def _():
                    r.part[b - 8, h, :, 384:576, :] = product.reshape(2, 192, D)

                return 0

            lax.fori_loop(0, 2, half, 0)

        pl.when(routed)(lambda: multiply(2 * CAPACITY))
        pl.when(full)(lambda: multiply(2 * FULL))

    def core_start(k):
        n = place_of(k)
        pl.when(n >= RING)(lambda: pl.semaphore_wait(r.free_sem.at[lax.rem(n, RING)], 1))
        core_copy(k).start()

    def add_into(target, source):
        (a, ia), (b, ib) = target, source
        a[ia] = (a[ia].astype(f32) + b[ib].astype(f32)).astype(bf16)

    def write(k, value):
        @pl.when(k < 3)
        def _():
            r.g_qkv[:, pl.ds(pl.multiple_of(k * D, D), D)] = value

        @pl.when(k == 3)
        def _():
            r.g_out[...] = value

        @pl.when((k > 3) & (k < 8))
        def _():
            r.g_up[:, pl.ds(pl.multiple_of((k - 4) * D, D), D)] = value

        @pl.when(k >= 8)
        def _():
            r.g_down[strip(k - 8), :] = value

    def core_arrived(k):
        n = place_of(k)
        slot = lax.rem(n, RING)
        core_copy(k).wait_recv()

        def one(i, _):
            zs, ys = i // 2, lax.rem(i, 2)
            add_into((r.part, (zs, ys, c, strip(k))), (r.core_in, (slot, zs, ys)))
            return 0

        lax.fori_loop(0, 8, one, 0)

        @pl.when(n + RING < STRIPS)
        def _():
            pl.semaphore_signal(r.free_sem.at[slot], inc=1, device_id=sibling, device_id_type=MESH_ID)

    def early_strip(b, t):
        rows, begin = early_rows(b), early_begin(b)
        pl.when(t == begin)(lambda: core_arrived(early(b)))

        @pl.when((t == begin + 2 * z) & (z < 3))
        def _():
            def one(i, _):
                k = 3 - i

                @pl.when(z > 0)
                def _():
                    early_up_take(k, b).wait_recv()
                    for ys in range(2):
                        add_into((r.part, (k, ys, c, rows)), (r.early_up, (b, k - z, ys)))

                early_up_send(k, b).start()
                return 0

            lax.fori_loop(0, 3 - z, one, 0)

        @pl.when((t == begin + 6 - 2 * z) & (z > 0))
        def _():
            def one(k, _):
                @pl.when(z < 3)
                def _():
                    early_down_take(k, b).wait_recv()
                    for ys in range(2):
                        add_into((r.part, (k, ys, c, rows)), (r.early_down, (b, z - k, ys)))

                early_down_send(k, b).start()
                return 0

            lax.fori_loop(0, z, one, 0)

        @pl.when(t == begin + 8)
        def _():
            @pl.when(z > 0)
            def _():
                early_up_take(z, b).wait_recv()
                for ys in range(2):
                    add_into((r.part, (z, ys, c, rows)), (r.early_up, (b, 0, ys)))

            @pl.when(z < 3)
            def _():
                early_down_take(z, b).wait_recv()
                for ys in range(2):
                    add_into((r.part, (z, ys, c, rows)), (r.early_down, (b, 0, ys)))

            early_side(b).start()

        @pl.when(t == begin + 10)
        def _():
            early_side(b).wait_recv()
            write(early(b), r.part[z, y, c, rows, :].astype(f32) + r.early_side[b].astype(f32))

    def serve(t):
        turn = jnp.minimum(t + 1, len(YCOUNT[0]) - 1)
        many = jnp.where(t + 1 < len(YCOUNT[0]), listed(YCOUNT, turn), 0)
        start = listed(tuple(running(counts) for counts in YCOUNT), turn)

        def set_out(i, _):
            core_arrived(late(start + i))
            side_copy(start + i).start()
            return 0

        lax.fori_loop(0, many, set_out, 0)
        for b in range(HASTE):
            early_strip(b, t)

        a_sum = sum_at(t)

        @pl.when(a_sum >= 0)
        def _():
            a = a_sum
            side_copy(a).wait_recv()

            def one(zs, _):
                add_into((r.part, (zs, y, c, strip(late(a)))), (r.side_in, (zs, strip(a))))
                return 0

            lax.fori_loop(0, 4, one, 0)

        au = sum_at(t - 2 * z)

        @pl.when((au >= 0) & (z < 3))
        def _():
            def one(i, _):
                k = 3 - i

                @pl.when(z > 0)
                def _():
                    up_take(k, au).wait_recv()
                    add_into((r.part, (k, y, c, strip(late(au)))), (r.up_in, (k - z, strip(au))))

                up_send(k, au).start()
                return 0

            lax.fori_loop(0, 3 - z, one, 0)

        ad = sum_at(t - 6 + 2 * z)

        @pl.when((ad >= 0) & (z > 0))
        def _():
            def one(k, _):
                @pl.when(z < 3)
                def _():
                    down_take(k, ad).wait_recv()
                    add_into((r.part, (k, y, c, strip(late(ad)))), (r.down_in, (z - k, strip(ad))))

                down_send(k, ad).start()
                return 0

            lax.fori_loop(0, z, one, 0)

        a_final = sum_at(t - 6)

        @pl.when(a_final >= 0)
        def _():
            a = a_final
            r.final[...] = r.part[z, y, c, strip(late(a)), :].astype(f32)

            @pl.when(z > 0)
            def _():
                up_take(z, a).wait_recv()
                r.final[...] += r.up_in[0, strip(a), :].astype(f32)

            @pl.when(z < 3)
            def _():
                down_take(z, a).wait_recv()
                r.final[...] += r.down_in[0, strip(a), :].astype(f32)

            write(late(a), r.final[...])

        @pl.when(t == PHASES[-1] + 1)
        def _():
            pl.when(full)(lambda: copy_sums())
            for k in range(6):
                rows = slice(8 * k, 8 * k + 8)
                r.small[0, k : k + 1, :] = jnp.sum(r.sums_a[rows, :] + r.sums[rows, :], axis=0, keepdims=True)
            r.small[0, 6:8, :] = jnp.zeros((2, D), f32)
            small_copy(0).start()

        for k in range(4):

            @pl.when(t == 2 * k + PHASES[-1] + 3)
            def _():
                small_copy(k).wait_recv()
                r.small[k + 1] = r.small[k] + r.small_in[k]
                if k < 3:
                    small_copy(k + 1).start()
                else:
                    pl.when(routed)(lambda: across().start())

    def copy_sums():
        r.sums[...] = r.sums_b[...]

    @pl.when(routed)
    def _():
        each(first, "start")

    operands(zero, "start")

    @pl.when(routed)
    def _():
        each(feed_in + middle, "start")
        each(first, "wait")
        gates_backward(s, bounds, True)

        def one(rows):
            s.gl[rows, :] = r.grad[rows, :].astype(bf16)

        rows_loop(CAPACITY, one, True)

    pl.semaphore_wait(barrier, 3 + (z > 0).astype(i32) + (z < 3).astype(i32) + routed.astype(i32))

    def step(turn, _):
        t = turn - 1
        serve(t)
        index = jnp.minimum(turn, len(AMOUNTS[0]) - 1)
        begin = listed(tuple(running(amounts) for amounts in AMOUNTS), index)
        amount = jnp.where(turn < len(AMOUNTS[0]), listed(AMOUNTS, index), 0)
        lax.fori_loop(0, amount, lambda i, _: (block(begin + i), 0)[1], 0)
        index = jnp.minimum(turn, len(leaving[0]) - 1)
        begin_core = listed(tuple(running(counts) for counts in leaving), index)
        amount = jnp.where(turn < len(leaving[0]), listed(leaving, index), 0)
        lax.fori_loop(0, amount, lambda i, _: (core_start(listed(sequences, begin_core + i)), 0)[1], 0)
        pl.when(routed & (t == PHASES[0]))(phase_feed)
        pl.when(routed & (t == PHASES[1]))(phase_norm)
        pl.when(routed & (t == PHASES[2]))(lambda: phase_window(0, 2))
        pl.when(routed & (t == PHASES[3]))(lambda: phase_window(1))
        pl.when(routed & (t == PHASES[4]))(phase_last)
        return 0

    lax.fori_loop(0, 19, step, 0)
    r.small_out[...] = r.small[4]


    @pl.when(routed)
    def _():
        across().wait_send()
        part_out.wait()

    @pl.when(full)
    def _():
        across().wait_recv()
        r.small_out[4:6, :] = r.cross_in[4:6, :]


    lax.fori_loop(0, STRIPS, lambda k, _: (core_copy(k).wait_send(), 0)[1], 0)

    def drain(a, _):
        side_copy(a).wait_send()
        for k in range(1, 4):
            pl.when(k > z)(lambda k=k: up_send(k, a).wait_send())
        for k in range(3):
            pl.when(k < z)(lambda k=k: down_send(k, a).wait_send())
        return 0

    lax.fori_loop(0, LATE, drain, 0)
    for b in range(HASTE):
        early_side(b).wait_send()
        for k in range(1, 4):
            pl.when(k > z)(lambda k=k: early_up_send(k, b).wait_send())
        for k in range(3):
            pl.when(k < z)(lambda k=k: early_down_send(k, b).wait_send())
    for k in range(4):
        small_copy(k).wait_send()


HBM = pl.ANY
VMEM = pltpu.VMEM
SMEM = pltpu.SMEM


def body(
    tokens, layout, selected, cotangent, w_qkv, w_out, w_up, w_down, norm_gain, norm_bias, w_router
):
    ways = lax.axis_size("dp")
    common = dict(
        layout=(layout, SMEM),
        chosen=(selected, VMEM),
        gain=(norm_gain[0], VMEM),
        bias=(norm_bias[0], VMEM),
        router=(w_router, VMEM),
        w_qkv=(w_qkv[0], HBM),
        w_out=(w_out[0], HBM),
        w_up=(w_up[0], HBM),
        w_down=(w_down[0], HBM),
    )
    tokens = jnp.transpose(tokens, (1, 2, 0, 3)).reshape(ROW_LEN, 2, D)
    cotangent = jnp.transpose(cotangent, (1, 2, 0, 3)).reshape(ROW_LEN, 2, D)
    ops_spec = ((SLOTS, 2 * FULL, D), bf16, HBM)
    acts_spec = ((ROW_LEN, 2, D), bf16, HBM)
    grads_spec = ((2, ROW_LEN, 1, D), f32, HBM)
    stash_spec = dict(
        st_x=((CAPACITY, D), bf16, HBM, None),
        st_qkv=((CAPACITY, 3 * D), bf16, HBM, None),
        st_slope=((CAPACITY, FF), bf16, HBM, None),
        st_hidden=((CAPACITY, D), f32, HBM, None),
        st_branch=((CAPACITY, D), f32, HBM, None),
        st_lse=((16, CAPACITY), f32, HBM, None),
        bounds=((1, 8), i32, SMEM, None),
    )
    laid_spec = dict(
        x_rest=((2, FULL, D), bf16, HBM, None),
        cot=((2, FULL, D), bf16, HBM, None),
        slot_picks=((2, CAPACITY, FULL), bf16, HBM, None),
        spread=((2, FULL, CAPACITY), bf16, HBM, None),
        spares=((2, SPARE, FULL), bf16, HBM, None),
    )
    buffers = dict(sems=pltpu.SemaphoreType.DMA((40,)), **weight_scratch())
    ops = None
    handed, stashes, picks, y0ps = [], [], [], []
    for mb in range(2):
        inputs = dict(common, tokens=(tokens, HBM), cotangent=(cotangent, HBM))
        outputs = dict(
            ops=ops_spec + ("ops_old" if mb else None,), y0p=((CAPACITY, D), bf16, HBM, None), **stash_spec
        )
        scratch = dict(
            **buffers,
            pair=pltpu.VMEM((ROW_LEN, 2, D), bf16),
            flat=pltpu.VMEM((PAIR, D), bf16),
            v_picks=pltpu.VMEM((CAPACITY, PAIR), bf16),
            x=pltpu.VMEM((CAPACITY, D), f32),
            x_low=pltpu.VMEM((CAPACITY, D), bf16),
            lse_rows=pltpu.VMEM((16, CAPACITY), f32),
            y_low=pltpu.VMEM((CAPACITY, D), bf16),
            **forward_scratch(CAPACITY),
            **shared_scratch(CAPACITY),
        )
        outputs.update(picks_out=((CAPACITY, PAIR), bf16, HBM, None))
        if mb == 0:
            outputs.update(laid_spec)
            scratch.update(
                flat_two=pltpu.VMEM((PAIR, D), bf16),
                v_x=pltpu.VMEM((2, FULL, D), bf16),
                v_cot=pltpu.VMEM((2, FULL, D), bf16),
                v_slot_picks=pltpu.VMEM((2, CAPACITY, FULL), bf16),
                v_spread=pltpu.VMEM((2, FULL, CAPACITY), bf16),
                v_spares=pltpu.VMEM((2, SPARE, FULL), bf16),
            )
        else:
            inputs.update(ops_old=(ops, HBM))
        found = launch(
            functools.partial(routed_forward_kernel, mb), inputs, outputs, scratch, f"routed_forward_{mb}", 6 * 10**9
        )
        ops, y0p = found["ops"], found["y0p"]
        if mb == 0:
            laid = {name: (found[name], HBM) for name in laid_spec}
        picks.append(found["picks_out"])
        y0ps.append(y0p)
        stashes.append({name: (found[name], SMEM if name == "bounds" else HBM) for name in stash_spec})
        handed.append(lax.ppermute(y0p, "section", [(0, 1)]))
    acts = launch(
        routed_outputs_kernel,
        dict(
            tokens=(tokens, HBM), picks_a=(picks[0], HBM), picks_b=(picks[1], HBM), y_a=(y0ps[0], HBM), y_b=(y0ps[1], HBM)
        ),
        dict(acts=acts_spec + (None,)),
        dict(
            sems=pltpu.SemaphoreType.DMA((8,)),
            pair=pltpu.VMEM((ROW_LEN, 2, D), bf16),
            flat=pltpu.VMEM((PAIR, D), bf16),
            v_picks=pltpu.VMEM((2, CAPACITY, PAIR), bf16),
            v_y=pltpu.VMEM((2, CAPACITY, D), bf16),
        ),
        "routed_outputs",
        10**9,
    )["acts"]
    sums, returned, ends = [], [], []
    for mb in range(2):
        outputs = dict(
            ops=ops_spec + ("ops_old",),
            sent=((FULL if mb == 0 else CAPACITY, D), bf16, HBM, None),
            y1=((FULL, D), bf16, HBM, None),
            dx=((FULL, D), f32, HBM, None),
            sums_out=((48, D), f32, HBM, None),
        )
        found = launch(
            functools.partial(full_kernel, mb),
            dict(common, **laid, y0p=(handed[mb], HBM), ops_old=(ops, HBM)),
            outputs,
            dict(
                **buffers,
                tok=pltpu.VMEM((FULL, D), bf16),
                x=pltpu.VMEM((FULL, D), f32),
                low_in=pltpu.VMEM((CAPACITY, D), bf16),
                v_spread=pltpu.VMEM((FULL, CAPACITY), bf16),
                v_picks=pltpu.VMEM((CAPACITY, FULL), bf16),
                v_spares=pltpu.VMEM((SPARE, FULL), bf16),
                high=pltpu.VMEM((FULL, D), bf16),
                v_sent=pltpu.VMEM((CAPACITY, D), bf16),
                v_sent_spares=pltpu.VMEM((SPARE, D), bf16),
                **forward_scratch(FULL),
                **shared_scratch(FULL),
                **backward_scratch(FULL),
            ),
            f"full_{mb}",
            20 * 10**9,
        )
        ops = found["ops"]
        sums.append(found["sums_out"])
        ends.append((found["y1"], found["dx"]))
        returned.append(lax.ppermute(found["sent"], "section", [(1, 0)]))
    for mb in range(1 if ways == 16 else 2):
        inputs = dict(
            common, back=(returned[mb], HBM), **stashes[mb], ops_old=(ops, HBM), sums_old=(sums[mb], HBM)
        )
        outputs = dict(ops=ops_spec + ("ops_old",), sums_out=((48, D), f32, HBM, "sums_old"))
        scratch = dict(
            **buffers,
            x_low=pltpu.VMEM((CAPACITY, D), bf16),
            v_back=pltpu.VMEM((CAPACITY, D), bf16),
            v_part=pltpu.VMEM((CAPACITY, D), f32),
            lse_rows=pltpu.VMEM((16, CAPACITY), f32),
            **shared_scratch(CAPACITY),
            **backward_scratch(CAPACITY),
        )
        if mb == 0:
            outputs.update(grads=grads_spec + (None,))
            scratch.update(v_spares=pltpu.VMEM((SPARE, D), bf16), row=pltpu.VMEM((ROW_LEN, 1, D), f32))
        else:
            outputs.update(part=((CAPACITY, D), f32, HBM, None))
        found = launch(
            functools.partial(routed_backward_kernel, mb), inputs, outputs, scratch, f"routed_backward_{mb}", 7 * 10**9
        )
        ops, sums[mb] = found["ops"], found["sums_out"]
        if mb == 0:
            grads = found["grads"]
            ends = launch(
                full_outputs_kernel,
                dict(
                    layout=(layout, SMEM), chosen=(selected, VMEM), y1_a=(ends[0][0], HBM), y1_b=(ends[1][0], HBM),
                    dx_a=(ends[0][1], HBM), dx_b=(ends[1][1], HBM), acts_old=(acts, HBM), grads_old=(grads, HBM),
                ),
                dict(
                    acts=acts_spec + ("acts_old",), grads=grads_spec + ("grads_old",),
                    sent_spares=((SPARE, D), bf16, HBM, None),
                ),
                dict(
                    sems=pltpu.SemaphoreType.DMA((16,)),
                    v_spares=pltpu.VMEM((SPARE, D), bf16),
                    v_dx_a=pltpu.VMEM((FULL, D), f32),
                    v_dx_b=pltpu.VMEM((FULL, D), f32),
                    v_y1=pltpu.VMEM((2, FULL, D), bf16),
                    pair=pltpu.VMEM((ROW_LEN, 2, D), bf16),
                    row=pltpu.VMEM((ROW_LEN, 1, D), f32),
                    row_two=pltpu.VMEM((ROW_LEN, 1, D), f32),
                ),
                "full_outputs",
                4 * 10**9,
            )
            acts, grads = ends["acts"], ends["grads"]
            back_spares = lax.ppermute(ends["sent_spares"], "section", [(1, 0)])
    if ways == 16:
        shares, small, rows = summed_by_kernel(ops, sums, dict(common, back=(returned[1], HBM), **stashes[1]))
    else:
        rows = found["part"]
        shares, small = summed_by_collectives(ops, sums, ways)
    found = launch(
        closing_kernel,
        dict(
            small=(small, VMEM), rows=(rows, VMEM), back_spares=(back_spares, VMEM), grads_old=(grads, HBM),
            layout=(layout, SMEM), chosen=(selected, VMEM),
            **{"g_" + name: (share, VMEM) for name, share in shares.items()},
        ),
        dict(
            grads=grads_spec + ("grads_old",),
            o_gain=((2, D // ways), f32, VMEM, None),
            o_bias=((2, D // ways), f32, VMEM, None),
            o_router=((D,), f32, VMEM, None),
            o_counts=((2,), i32, SMEM, None),
            **{"o_" + name: (share.shape, f32, VMEM, None) for name, share in shares.items()},
        ),
        dict(sems=pltpu.SemaphoreType.DMA((4,)), row=pltpu.VMEM((ROW_LEN, 1, D), f32)),
        "closing",
        10**9,
        ways=ways,
    )
    return (
        jnp.transpose(acts.reshape(1, ROW_LEN, 2, D), (2, 0, 1, 3))[None],
        found["grads"].reshape(1, 2, 1, ROW_LEN, D),
        found["o_qkv"][None],
        found["o_out"][None],
        found["o_up"][None],
        found["o_down"][None],
        found["o_gain"][None],
        found["o_bias"][None],
        found["o_router"],
        found["o_counts"],
    )


def summed_by_kernel(ops, sums, routed):
    found = launch(
        gradient_kernel,
        dict(routed, ops=(ops, HBM), sums_a=(sums[0], VMEM), sums_b=(sums[1], VMEM)),
        dict(
            g_qkv=((STRIP, 3 * D), f32, VMEM, None),
            g_out=((STRIP, D), f32, VMEM, None),
            g_up=((STRIP, FF), f32, VMEM, None),
            g_down=((4 * STRIP, D), f32, VMEM, None),
            small_out=((8, D), f32, VMEM, None),
            part_rows=((CAPACITY, D), f32, HBM, None),
        ),
        dict(
            left=pltpu.VMEM((2, 2 * FULL, D), bf16),
            right=pltpu.VMEM((2, 2 * FULL, D), bf16),
            part=pltpu.VMEM((4, 2, 2, SHARD_ROWS, D), bf16),
            core_in=pltpu.VMEM((RING, 4, 2, STRIP, D), bf16),
            side_in=pltpu.VMEM((4, LATE * STRIP, D), bf16),
            up_in=pltpu.VMEM((3, LATE * STRIP, D), bf16),
            down_in=pltpu.VMEM((3, LATE * STRIP, D), bf16),
            early_up=pltpu.VMEM((HASTE, 3, 2, STRIP, D), bf16),
            early_down=pltpu.VMEM((HASTE, 3, 2, STRIP, D), bf16),
            early_side=pltpu.VMEM((HASTE, STRIP, D), bf16),
            final=pltpu.VMEM((STRIP, D), f32),
            small=pltpu.VMEM((5, 8, D), f32),
            small_in=pltpu.VMEM((4, 8, D), f32),
            cross_in=pltpu.VMEM((8, D), f32),
            cross_sem=pltpu.SemaphoreType.DMA((2,)),
            v_up=pltpu.VMEM((D, FF), bf16),
            v_down=pltpu.VMEM((FF, D), bf16),
            x_low=pltpu.VMEM((CAPACITY, D), bf16),
            v_part=pltpu.VMEM((CAPACITY, D), f32),
            lse_rows=pltpu.VMEM((16, CAPACITY), f32),
            **shared_scratch(CAPACITY),
            grad=pltpu.VMEM((CAPACITY, D), f32),
            da=pltpu.VMEM((CAPACITY, D), bf16),
            grad_mixed=pltpu.VMEM((CAPACITY, D), bf16),
            grad_qkv=pltpu.VMEM((CAPACITY, 3 * D), bf16),
            sums=pltpu.VMEM((48, D), f32),
            sems=pltpu.SemaphoreType.DMA((18,)),
            load_sem=pltpu.SemaphoreType.DMA((2, 2)),
            core_sem=pltpu.SemaphoreType.DMA((2, STRIPS)),
            side_sem=pltpu.SemaphoreType.DMA((2, LATE)),
            up_sem=pltpu.SemaphoreType.DMA((2, 4, LATE)),
            down_sem=pltpu.SemaphoreType.DMA((2, 4, LATE)),
            early_sem=pltpu.SemaphoreType.DMA((2, 2, 4, HASTE)),
            early_side_sem=pltpu.SemaphoreType.DMA((2, HASTE)),
            small_sem=pltpu.SemaphoreType.DMA((2, 4)),
            free_sem=pltpu.SemaphoreType.REGULAR((RING,)),
        ),
        "gradients",
        20 * 10**9,
        collective_id=0,
    )
    shares = {name: found["g_" + name] for name in ("qkv", "out", "up", "down")}
    return shares, found["small_out"], found["part_rows"]


def summed_by_collectives(ops, sums, count):
    first = lax.axis_index("section") == 0
    used = jnp.where(first, 2 * CAPACITY, 2 * FULL)
    ops = jnp.where(lax.broadcasted_iota(i32, (1, 2 * FULL, 1), 1) < used, ops, 0)

    def gradient(left, lefts, right, rights):
        a = jnp.concatenate([ops[left + k] for k in range(lefts)], axis=1)
        b = jnp.concatenate([ops[right + k] for k in range(rights)], axis=1)
        return lax.psum_scatter(t_mm(a, b), "dp", scatter_dimension=0, tiled=True)

    shares = dict(
        qkv=gradient(SLOT_N1, 1, SLOT_DQKV, 3),
        out=gradient(SLOT_MIXED, 1, SLOT_DA, 1),
        up=gradient(SLOT_N2, 1, SLOT_DU, 4),
        down=gradient(SLOT_ACT, 4, SLOT_GL, 1),
    )
    small = jnp.sum((sums[0] + sums[1]).reshape(6, 8, D), axis=1)
    small = jnp.concatenate([small, jnp.zeros((2, D), f32)])
    small = lax.psum(small, "dp")
    shared = lax.psum(jnp.where(first, small[4:6], 0.0), "section")
    return shares, jnp.concatenate([small[:4], shared, small[6:]])


def solution(mesh):
    return jax.shard_map(
        body,
        mesh=mesh,
        in_specs=(
            P(None, "dp", None, None),
            P(None, "dp", None),
            P(None, "dp", None),
            P(None, "dp", None, None),
            P("section", None, None),
            P("section", None, None),
            P("section", None, None),
            P("section", None, None),
            P("section", None, None),
            P("section", None, None),
            P(),
        ),
        out_specs=(
            P("section", None, "dp", None, None),
            P("section", None, "dp", None, None),
            P("section", "dp", None),
            P("section", "dp", None),
            P("section", "dp", None),
            P("section", "dp", None),
            P("section", None, "dp"),
            P("section", None, "dp"),
            P(),
            P(),
        ),
        check_vma=False,
    )
```

```python
import functools

import jax
import jax.numpy as jnp
from jax import lax
from jax.experimental import pallas as pl
from jax.experimental.pallas import tpu as pltpu
from jax.sharding import PartitionSpec as P

D = 768
HEADS = 12
FF = 3072
BIG_CROP = 197
SMALL_CROP = 37
ROW_LEN = 542
CAPACITY = 384
FULL = 544
PAIR = 2 * FULL
SPARE = 160
QUAD = 256
SCALE = 0.125
EPSILON = 1e-06
MASKED = -1e30
BLOCK = 32
CHUNK = 768
SLOT_STARTS = (0, 197, 394, 431, 468, 505)
SLOTS = 16
SLOT_N1, SLOT_MIXED, SLOT_N2, SLOT_ACT, SLOT_GL, SLOT_DA, SLOT_DQKV, SLOT_DU = 0, 1, 2, 3, 7, 8, 9, 12
SHARD_ROWS = 576
STRIP = 48
STRIPS = SHARD_ROWS // STRIP
BLOCKS = ((8, 9, 10, 11, 4, 5, 6, 7, 3, 0, 1, 2), (4, 5, 6, 7, 3, 0, 1, 2, 8, 9, 10, 11))
AMOUNTS = ((4, 0, 3, 0, 0, 2, 0, 1, 1, 1), (2, 1, 2, 2, 2, 2, 1, 0, 0, 0))
YFIRST = ((8, 10, 4, 5, 6, 3, 0, 1, 2), (5, 7, 3, 0, 1, 2, 8, 9, 10))
YCOUNT = ((0, 2, 0, 1, 2, 0, 1, 0, 1, 1, 0, 1), (0, 0, 1, 2, 2, 1, 0, 2, 1, 0, 0, 0))
EARLY = ((11, 9, 7), (6, 4, 11))
EARLY_BEGIN = ((1, 0, 7), (1, 0, 6))
PHASES = (0, 1, 3, 4, 5)
LATE, HASTE = len(YFIRST[0]), len(EARLY[0])
RING = 4
MESH_ID = pl.DeviceIdType.MESH
VMEM_LIMIT = 64 * 2**20 - 200 * 2**10

f32 = jnp.float32
bf16 = jnp.bfloat16
i32 = jnp.int32


def mm(left, right):
    return jnp.dot(left, right, preferred_element_type=f32)


def mm_t(left, right):
    return lax.dot_general(left, right, (((1,), (1,)), ((), ())), preferred_element_type=f32)


def t_mm(left, right):
    return lax.dot_general(left, right, (((0,), (0,)), ((), ())), preferred_element_type=f32)


def rows_loop(count, body, rolled=False):
    if not rolled:
        for start in range(0, count, BLOCK):
            body(pl.ds(start, BLOCK))
        return

    def some(i, _):
        for k in range(4):
            body(pl.ds(pl.multiple_of((4 * i + k) * BLOCK, BLOCK), BLOCK))
        return 0

    lax.fori_loop(0, count // (4 * BLOCK), some, 0)


def col_chunk(j):
    return pl.ds(pl.multiple_of(j * CHUNK, CHUNK), CHUNK)


def repeat(count, body, rolled):
    if rolled:
        lax.fori_loop(0, count, lambda i, _: (body(i), 0)[1], 0)
    else:
        for i in range(count):
            body(i)


def multiply_into(target, product, left, right, rolled, by_rows):
    if not rolled:
        target[...] = product(left[...], right[...])
        return

    def one(j):
        cols = pl.ds(pl.multiple_of(j * 256, 256), 256)
        target[:, cols] = product(left[...], right[cols, :] if by_rows else right[:, cols])

    repeat(3, one, True)


def normalised(rows):
    centred = rows - jnp.mean(rows, axis=-1, keepdims=True)
    inverse = lax.rsqrt(jnp.mean(centred * centred, axis=-1, keepdims=True) + EPSILON)
    return centred * inverse, inverse


def crop_table(layout, mb):
    start, bigs, smalls = jnp.int32(0), jnp.int32(0), jnp.int32(0)
    starts, moves, slots = [], [], []
    for crop in range(6):
        is_big = layout[mb, 0, crop]
        slot = jnp.where(is_big == 1, BIG_CROP * bigs, 2 * BIG_CROP + SMALL_CROP * smalls)
        starts.append(start)
        moves.append(slot - start)
        slots.append(slot)
        start = start + jnp.where(is_big == 1, BIG_CROP, SMALL_CROP)
        bigs = bigs + is_big
        smalls = smalls + 1 - is_big
    back = []
    for slot_start in SLOT_STARTS:
        value = jnp.int32(0)
        for crop in range(6):
            value = value - jnp.where(slots[crop] == slot_start, moves[crop], 0)
        back.append(value)
    return starts, moves, back


def to_slot(places, table):
    starts, moves, _ = table
    move = jnp.full(places.shape, moves[0], i32)
    for crop in range(1, 6):
        move = jnp.where(places >= starts[crop], moves[crop], move)
    return jnp.where(places < ROW_LEN, places + move, places)


def from_slot(places, table):
    move = jnp.full(places.shape, table[2][0], i32)
    for crop in range(1, 6):
        move = jnp.where(places >= SLOT_STARTS[crop], table[2][crop], move)
    return jnp.where(places < ROW_LEN, places + move, places)


def one_hot(mask):
    return jnp.where(mask, 1.0, 0.0).astype(bf16)


def lane_places(count):
    return lax.broadcasted_iota(i32, (1, count), 1)


def row_places(count):
    return lax.broadcasted_iota(i32, (count, 1), 0)


class Chosen:
    def __init__(self, chosen, layout, mb):
        self.table = crop_table(layout, mb)
        row = chosen[mb].astype(f32)
        self.column = jnp.transpose(jnp.broadcast_to(row, (8, CAPACITY)))[:, :1].astype(i32)
        self.slots = to_slot(self.column, self.table)

    def bounds(self):
        return [jnp.sum(jnp.where(self.slots < start, 1, 0)) for start in SLOT_STARTS[1:]]

    def taken(self, places):
        return jnp.max(jnp.where(self.column == places, 1, 0), axis=0, keepdims=True)

    def rank(self, slots):
        return jnp.sum(jnp.where(self.slots < slots, 1, 0), axis=0, keepdims=True)

    def picks(self, places, valid):
        rank = self.rank(to_slot(places, self.table))
        return one_hot((rank == row_places(CAPACITY)) & (self.taken(places) == 1) & valid)

    def spares(self, places):
        slots = to_slot(places, self.table)
        rank = slots - self.rank(slots)
        return one_hot((rank == row_places(SPARE)) & (self.taken(places) == 0) & (places < ROW_LEN))


def both_rows(mb):
    lanes = lane_places(PAIR)
    places = lanes // 2
    return places, (lanes - 2 * places == mb) & (places < ROW_LEN)


def crop_numbers(places, bounds):
    number = jnp.zeros(places.shape, i32)
    for bound in bounds:
        number = number + jnp.where(places >= bound, 1, 0)
    return number


def owned(numbers, kind):
    if kind == 0:
        return numbers == 0
    if kind == 1:
        return numbers == 1
    return numbers >= 2


def head_lanes(head, value):
    lanes = lane_places(QUAD)
    return jnp.where((lanes >= 64 * head) & (lanes < 64 * head + 64), value, 0.0).astype(bf16)


def quad(part, group):
    return pl.ds(pl.multiple_of(part * D + group * QUAD, QUAD), QUAD)


class Window:
    def __init__(self, kind, start, size, bounds):
        self.kind, self.rows, self.lanes = kind, pl.ds(start, size), slice(0, size)
        numbers = crop_numbers(start + row_places(size), bounds)
        self.start, self.size = start, size
        self.own = owned(numbers, kind)
        self.same = (numbers == crop_numbers(start + lane_places(size), bounds)) & self.own


    def log_row(self, lse, row):
        if len(lse.shape) == 3:
            return lse[self.kind, row : row + 1, self.lanes]
        return lse[pl.ds(row, 1), self.start : self.start + self.size]


def lse_by_row(lse, middle, bounds):
    def moved(kind, start):
        wide = jnp.concatenate([lse[kind], jnp.zeros((16, CAPACITY - 256), f32)], axis=1)
        return pltpu.roll(wide, start, axis=1)

    numbers = crop_numbers(lane_places(CAPACITY), bounds)
    later = jnp.where(numbers == 1, moved(1, middle), moved(2, 224))
    return jnp.where(numbers == 0, moved(0, 0), later)


def staggered(windows, bounds, first, second, third, rolled=False):
    heads = []
    for kind, start, size in windows:
        window = Window(kind, start, size, bounds)
        if rolled:

            def one(group, _):
                run_heads([(window, group, head) for head in range(4)], first, second, third)
                return 0

            lax.fori_loop(0, 3, one, 0)
        else:
            heads += [(window, group, head) for group in range(3) for head in range(4)]
    if heads:
        run_heads(heads, first, second, third)


def run_heads(heads, first, second, third):
    for t in range(len(heads) + 3):
        if t < len(heads):
            first(*heads[t])
        if 0 <= t - 2 < len(heads):
            second(*heads[t - 2])
        if 0 <= t - 3 < len(heads):
            third(*heads[t - 3])


def attention_forward(windows, bounds, qkv, mixed, lse, rolled=False):
    held = {}

    def first(window, group, head):
        rows = window.rows
        if head == 0:
            q4 = qkv[rows, quad(0, group)] * jnp.full((1, QUAD), SCALE, bf16)
            held[0] = q4, qkv[rows, quad(1, group)], jnp.transpose(qkv[rows, quad(2, group)])
        q4, k4, values = held[0]
        held[1, head] = mm_t(k4 * head_lanes(head, 1.0), q4), values

    def second(window, group, head):
        scores, values = held.pop((1, head))
        scores = jnp.where(window.same, scores, MASKED)
        top = jnp.max(scores, axis=0, keepdims=True)
        powers = jnp.exp(scores - top)
        power_sum = jnp.sum(powers, axis=0, keepdims=True)
        held[2, head] = (powers * (1.0 / power_sum)).astype(bf16), values
        row = 4 * group + head
        lse[window.kind, pl.ds(row, 1), window.lanes] = top + jnp.log(power_sum)

    def third(window, group, head):
        probs, values = held.pop((2, head))
        held[3, head] = mm(values[64 * head : 64 * head + 64, :], probs)
        if head == 3:
            total = jnp.transpose(jnp.concatenate([held.pop((3, k)) for k in range(4)], axis=0))
            old = mixed[window.rows, quad(0, group)].astype(f32)
            mixed[window.rows, quad(0, group)] = jnp.where(window.own, total, old).astype(bf16)

    staggered(windows, bounds, first, second, third, rolled)


def attention_backward(windows, bounds, qkv, grad_mixed, lse, grad_qkv, rolled=False):
    held = {}

    def first(window, group, head):
        rows = window.rows
        if head == 0:
            q4 = qkv[rows, quad(0, group)] * jnp.full((1, QUAD), SCALE, bf16)
            k4 = qkv[rows, quad(1, group)]
            held[0] = q4, k4, qkv[rows, quad(2, group)], grad_mixed[rows, quad(0, group)], jnp.transpose(k4)
        q4, k4, v4, g4, _ = held[0]
        lanes = head_lanes(head, 1.0)
        held[1, head] = mm_t(k4 * lanes, q4), mm_t(v4 * lanes, g4), held[0]

    def second(window, group, head):
        scores, grad_probs, whole = held.pop((1, head))
        row = 4 * group + head
        log_row = window.log_row(lse, row)
        probs = jnp.where(window.same, jnp.exp(scores - log_row), 0.0)
        spread = jnp.sum(probs * grad_probs, axis=0, keepdims=True)
        held[2, head] = probs.astype(bf16), (probs * (grad_probs - spread)).astype(bf16), whole

    def third(window, group, head):
        probs, grad_scores, (q4, _, _, g4, keys) = held.pop((2, head))
        lanes = head_lanes(head, 1.0)
        dv, dk = mm(probs, g4 * lanes), mm(grad_scores, q4 * lanes)
        dq = mm(keys[64 * head : 64 * head + 64, :], grad_scores)
        if head:
            dv, dk, dq = dv + held[3][0], dk + held[3][1], held[3][2] + [dq]
        else:
            dq = [dq]
        held[3] = dv, dk, dq
        if head == 3:
            dq = jnp.transpose(jnp.concatenate(dq, axis=0)) * SCALE
            for part, grad in enumerate((dq, dk, dv)):
                old = grad_qkv[window.rows, quad(part, group)].astype(f32)
                grad_qkv[window.rows, quad(part, group)] = jnp.where(window.own, grad, old).astype(bf16)

    staggered(windows, bounds, first, second, third, rolled)


def gelu_and_slope(u):
    power = jnp.exp(u * u * -0.5)
    cdf = 0.5 + 0.5 * lax.erf(u * 0.7071067811865476)
    return u * cdf, cdf + u * power * 0.3989422804014327


def norm_rows(count, x, gain_row, bias_row, out, rolled):
    def one(rows):
        z, _ = normalised(x[rows, :])
        out[rows, :] = (z * gain_row + bias_row).astype(bf16)

    rows_loop(count, one, rolled)


def project(s, w_qkv, rolled):
    def one(j):
        cols = col_chunk(j)
        s.qkv[:, cols] = mm(s.n1[...], w_qkv[:, cols]).astype(bf16)

    repeat(3, one, rolled)


def add_norm(count, x, gain_row, bias_row, s, rolled):
    def one(rows):
        hidden = x[rows, :] + s.att[rows, :]
        s.hidden[rows, :] = hidden
        z, _ = normalised(hidden)
        s.n2[rows, :] = (z * gain_row + bias_row).astype(bf16)

    rows_loop(count, one, rolled)


def feed_forward(count, s, w_up, w_down, rolled):
    def one(j):
        cols = col_chunk(j)
        upper = mm(s.n2[...], w_up[:, cols])
        for start in range(0, count, BLOCK):
            active, slope = gelu_and_slope(upper[start : start + BLOCK, :])
            s.act[start : start + BLOCK, cols] = active.astype(bf16)
            s.slope[start : start + BLOCK, cols] = slope.astype(bf16)

    repeat(FF // CHUNK, one, rolled)
    multiply_into(s.low, mm, s.act, w_down, rolled, False)


def branch_forward(count, windows, bounds, x, gain, bias, w, s, wait, send, rolled=False):
    w_qkv, w_out, w_up, w_down = w
    norm_rows(count, x, gain[0:1, :], bias[0:1, :], s.n1, rolled)
    send("n1")
    wait(0)
    project(s, w_qkv, rolled)
    send("qkv")
    attention_forward(windows, bounds, s.qkv, s.mixed, s.lse, rolled)
    send("mixed")
    wait(1)
    s.att[...] = mm(s.mixed[...], w_out[...])
    add_norm(count, x, gain[1:2, :], bias[1:2, :], s, rolled)
    send("n2")
    wait(2)
    wait(3)
    feed_forward(count, s, w_up, w_down, rolled)
    send("act")


def norm_backward(dn, z, inverse, gain_row):
    dz = dn * gain_row
    return inverse * (
        dz - jnp.mean(dz, axis=-1, keepdims=True) - z * jnp.mean(dz * z, axis=-1, keepdims=True)
    )


def fold(rows):
    total = rows[0:8, :]
    for k in range(8, BLOCK, 8):
        total = total + rows[k : k + 8, :]
    return total


def lower(count, s):
    def one(rows):
        s.gl[rows, :] = s.grad[rows, :].astype(bf16)

    rows_loop(count, one)


def feed_backward(count, s, w_up, w_down, wait, rolled=False):
    if rolled:
        for j in range(5):
            wait(j)

    def one(j):
        cols = col_chunk(j)
        if not rolled:
            wait(j)
        grad = mm_t(s.gl[...], w_down[cols, :])
        for start in range(0, count, BLOCK):
            slope = s.slope[start : start + BLOCK, cols].astype(f32)
            s.du[start : start + BLOCK, cols] = (grad[start : start + BLOCK, :] * slope).astype(bf16)

    repeat(FF // CHUNK, one, rolled)
    if not rolled:
        wait(4)
    multiply_into(s.low, mm_t, s.du, w_up, rolled, True)


def norm_two_backward(count, gain_row, s, rolled=False):
    s.sums[0:32, :] = jnp.zeros((32, D), f32)

    def one(rows):
        z, inverse = normalised(s.hidden[rows, :])
        dn = s.low[rows, :]
        dh = norm_backward(dn, z, inverse, gain_row)
        s.sums[8:16, :] += fold(dn * z)
        s.sums[24:32, :] += fold(dn)
        s.att[rows, :] = dh
        s.da[rows, :] = (s.grad[rows, :] + dh).astype(bf16)

    rows_loop(count, one, rolled)


def norm_one_backward(count, x, gain_row, s, rolled=False):
    def one(rows):
        z, inverse = normalised(x[rows, :].astype(f32))
        dn = s.low[rows, :]
        s.sums[0:8, :] += fold(dn * z)
        s.sums[16:24, :] += fold(dn)
        s.grad[rows, :] = s.att[rows, :] + norm_backward(dn, z, inverse, gain_row)

    rows_loop(count, one, rolled)


def branch_backward(count, windows, bounds, x, gain, w, s, wait, send, rolled=False):
    w_qkv, w_out, w_up, w_down = w
    if count != FULL:
        lower(count, s)
    send("gl")
    feed_backward(count, s, w_up, w_down, wait, rolled)
    send("du")
    wait(5)
    norm_two_backward(count, gain[1:2, :], s)
    send("da")
    s.grad_mixed[...] = mm_t(s.da[...], w_out[...]).astype(bf16)
    attention_backward(windows, bounds, s.qkv, s.grad_mixed, s.lse_rows, s.grad_qkv, rolled)
    send("dqkv")
    wait(6)
    multiply_into(s.low, mm_t, s.grad_qkv, w_qkv, rolled, True)
    norm_one_backward(count, x, gain[0:1, :], s)


class Refs:
    def __init__(self, names, refs, constants):
        self.__dict__.update(zip(names, refs), **constants)


class Copies:
    def __init__(self, sems, first):
        self.sems, self.next, self.open = sems, first, []

    def start(self, source, target):
        copy = pltpu.make_async_copy(source, target, self.sems.at[self.next])
        self.next += 1
        copy.start()
        return copy

    def out(self, source, target):
        self.open.append(self.start(source, target))

    def finish(self):
        for copy in self.open:
            copy.wait()


def slot_rows(ops, slot, mb, count):
    return ops.at[slot, pl.ds(mb * count, count), :]


def send_slots(copies, ops, s, mb, count):
    wide = {"act": (SLOT_ACT, 4), "du": (SLOT_DU, 4), "dqkv": (SLOT_DQKV, 3)}
    flat = {"n1": SLOT_N1, "mixed": SLOT_MIXED, "n2": SLOT_N2, "gl": SLOT_GL, "da": SLOT_DA}

    def send(what):
        if what in flat:
            copies.out(getattr(s, what), slot_rows(ops, flat[what], mb, count))
        elif what in wide:
            source = {"act": "act", "du": "du", "dqkv": "grad_qkv"}[what]
            slot, parts = wide[what]
            for k in range(parts):
                copies.out(getattr(s, source).at[:, pl.ds(k * D, D)], slot_rows(ops, slot + k, mb, count))

    return send


def weight_scratch():
    return dict(
        v_qkv=pltpu.VMEM((D, 3 * D), bf16),
        v_out=pltpu.VMEM((D, D), bf16),
        v_up=pltpu.VMEM((D, FF), bf16),
        v_down=pltpu.VMEM((FF, D), bf16),
    )


def forward_scratch(count):
    return dict(
        n1=pltpu.VMEM((count, D), bf16),
        mixed=pltpu.VMEM((count, D), bf16),
        n2=pltpu.VMEM((count, D), bf16),
        act=pltpu.VMEM((count, FF), bf16),
    )


def shared_scratch(count):
    return dict(
        qkv=pltpu.VMEM((count, 3 * D), bf16),
        lse=pltpu.VMEM((3, 16, 256), f32),
        att=pltpu.VMEM((count, D), f32),
        hidden=pltpu.VMEM((count, D), f32),
        slope=pltpu.VMEM((count, FF), bf16),
        low=pltpu.VMEM((count, D), f32),
    )


def backward_scratch(count):
    return dict(
        grad=pltpu.VMEM((count, D), f32),
        gl=pltpu.VMEM((count, D), bf16),
        du=pltpu.VMEM((count, FF), bf16),
        da=pltpu.VMEM((count, D), bf16),
        grad_mixed=pltpu.VMEM((count, D), bf16),
        grad_qkv=pltpu.VMEM((count, 3 * D), bf16),
        sums=pltpu.VMEM((48, D), f32),
    )


def routed_bounds(column_slots):
    bounds = []
    for slot_start in SLOT_STARTS[1:]:
        bounds.append(jnp.sum(jnp.where(column_slots < slot_start, 1, 0)))
    return bounds


def routed_windows(bounds):
    middle = pl.multiple_of(jnp.minimum(bounds[0] // 16 * 16, 160), 16)
    return ((0, 0, 208), (1, middle, 224), (2, 224, 160))


FULL_BOUNDS = SLOT_STARTS[1:] + (ROW_LEN,)
FULL_WINDOWS = ((0, 0, 208), (1, 192, 208), (2, 384, 160))
FIXED_WINDOWS = ((0, 0, 208), (1, 32, 352), (2, 224, 160))


def flatten(target, source):
    target[PAIR - 16 :, :] = jnp.zeros((16, D), target.dtype)
    target[0 : 2 * ROW_LEN, :] = source[...].reshape(2 * ROW_LEN, D)


def running(amounts):
    return tuple(sum(amounts[:place]) for place in range(len(amounts)))


def planned(section):
    steps = len(YCOUNT[section])
    done = {}
    for k in range(STRIPS):
        place = BLOCKS[section].index(k)
        done[k] = next(t for t, before in enumerate(running(AMOUNTS[section] + (0,))[1:]) if before > place) - 1
    for k in range(8, 12):
        done[k] = max(done[k] for k in range(8, 12))
    sequence, taken, place = [], [], 0
    for t in range(-1, steps - 1):
        group = YFIRST[section][place : place + YCOUNT[section][t + 1]]
        place += len(group)
        hasty = [k for k, begin in zip(EARLY[section], EARLY_BEGIN[section]) if begin == t]
        for k in (*group, *hasty):
            sequence.append(k)
            taken.append(t)
    leave, last = [], -1
    for n, k in enumerate(sequence):
        last = max(last, done[k], taken[n] - 2)
        leave.append(last)
        assert last < taken[n] and (n < RING or taken[n - RING] <= last)
    sums, last = [-1] * (steps + 3), 1
    for a, k in enumerate(YFIRST[section]):
        last = max(last + 1, taken[sequence.index(k)] + 1)
        sums[last] = a
    return tuple(sequence), tuple(leave.count(t) for t in range(-1, steps - 1)), tuple(sums)


def parts_of(value):
    high = value.astype(bf16)
    return high, (value - high.astype(f32)).astype(bf16)


def launch(kernel, inputs, outputs, scratch, name, flops, collective_id=None, **constants):
    names = tuple(inputs) + tuple(outputs) + tuple(scratch)
    places = list(inputs)
    aliases = {}
    for k, (_, _, _, same) in enumerate(outputs.values()):
        if same is not None:
            aliases[places.index(same)] = k
    params = dict(vmem_limit_bytes=VMEM_LIMIT, has_side_effects=True)
    if collective_id is not None:
        params["collective_id"] = collective_id
    found = pl.pallas_call(
        lambda *refs: kernel(Refs(names, refs, constants)),
        out_shape=[jax.ShapeDtypeStruct(shape, kind) for shape, kind, _, _ in outputs.values()],
        in_specs=[pl.BlockSpec(memory_space=space) for _, space in inputs.values()],
        out_specs=[pl.BlockSpec(memory_space=space) for _, _, space, _ in outputs.values()],
        scratch_shapes=list(scratch.values()),
        input_output_aliases=aliases,
        compiler_params=pltpu.CompilerParams(**params),
        cost_estimate=pl.CostEstimate(flops=flops, bytes_accessed=30 * 2**20, transcendentals=0),
        name=name,
    )(*(array for array, _ in inputs.values()))
    return dict(zip(outputs, found))


def routed_forward_kernel(mb, r):
    w = (r.v_qkv, r.v_out, r.v_up, r.v_down)
    section = lax.axis_index("section")
    places, mine = both_rows(mb)

    @pl.when(section == 0)
    def _():
        copies = Copies(r.sems, 0)
        tok_in = copies.start(r.tokens, r.pair)
        loads = [copies.start(a, b) for a, b in zip((r.w_qkv, r.w_out, r.w_up, r.w_down), w)]
        chosen = Chosen(r.chosen, r.layout, mb)
        r.v_picks[...] = chosen.picks(places, mine)
        bounds = chosen.bounds()
        for k in range(5):
            r.bounds[0, k] = bounds[k]
        tok_in.wait()
        flatten(r.flat, r.pair)
        r.x[...] = mm(r.v_picks[...], r.flat[...])
        r.x_low[...] = r.x[...].astype(bf16)
        copies.out(r.x_low, r.st_x)
        slots = send_slots(copies, r.ops, r, mb, CAPACITY)

        def send(what):
            slots(what)
            if what == "qkv":
                copies.out(r.qkv, r.st_qkv)
            elif what == "mixed":
                r.lse_rows[...] = lse_by_row(r.lse, windows[1][1], bounds)
                copies.out(r.lse_rows, r.st_lse)
            elif what == "n2":
                copies.out(r.hidden, r.st_hidden)
            elif what == "act":
                copies.out(r.slope, r.st_slope)

        windows = routed_windows(bounds)
        branch_forward(
            CAPACITY, windows, bounds, r.x, r.gain, r.bias, w, r, lambda i: loads[i].wait(), send, mb == 1
        )
        router = r.router[...].reshape(1, D)

        def add(rows):
            branch = r.att[rows, :] + r.low[rows, :]
            r.low[rows, :] = branch
            here = r.x[rows, :]
            gates = jax.nn.sigmoid(jnp.sum(here * router, axis=-1, keepdims=True))
            r.y_low[rows, :] = (here + gates * branch).astype(bf16)

        rows_loop(CAPACITY, add)
        copies.out(r.y_low, r.y0p)
        copies.out(r.low, r.st_branch)
        copies.out(r.v_picks, r.picks_out)
        copies.finish()

    if mb == 0:
        @pl.when(section == 1)
        def _():
            copies = Copies(r.sems, 0)
            copies.start(r.tokens, r.pair).wait()
            flatten(r.flat, r.pair)
            copies.start(r.cotangent, r.pair).wait()
            flatten(r.flat_two, r.pair)
            for row in range(2):
                chosen = Chosen(r.chosen, r.layout, row)
                places, mine = both_rows(row)
                here = (to_slot(places, chosen.table) == row_places(FULL)) & mine
                fresh = here & (chosen.taken(places) == 0)
                r.v_x[row] = mm(one_hot(fresh), r.flat[...]).astype(bf16)
                r.v_cot[row] = mm(one_hot(here), r.flat_two[...]).astype(bf16)
                back = from_slot(lane_places(FULL), chosen.table)
                picks = chosen.picks(back, lane_places(FULL) < ROW_LEN)
                r.v_slot_picks[row] = picks
                r.v_spread[row] = jnp.transpose(picks)
                r.v_spares[row] = chosen.spares(back)
            for source, target in (
                (r.v_x, r.x_rest),
                (r.v_cot, r.cot),
                (r.v_slot_picks, r.slot_picks),
                (r.v_spread, r.spread),
                (r.v_spares, r.spares),
            ):
                copies.out(source, target)
            copies.finish()


def routed_outputs_kernel(r):
    @pl.when(lax.axis_index("section") == 0)
    def _():
        copies = Copies(r.sems, 0)
        loads = [
            copies.start(a, b)
            for a, b in (
                (r.tokens, r.pair), (r.picks_a, r.v_picks.at[0]), (r.picks_b, r.v_picks.at[1]),
                (r.y_a, r.v_y.at[0]), (r.y_b, r.v_y.at[1]),
            )
        ]
        for copy in loads:
            copy.wait()
        flatten(r.flat, r.pair)
        ones = jnp.ones((CAPACITY, 128), bf16)
        spread = t_mm(r.v_picks[0], r.v_y[0]) + t_mm(r.v_picks[1], r.v_y[1])
        is_in = (t_mm(r.v_picks[0], ones) + t_mm(r.v_picks[1], ones))[:, :1]
        result = jnp.where(is_in > 0.5, spread, r.flat[...].astype(f32)).astype(bf16)
        r.pair[...] = result[: 2 * ROW_LEN, :].reshape(ROW_LEN, 2, D)
        copies.out(r.pair, r.acts)
        copies.finish()


def full_kernel(mb, r):
    w = (r.v_qkv, r.v_out, r.v_up, r.v_down)

    @pl.when(lax.axis_index("section") == 1)
    def _():
        copies = Copies(r.sems, 0)
        first = [
            copies.start(a, b)
            for a, b in ((r.x_rest.at[mb], r.tok), (r.y0p, r.low_in), (r.spread.at[mb], r.v_spread))
        ]
        loads = [copies.start(a, b) for a, b in zip((r.w_qkv, r.w_out, r.w_up, r.w_down), w)]
        cot_in = copies.start(r.cot.at[mb], r.gl)
        picks_in = [copies.start(r.slot_picks.at[mb], r.v_picks), copies.start(r.spares.at[mb], r.v_spares)]
        for copy in first:
            copy.wait()
        r.x[...] = r.tok[...].astype(f32) + mm(r.v_spread[...], r.low_in[...])
        send = send_slots(copies, r.ops, r, mb, FULL)
        branch_forward(
            FULL, FULL_WINDOWS, FULL_BOUNDS, r.x, r.gain, r.bias, w, r, lambda i: loads[i].wait(), send
        )
        cot_in.wait()

        def add(rows):
            r.tok[rows, :] = (r.x[rows, :] + r.att[rows, :] + r.low[rows, :]).astype(bf16)
            r.grad[rows, :] = r.gl[rows, :].astype(f32)

        rows_loop(FULL, add)
        copies.out(r.tok, r.y1)
        r.lse_rows = r.lse
        branch_backward(FULL, FULL_WINDOWS, FULL_BOUNDS, r.x, r.gain, w, r, lambda i: None, send)
        r.sums[32:48, :] = jnp.zeros((16, D), f32)
        copies.out(r.sums, r.sums_out)

        def join(rows):
            total = r.gl[rows, :].astype(f32) + r.grad[rows, :]
            r.low[rows, :] = total
            r.high[rows, :] = total.astype(bf16)

        rows_loop(FULL, join)
        copies.out(r.low, r.dx)
        for copy in picks_in:
            copy.wait()
        r.v_sent[...] = mm(r.v_picks[...], r.high[...]).astype(bf16)
        copies.out(r.v_sent, r.sent.at[0:CAPACITY, :])
        if mb == 0:
            r.v_sent_spares[...] = mm(r.v_spares[...], r.high[...]).astype(bf16)
            copies.out(r.v_sent_spares, r.sent.at[CAPACITY:, :])
        copies.finish()


def placed_gradients(chosen, part, spare, out):
    places = lane_places(FULL)
    picks = chosen.picks(places, places < ROW_LEN)
    high, rest = parts_of(part[...])
    total = t_mm(picks, high) + t_mm(chosen.spares(places), spare[...]) + t_mm(picks, rest)
    out[...] = total[0:ROW_LEN, :].reshape(ROW_LEN, 1, D)


def gates_backward(r, bounds, rolled=False):
    router = r.router[...].reshape(1, D)
    r.sums[32:48, :] = jnp.zeros((16, D), f32)

    def gate(rows):
        here = r.x_low[rows, :].astype(f32)
        gates = jax.nn.sigmoid(jnp.sum(here * router, axis=-1, keepdims=True))
        dy = r.v_back[rows, :].astype(f32)
        slopes = jnp.sum(r.v_part[rows, :] * dy, axis=-1, keepdims=True) * gates * (1.0 - gates)
        r.grad[rows, :] = gates * dy
        r.sums[32:40, :] += fold(slopes * here)
        r.v_part[rows, :] = dy + slopes * router

    rows_loop(CAPACITY, gate, rolled)
    r.sums[40:41, :] = jnp.where(lane_places(D) == 0, bounds[1], 0).astype(f32)


def routed_backward_kernel(mb, r):
    w = (r.v_qkv, r.v_out, r.v_up, r.v_down)
    section = lax.axis_index("section")

    @pl.when(section == 0)
    def _():
        copies = Copies(r.sems, 0)

        def load(*pairs):
            return [copies.start(a, b) for a, b in pairs]

        first = load((r.back.at[0:CAPACITY, :], r.v_back), (r.st_x, r.x_low), (r.st_branch, r.v_part))
        chunks = []
        for j in range(4):
            cols = pl.ds(j * CHUNK, CHUNK)
            chunks.append(
                load((r.w_down.at[cols, :], r.v_down.at[cols, :]), (r.st_slope.at[:, cols], r.slope.at[:, cols]))
            )
        chunks.append(load((r.w_up, r.v_up)))
        chunks.append(
            load((r.st_hidden, r.hidden), (r.w_out, r.v_out), (r.st_qkv, r.qkv), (r.st_lse, r.lse_rows))
        )
        chunks.append(load((r.w_qkv, r.v_qkv)))
        if mb == 0:
            spare_in = copies.start(r.back.at[CAPACITY:, :], r.v_spares)
        bounds = [r.bounds[0, k] for k in range(5)]
        for copy in first:
            copy.wait()
        gates_backward(r, bounds)

        def wait(i):
            for copy in chunks[i]:
                copy.wait()

        send = send_slots(copies, r.ops, r, mb, CAPACITY)
        branch_backward(CAPACITY, FIXED_WINDOWS, bounds, r.x_low, r.gain, w, r, wait, send, True)
        copies.out(r.sums, r.sums_out)

        def join(rows):
            r.v_part[rows, :] += r.grad[rows, :]

        rows_loop(CAPACITY, join)
        if mb == 0:
            spare_in.wait()
            placed_gradients(Chosen(r.chosen, r.layout, 0), r.v_part, r.v_spares, r.row)
            copies.out(r.row, r.grads.at[0])
        else:
            copies.out(r.v_part, r.part)
        copies.finish()


def full_outputs_kernel(r):
    @pl.when(lax.axis_index("section") == 1)
    def _():
        copies = Copies(r.sems, 0)
        halves = (r.v_dx_a, r.v_dx_b)
        dx_in = [copies.start(r.dx_a, halves[0]), copies.start(r.dx_b, halves[1])]
        y_in = [copies.start(r.y1_a, r.v_y1.at[0]), copies.start(r.y1_b, r.v_y1.at[1])]
        dx_in[1].wait()
        chosen = Chosen(r.chosen, r.layout, 1)
        back = from_slot(lane_places(FULL), chosen.table)
        r.v_spares[...] = mm(chosen.spares(back), r.v_dx_b[...].astype(bf16)).astype(bf16)
        copies.out(r.v_spares, r.sent_spares)
        for copy in y_in:
            copy.wait()
        rows = row_places(PAIR)
        total = jnp.zeros((PAIR, D), f32)
        for row in range(2):
            table = crop_table(r.layout, row)
            slots = lane_places(FULL)
            target = jnp.where(slots < ROW_LEN, 2 * from_slot(slots, table) + row, -1)
            total = total + mm(one_hot(rows == target), r.v_y1[row])
        r.pair[...] = total[: 2 * ROW_LEN, :].reshape(ROW_LEN, 2, D).astype(bf16)
        copies.out(r.pair, r.acts)
        dx_in[0].wait()
        for row in range(2):
            table = crop_table(r.layout, row)
            slots = lane_places(FULL)
            move = one_hot((from_slot(slots, table) == row_places(FULL)) & (slots < ROW_LEN))
            high, rest = parts_of(halves[row][...])
            total = mm(move, high) + mm(move, rest)
            target = (r.row, r.row_two)[row]
            target[...] = total[0:ROW_LEN, :].reshape(ROW_LEN, 1, D)
            copies.out(target, r.grads.at[row])
        copies.finish()


def closing_kernel(r):
    def row_copy():
        return pltpu.make_async_copy(r.row, r.grads.at[1], r.sems.at[0])

    @pl.when(lax.axis_index("section") == 0)
    def _():
        placed_gradients(Chosen(r.chosen, r.layout, 1), r.rows, r.back_spares, r.row)
        row_copy().start()

    for name in ("qkv", "out", "up", "down"):
        getattr(r, "o_" + name)[...] = getattr(r, "g_" + name)[...]
    width = D // r.ways
    me = lax.axis_index("dp")
    turned = pltpu.roll(r.small[...], lax.rem(D - width * me, D), axis=1)
    r.o_gain[...] = turned[0:2, 0:width]
    r.o_bias[...] = turned[2:4, 0:width]
    r.o_router[...] = r.small[4, :]
    big = jnp.sum(r.small[5:6, :]).astype(i32)
    r.o_counts[0] = big
    r.o_counts[1] = 2 * CAPACITY * r.ways - big
    pl.when(lax.axis_index("section") == 0)(lambda: row_copy().wait())


def gradient_kernel(r):
    me = lax.axis_index("dp")
    zero = me - me
    section = lax.axis_index("section")
    routed, full = section == 0, section == 1
    c = lax.rem(me, 2)
    y = lax.rem(me // 2, 2)
    z = me // 4
    sibling = {"dp": me + 1 - 2 * c}
    beside = {"dp": me + 2 - 4 * y}
    above, below = {"dp": me + 4}, {"dp": me - 4}
    far = {"dp": me + 8 - 16 * (z // 2)}
    paired = {"dp": me + 4 - 8 * lax.rem(z, 2)}

    barrier = pltpu.get_barrier_semaphore()

    def greet(device):
        pl.semaphore_signal(barrier, inc=1, device_id=device, device_id_type=MESH_ID)

    for device in (sibling, beside, far):
        greet(device)
    pl.when(z > 0)(lambda: greet(below))
    pl.when(z < 3)(lambda: greet(above))
    pl.when(full)(lambda: greet({"section": 0}))

    def strip(k):
        return pl.ds(pl.multiple_of(k * STRIP, STRIP), STRIP)

    def remote(source, target, sems, index, device):
        return pltpu.make_async_remote_copy(
            source, target, sems.at[(0,) + index], sems.at[(1,) + index], device_id=device, device_id_type=MESH_ID
        )

    def listed(orders, n):
        found = []
        for order in orders:
            value = zero + order[0]
            for place, entry in enumerate(order[1:], 1):
                value = jnp.where(n == place, entry, value)
            found.append(value)
        return jnp.where(routed, found[0], found[1])

    def placed(orders, k):
        found = []
        for order in orders:
            value = zero
            for place, entry in enumerate(order):
                value = jnp.where(k == entry, place, value)
            found.append(value)
        return jnp.where(routed, found[0], found[1])

    def block_at(n):
        return listed(BLOCKS, n)

    plans = planned(0), planned(1)
    sequences, leaving, sums_at = zip(*plans)

    def place_of(k):
        return placed(sequences, k)

    def late(a):
        return listed(YFIRST, a)

    def sum_at(t):
        return jnp.where((t >= 0) & (t < len(sums_at[0])), listed(sums_at, t), -1)

    def early(b):
        return jnp.where(routed, EARLY[0][b], EARLY[1][b])

    def early_begin(b):
        return jnp.where(routed, EARLY_BEGIN[0][b], EARLY_BEGIN[1][b])

    def core_copy(k):
        slot = lax.rem(place_of(k), RING)
        return remote(r.part.at[:, :, 1 - c, strip(k), :], r.core_in.at[slot], r.core_sem, (k,), sibling)

    def side_copy(a):
        return remote(r.part.at[:, 1 - y, c, strip(late(a)), :], r.side_in.at[:, strip(a), :], r.side_sem, (a,), beside)

    def up_send(s, a):
        return remote(
            r.part.at[s, y, c, strip(late(a)), :], r.up_in.at[s - z - 1, strip(a), :], r.up_sem, (s, a), above
        )

    def up_take(s, a):
        return remote(r.part.at[s, y, c, strip(late(a)), :], r.up_in.at[s - z, strip(a), :], r.up_sem, (s, a), below)

    def down_send(s, a):
        return remote(
            r.part.at[s, y, c, strip(late(a)), :], r.down_in.at[z - 1 - s, strip(a), :], r.down_sem, (s, a), below
        )

    def down_take(s, a):
        return remote(
            r.part.at[s, y, c, strip(late(a)), :], r.down_in.at[z - s, strip(a), :], r.down_sem, (s, a), above
        )

    def early_rows(b):
        return strip(early(b))

    def early_up_send(s, b):
        return remote(
            r.part.at[s, :, c, early_rows(b), :], r.early_up.at[b, s - z - 1], r.early_sem, (0, s, b), above
        )

    def early_up_take(s, b):
        return remote(r.part.at[s, :, c, early_rows(b), :], r.early_up.at[b, s - z], r.early_sem, (0, s, b), below)

    def early_down_send(s, b):
        return remote(
            r.part.at[s, :, c, early_rows(b), :], r.early_down.at[b, z - 1 - s], r.early_sem, (1, s, b), below
        )

    def early_down_take(s, b):
        return remote(r.part.at[s, :, c, early_rows(b), :], r.early_down.at[b, z - s], r.early_sem, (1, s, b), above)

    def early_side(b):
        return remote(
            r.part.at[z, 1 - y, c, early_rows(b), :], r.early_side.at[b], r.early_side_sem, (b,), beside
        )

    def small_copy(k):
        device = (sibling, beside, paired, far)[k]
        return remote(r.small.at[k], r.small_in.at[k], r.small_sem, (k,), device)

    def across():
        return remote(r.small.at[4], r.cross_in, r.cross_sem, (), {"section": 1})

    s = Refs((), (), dict(r.__dict__, gl=r.grad_mixed, du=r.slope, v_back=r.da))
    v_out = r.v_down.at[pl.ds(0, D), :]
    v_qkv = r.v_up.at[:, pl.ds(0, 3 * D)]
    bounds = [r.bounds[0, k] for k in range(5)]

    def load(k, source, target):
        return pltpu.make_async_copy(source, target, r.sems.at[k])

    first = [load(0, r.back, r.da), load(1, r.st_x, r.x_low), load(2, r.st_branch, r.v_part)]
    middle = [load(12, r.st_hidden, r.hidden), load(13, r.st_qkv, r.qkv), load(14, r.st_lse, r.lse_rows)]
    again = [load(15, r.w_out, v_out), load(16, r.w_qkv, v_qkv)]
    feed_in = [load(3, r.w_down, r.v_down), load(4, r.st_slope, r.slope), load(5, r.w_up, r.v_up)]
    part_out = load(17, r.v_part, r.part_rows)

    def each(copies, act):
        for copy in copies:
            getattr(copy, act)()

    def thirds(target, left, right):
        def one(j, _):
            cols = pl.ds(pl.multiple_of(j * 256, 256), 256)
            target[:, cols] = mm_t(left[...], right[cols, :])
            return 0

        lax.fori_loop(0, 3, one, 0)

    def phase_feed():
        each(feed_in, "wait")

        def one(j, _):
            cols = pl.ds(pl.multiple_of(j * CHUNK, CHUNK), CHUNK)
            grad = mm_t(s.gl[...], r.v_down[cols, :])
            for start in range(0, CAPACITY, BLOCK):
                slope = r.slope[start : start + BLOCK, cols].astype(f32)
                r.slope[start : start + BLOCK, cols] = (grad[start : start + BLOCK, :] * slope).astype(bf16)
            return 0

        lax.fori_loop(0, 4, one, 0)
        thirds(r.low, s.du, r.v_up)
        each(again, "start")

    def phase_norm():
        each(middle, "wait")
        norm_two_backward(CAPACITY, r.gain[1:2, :], s)
        again[0].wait()
        r.grad_mixed[...] = mm_t(r.da[...], v_out[...]).astype(bf16)

    def phase_window(*kinds):
        windows = [FIXED_WINDOWS[kind] for kind in kinds]
        attention_backward(windows, bounds, r.qkv, r.grad_mixed, r.lse_rows, r.grad_qkv, True)

    def phase_last():
        again[1].wait()
        thirds(r.low, r.grad_qkv, v_qkv)
        norm_one_backward(CAPACITY, r.x_low, r.gain[0:1, :], s)

        def join(rows):
            r.v_part[rows, :] += r.grad[rows, :]

        rows_loop(CAPACITY, join, True)
        part_out.start()

    def slot_pair(b):
        left = jnp.where(b < 3, SLOT_N1, jnp.where(b == 3, SLOT_MIXED, jnp.where(b < 8, SLOT_N2, b - 8 + SLOT_ACT)))
        right = jnp.where(b < 3, b + SLOT_DQKV, jnp.where(b == 3, SLOT_DA, jnp.where(b < 8, b - 4 + SLOT_DU, SLOT_GL)))
        return left, right

    def operand_copies(n, left_rows, right_rows):
        left, right = slot_pair(block_at(n))
        side = lax.rem(n, 2)
        return (
            pltpu.make_async_copy(r.ops.at[left, 0:left_rows, :], r.left.at[side, 0:left_rows, :], r.load_sem.at[0, side]),
            pltpu.make_async_copy(
                r.ops.at[right, 0:right_rows, :], r.right.at[side, 0:right_rows, :], r.load_sem.at[1, side]
            ),
        )

    def operands(n, act):
        pl.when(routed)(lambda: each(operand_copies(n, 2 * CAPACITY, CAPACITY), act))
        pl.when(full)(lambda: each(operand_copies(n, 2 * FULL, 2 * FULL), act))

    def block(n):
        side = lax.rem(n, 2)
        b = block_at(n)
        operands(n, "wait")
        pl.when(n + 1 < STRIPS)(lambda: operands(n + 1, "start"))
        second = pl.ds(CAPACITY, CAPACITY)

        @pl.when(routed)
        def _():
            @pl.when(b >= 8)
            def _():
                r.right[side, second, :] = s.gl[...]

            @pl.when((b >= 4) & (b < 8))
            def _():
                r.right[side, second, :] = s.du[:, pl.ds(pl.multiple_of((b - 4) * D, D), D)]

            @pl.when(b == 3)
            def _():
                r.right[side, second, :] = r.da[...]

            @pl.when(b < 3)
            def _():
                r.right[side, second, :] = r.grad_qkv[:, pl.ds(pl.multiple_of(b * D, D), D)]

        def multiply(rows):
            def half(h, _):
                cols = pl.ds(pl.multiple_of(h * 384, 384), 384)
                product = t_mm(r.left[side, 0:rows, cols], r.right[side, 0:rows, :]).astype(bf16)

                @pl.when(b < 8)
                def _():
                    r.part[pl.ds(2 * h, 2), :, :, strip(b), :] = product.reshape(2, 2, 2, STRIP, D)

                @pl.when(b >= 8)
                def _():
                    r.part[b - 8, h, :, 384:576, :] = product.reshape(2, 192, D)

                return 0

            lax.fori_loop(0, 2, half, 0)

        pl.when(routed)(lambda: multiply(2 * CAPACITY))
        pl.when(full)(lambda: multiply(2 * FULL))

    def core_start(k):
        n = place_of(k)
        pl.when(n >= RING)(lambda: pl.semaphore_wait(r.free_sem.at[lax.rem(n, RING)], 1))
        core_copy(k).start()

    def add_into(target, source):
        (a, ia), (b, ib) = target, source
        a[ia] = (a[ia].astype(f32) + b[ib].astype(f32)).astype(bf16)

    def write(k, value):
        @pl.when(k < 3)
        def _():
            r.g_qkv[:, pl.ds(pl.multiple_of(k * D, D), D)] = value

        @pl.when(k == 3)
        def _():
            r.g_out[...] = value

        @pl.when((k > 3) & (k < 8))
        def _():
            r.g_up[:, pl.ds(pl.multiple_of((k - 4) * D, D), D)] = value

        @pl.when(k >= 8)
        def _():
            r.g_down[strip(k - 8), :] = value

    def core_arrived(k):
        n = place_of(k)
        slot = lax.rem(n, RING)
        core_copy(k).wait_recv()

        def one(i, _):
            zs, ys = i // 2, lax.rem(i, 2)
            add_into((r.part, (zs, ys, c, strip(k))), (r.core_in, (slot, zs, ys)))
            return 0

        lax.fori_loop(0, 8, one, 0)

        @pl.when(n + RING < STRIPS)
        def _():
            pl.semaphore_signal(r.free_sem.at[slot], inc=1, device_id=sibling, device_id_type=MESH_ID)

    def early_strip(b, t):
        rows, begin = early_rows(b), early_begin(b)
        pl.when(t == begin)(lambda: core_arrived(early(b)))

        @pl.when((t == begin + 2 * z) & (z < 3))
        def _():
            def one(i, _):
                k = 3 - i

                @pl.when(z > 0)
                def _():
                    early_up_take(k, b).wait_recv()
                    for ys in range(2):
                        add_into((r.part, (k, ys, c, rows)), (r.early_up, (b, k - z, ys)))

                early_up_send(k, b).start()
                return 0

            lax.fori_loop(0, 3 - z, one, 0)

        @pl.when((t == begin + 6 - 2 * z) & (z > 0))
        def _():
            def one(k, _):
                @pl.when(z < 3)
                def _():
                    early_down_take(k, b).wait_recv()
                    for ys in range(2):
                        add_into((r.part, (k, ys, c, rows)), (r.early_down, (b, z - k, ys)))

                early_down_send(k, b).start()
                return 0

            lax.fori_loop(0, z, one, 0)

        @pl.when(t == begin + 8)
        def _():
            @pl.when(z > 0)
            def _():
                early_up_take(z, b).wait_recv()
                for ys in range(2):
                    add_into((r.part, (z, ys, c, rows)), (r.early_up, (b, 0, ys)))

            @pl.when(z < 3)
            def _():
                early_down_take(z, b).wait_recv()
                for ys in range(2):
                    add_into((r.part, (z, ys, c, rows)), (r.early_down, (b, 0, ys)))

            early_side(b).start()

        @pl.when(t == begin + 10)
        def _():
            early_side(b).wait_recv()
            write(early(b), r.part[z, y, c, rows, :].astype(f32) + r.early_side[b].astype(f32))

    def serve(t):
        turn = jnp.minimum(t + 1, len(YCOUNT[0]) - 1)
        many = jnp.where(t + 1 < len(YCOUNT[0]), listed(YCOUNT, turn), 0)
        start = listed(tuple(running(counts) for counts in YCOUNT), turn)

        def set_out(i, _):
            core_arrived(late(start + i))
            side_copy(start + i).start()
            return 0

        lax.fori_loop(0, many, set_out, 0)
        for b in range(HASTE):
            early_strip(b, t)

        a_sum = sum_at(t)

        @pl.when(a_sum >= 0)
        def _():
            a = a_sum
            side_copy(a).wait_recv()

            def one(zs, _):
                add_into((r.part, (zs, y, c, strip(late(a)))), (r.side_in, (zs, strip(a))))
                return 0

            lax.fori_loop(0, 4, one, 0)

        au = sum_at(t - 2 * z)

        @pl.when((au >= 0) & (z < 3))
        def _():
            def one(i, _):
                k = 3 - i

                @pl.when(z > 0)
                def _():
                    up_take(k, au).wait_recv()
                    add_into((r.part, (k, y, c, strip(late(au)))), (r.up_in, (k - z, strip(au))))

                up_send(k, au).start()
                return 0

            lax.fori_loop(0, 3 - z, one, 0)

        ad = sum_at(t - 6 + 2 * z)

        @pl.when((ad >= 0) & (z > 0))
        def _():
            def one(k, _):
                @pl.when(z < 3)
                def _():
                    down_take(k, ad).wait_recv()
                    add_into((r.part, (k, y, c, strip(late(ad)))), (r.down_in, (z - k, strip(ad))))

                down_send(k, ad).start()
                return 0

            lax.fori_loop(0, z, one, 0)

        a_final = sum_at(t - 6)

        @pl.when(a_final >= 0)
        def _():
            a = a_final
            r.final[...] = r.part[z, y, c, strip(late(a)), :].astype(f32)

            @pl.when(z > 0)
            def _():
                up_take(z, a).wait_recv()
                r.final[...] += r.up_in[0, strip(a), :].astype(f32)

            @pl.when(z < 3)
            def _():
                down_take(z, a).wait_recv()
                r.final[...] += r.down_in[0, strip(a), :].astype(f32)

            write(late(a), r.final[...])

        @pl.when(t == PHASES[-1] + 1)
        def _():
            pl.when(full)(lambda: copy_sums())
            for k in range(6):
                rows = slice(8 * k, 8 * k + 8)
                r.small[0, k : k + 1, :] = jnp.sum(r.sums_a[rows, :] + r.sums[rows, :], axis=0, keepdims=True)
            r.small[0, 6:8, :] = jnp.zeros((2, D), f32)
            small_copy(0).start()

        for k in range(4):

            @pl.when(t == 2 * k + PHASES[-1] + 3)
            def _():
                small_copy(k).wait_recv()
                r.small[k + 1] = r.small[k] + r.small_in[k]
                if k < 3:
                    small_copy(k + 1).start()
                else:
                    pl.when(routed)(lambda: across().start())

    def copy_sums():
        r.sums[...] = r.sums_b[...]

    @pl.when(routed)
    def _():
        each(first, "start")

    operands(zero, "start")

    @pl.when(routed)
    def _():
        each(feed_in + middle, "start")
        each(first, "wait")
        gates_backward(s, bounds, True)

        def one(rows):
            s.gl[rows, :] = r.grad[rows, :].astype(bf16)

        rows_loop(CAPACITY, one, True)

    pl.semaphore_wait(barrier, 3 + (z > 0).astype(i32) + (z < 3).astype(i32) + routed.astype(i32))

    def step(turn, _):
        t = turn - 1
        serve(t)
        index = jnp.minimum(turn, len(AMOUNTS[0]) - 1)
        begin = listed(tuple(running(amounts) for amounts in AMOUNTS), index)
        amount = jnp.where(turn < len(AMOUNTS[0]), listed(AMOUNTS, index), 0)
        lax.fori_loop(0, amount, lambda i, _: (block(begin + i), 0)[1], 0)
        index = jnp.minimum(turn, len(leaving[0]) - 1)
        begin_core = listed(tuple(running(counts) for counts in leaving), index)
        amount = jnp.where(turn < len(leaving[0]), listed(leaving, index), 0)
        lax.fori_loop(0, amount, lambda i, _: (core_start(listed(sequences, begin_core + i)), 0)[1], 0)
        pl.when(routed & (t == PHASES[0]))(phase_feed)
        pl.when(routed & (t == PHASES[1]))(phase_norm)
        pl.when(routed & (t == PHASES[2]))(lambda: phase_window(0, 2))
        pl.when(routed & (t == PHASES[3]))(lambda: phase_window(1))
        pl.when(routed & (t == PHASES[4]))(phase_last)
        return 0

    lax.fori_loop(0, 19, step, 0)
    r.small_out[...] = r.small[4]


    @pl.when(routed)
    def _():
        across().wait_send()
        part_out.wait()

    @pl.when(full)
    def _():
        across().wait_recv()
        r.small_out[4:6, :] = r.cross_in[4:6, :]


    lax.fori_loop(0, STRIPS, lambda k, _: (core_copy(k).wait_send(), 0)[1], 0)

    def drain(a, _):
        side_copy(a).wait_send()
        for k in range(1, 4):
            pl.when(k > z)(lambda k=k: up_send(k, a).wait_send())
        for k in range(3):
            pl.when(k < z)(lambda k=k: down_send(k, a).wait_send())
        return 0

    lax.fori_loop(0, LATE, drain, 0)
    for b in range(HASTE):
        early_side(b).wait_send()
        for k in range(1, 4):
            pl.when(k > z)(lambda k=k: early_up_send(k, b).wait_send())
        for k in range(3):
            pl.when(k < z)(lambda k=k: early_down_send(k, b).wait_send())
    for k in range(4):
        small_copy(k).wait_send()


HBM = pl.ANY
VMEM = pltpu.VMEM
SMEM = pltpu.SMEM


def body(
    tokens, layout, selected, cotangent, w_qkv, w_out, w_up, w_down, norm_gain, norm_bias, w_router
):
    ways = lax.axis_size("dp")
    common = dict(
        layout=(layout, SMEM),
        chosen=(selected, VMEM),
        gain=(norm_gain[0], VMEM),
        bias=(norm_bias[0], VMEM),
        router=(w_router, VMEM),
        w_qkv=(w_qkv[0], HBM),
        w_out=(w_out[0], HBM),
        w_up=(w_up[0], HBM),
        w_down=(w_down[0], HBM),
    )
    tokens = jnp.transpose(tokens, (1, 2, 0, 3)).reshape(ROW_LEN, 2, D)
    cotangent = jnp.transpose(cotangent, (1, 2, 0, 3)).reshape(ROW_LEN, 2, D)
    ops_spec = ((SLOTS, 2 * FULL, D), bf16, HBM)
    acts_spec = ((ROW_LEN, 2, D), bf16, HBM)
    grads_spec = ((2, ROW_LEN, 1, D), f32, HBM)
    stash_spec = dict(
        st_x=((CAPACITY, D), bf16, HBM, None),
        st_qkv=((CAPACITY, 3 * D), bf16, HBM, None),
        st_slope=((CAPACITY, FF), bf16, HBM, None),
        st_hidden=((CAPACITY, D), f32, HBM, None),
        st_branch=((CAPACITY, D), f32, HBM, None),
        st_lse=((16, CAPACITY), f32, HBM, None),
        bounds=((1, 8), i32, SMEM, None),
    )
    laid_spec = dict(
        x_rest=((2, FULL, D), bf16, HBM, None),
        cot=((2, FULL, D), bf16, HBM, None),
        slot_picks=((2, CAPACITY, FULL), bf16, HBM, None),
        spread=((2, FULL, CAPACITY), bf16, HBM, None),
        spares=((2, SPARE, FULL), bf16, HBM, None),
    )
    buffers = dict(sems=pltpu.SemaphoreType.DMA((40,)), **weight_scratch())
    ops = None
    handed, stashes, picks, y0ps = [], [], [], []
    for mb in range(2):
        inputs = dict(common, tokens=(tokens, HBM), cotangent=(cotangent, HBM))
        outputs = dict(
            ops=ops_spec + ("ops_old" if mb else None,), y0p=((CAPACITY, D), bf16, HBM, None), **stash_spec
        )
        scratch = dict(
            **buffers,
            pair=pltpu.VMEM((ROW_LEN, 2, D), bf16),
            flat=pltpu.VMEM((PAIR, D), bf16),
            v_picks=pltpu.VMEM((CAPACITY, PAIR), bf16),
            x=pltpu.VMEM((CAPACITY, D), f32),
            x_low=pltpu.VMEM((CAPACITY, D), bf16),
            lse_rows=pltpu.VMEM((16, CAPACITY), f32),
            y_low=pltpu.VMEM((CAPACITY, D), bf16),
            **forward_scratch(CAPACITY),
            **shared_scratch(CAPACITY),
        )
        outputs.update(picks_out=((CAPACITY, PAIR), bf16, HBM, None))
        if mb == 0:
            outputs.update(laid_spec)
            scratch.update(
                flat_two=pltpu.VMEM((PAIR, D), bf16),
                v_x=pltpu.VMEM((2, FULL, D), bf16),
                v_cot=pltpu.VMEM((2, FULL, D), bf16),
                v_slot_picks=pltpu.VMEM((2, CAPACITY, FULL), bf16),
                v_spread=pltpu.VMEM((2, FULL, CAPACITY), bf16),
                v_spares=pltpu.VMEM((2, SPARE, FULL), bf16),
            )
        else:
            inputs.update(ops_old=(ops, HBM))
        found = launch(
            functools.partial(routed_forward_kernel, mb), inputs, outputs, scratch, f"routed_forward_{mb}", 6 * 10**9
        )
        ops, y0p = found["ops"], found["y0p"]
        if mb == 0:
            laid = {name: (found[name], HBM) for name in laid_spec}
        picks.append(found["picks_out"])
        y0ps.append(y0p)
        stashes.append({name: (found[name], SMEM if name == "bounds" else HBM) for name in stash_spec})
        handed.append(lax.ppermute(y0p, "section", [(0, 1)]))
    acts = launch(
        routed_outputs_kernel,
        dict(
            tokens=(tokens, HBM), picks_a=(picks[0], HBM), picks_b=(picks[1], HBM), y_a=(y0ps[0], HBM), y_b=(y0ps[1], HBM)
        ),
        dict(acts=acts_spec + (None,)),
        dict(
            sems=pltpu.SemaphoreType.DMA((8,)),
            pair=pltpu.VMEM((ROW_LEN, 2, D), bf16),
            flat=pltpu.VMEM((PAIR, D), bf16),
            v_picks=pltpu.VMEM((2, CAPACITY, PAIR), bf16),
            v_y=pltpu.VMEM((2, CAPACITY, D), bf16),
        ),
        "routed_outputs",
        10**9,
    )["acts"]
    sums, returned, ends = [], [], []
    for mb in range(2):
        outputs = dict(
            ops=ops_spec + ("ops_old",),
            sent=((FULL if mb == 0 else CAPACITY, D), bf16, HBM, None),
            y1=((FULL, D), bf16, HBM, None),
            dx=((FULL, D), f32, HBM, None),
            sums_out=((48, D), f32, HBM, None),
        )
        found = launch(
            functools.partial(full_kernel, mb),
            dict(common, **laid, y0p=(handed[mb], HBM), ops_old=(ops, HBM)),
            outputs,
            dict(
                **buffers,
                tok=pltpu.VMEM((FULL, D), bf16),
                x=pltpu.VMEM((FULL, D), f32),
                low_in=pltpu.VMEM((CAPACITY, D), bf16),
                v_spread=pltpu.VMEM((FULL, CAPACITY), bf16),
                v_picks=pltpu.VMEM((CAPACITY, FULL), bf16),
                v_spares=pltpu.VMEM((SPARE, FULL), bf16),
                high=pltpu.VMEM((FULL, D), bf16),
                v_sent=pltpu.VMEM((CAPACITY, D), bf16),
                v_sent_spares=pltpu.VMEM((SPARE, D), bf16),
                **forward_scratch(FULL),
                **shared_scratch(FULL),
                **backward_scratch(FULL),
            ),
            f"full_{mb}",
            20 * 10**9,
        )
        ops = found["ops"]
        sums.append(found["sums_out"])
        ends.append((found["y1"], found["dx"]))
        returned.append(lax.ppermute(found["sent"], "section", [(1, 0)]))
    for mb in range(1 if ways == 16 else 2):
        inputs = dict(
            common, back=(returned[mb], HBM), **stashes[mb], ops_old=(ops, HBM), sums_old=(sums[mb], HBM)
        )
        outputs = dict(ops=ops_spec + ("ops_old",), sums_out=((48, D), f32, HBM, "sums_old"))
        scratch = dict(
            **buffers,
            x_low=pltpu.VMEM((CAPACITY, D), bf16),
            v_back=pltpu.VMEM((CAPACITY, D), bf16),
            v_part=pltpu.VMEM((CAPACITY, D), f32),
            lse_rows=pltpu.VMEM((16, CAPACITY), f32),
            **shared_scratch(CAPACITY),
            **backward_scratch(CAPACITY),
        )
        if mb == 0:
            outputs.update(grads=grads_spec + (None,))
            scratch.update(v_spares=pltpu.VMEM((SPARE, D), bf16), row=pltpu.VMEM((ROW_LEN, 1, D), f32))
        else:
            outputs.update(part=((CAPACITY, D), f32, HBM, None))
        found = launch(
            functools.partial(routed_backward_kernel, mb), inputs, outputs, scratch, f"routed_backward_{mb}", 7 * 10**9
        )
        ops, sums[mb] = found["ops"], found["sums_out"]
        if mb == 0:
            grads = found["grads"]
            ends = launch(
                full_outputs_kernel,
                dict(
                    layout=(layout, SMEM), chosen=(selected, VMEM), y1_a=(ends[0][0], HBM), y1_b=(ends[1][0], HBM),
                    dx_a=(ends[0][1], HBM), dx_b=(ends[1][1], HBM), acts_old=(acts, HBM), grads_old=(grads, HBM),
                ),
                dict(
                    acts=acts_spec + ("acts_old",), grads=grads_spec + ("grads_old",),
                    sent_spares=((SPARE, D), bf16, HBM, None),
                ),
                dict(
                    sems=pltpu.SemaphoreType.DMA((16,)),
                    v_spares=pltpu.VMEM((SPARE, D), bf16),
                    v_dx_a=pltpu.VMEM((FULL, D), f32),
                    v_dx_b=pltpu.VMEM((FULL, D), f32),
                    v_y1=pltpu.VMEM((2, FULL, D), bf16),
                    pair=pltpu.VMEM((ROW_LEN, 2, D), bf16),
                    row=pltpu.VMEM((ROW_LEN, 1, D), f32),
                    row_two=pltpu.VMEM((ROW_LEN, 1, D), f32),
                ),
                "full_outputs",
                4 * 10**9,
            )
            acts, grads = ends["acts"], ends["grads"]
            back_spares = lax.ppermute(ends["sent_spares"], "section", [(1, 0)])
    if ways == 16:
        shares, small, rows = summed_by_kernel(ops, sums, dict(common, back=(returned[1], HBM), **stashes[1]))
    else:
        rows = found["part"]
        shares, small = summed_by_collectives(ops, sums, ways)
    found = launch(
        closing_kernel,
        dict(
            small=(small, VMEM), rows=(rows, VMEM), back_spares=(back_spares, VMEM), grads_old=(grads, HBM),
            layout=(layout, SMEM), chosen=(selected, VMEM),
            **{"g_" + name: (share, VMEM) for name, share in shares.items()},
        ),
        dict(
            grads=grads_spec + ("grads_old",),
            o_gain=((2, D // ways), f32, VMEM, None),
            o_bias=((2, D // ways), f32, VMEM, None),
            o_router=((D,), f32, VMEM, None),
            o_counts=((2,), i32, SMEM, None),
            **{"o_" + name: (share.shape, f32, VMEM, None) for name, share in shares.items()},
        ),
        dict(sems=pltpu.SemaphoreType.DMA((4,)), row=pltpu.VMEM((ROW_LEN, 1, D), f32)),
        "closing",
        10**9,
        ways=ways,
    )
    return (
        jnp.transpose(acts.reshape(1, ROW_LEN, 2, D), (2, 0, 1, 3))[None],
        found["grads"].reshape(1, 2, 1, ROW_LEN, D),
        found["o_qkv"][None],
        found["o_out"][None],
        found["o_up"][None],
        found["o_down"][None],
        found["o_gain"][None],
        found["o_bias"][None],
        found["o_router"],
        found["o_counts"],
    )


def summed_by_kernel(ops, sums, routed):
    found = launch(
        gradient_kernel,
        dict(routed, ops=(ops, HBM), sums_a=(sums[0], VMEM), sums_b=(sums[1], VMEM)),
        dict(
            g_qkv=((STRIP, 3 * D), f32, VMEM, None),
            g_out=((STRIP, D), f32, VMEM, None),
            g_up=((STRIP, FF), f32, VMEM, None),
            g_down=((4 * STRIP, D), f32, VMEM, None),
            small_out=((8, D), f32, VMEM, None),
            part_rows=((CAPACITY, D), f32, HBM, None),
        ),
        dict(
            left=pltpu.VMEM((2, 2 * FULL, D), bf16),
            right=pltpu.VMEM((2, 2 * FULL, D), bf16),
            part=pltpu.VMEM((4, 2, 2, SHARD_ROWS, D), bf16),
            core_in=pltpu.VMEM((RING, 4, 2, STRIP, D), bf16),
            side_in=pltpu.VMEM((4, LATE * STRIP, D), bf16),
            up_in=pltpu.VMEM((3, LATE * STRIP, D), bf16),
            down_in=pltpu.VMEM((3, LATE * STRIP, D), bf16),
            early_up=pltpu.VMEM((HASTE, 3, 2, STRIP, D), bf16),
            early_down=pltpu.VMEM((HASTE, 3, 2, STRIP, D), bf16),
            early_side=pltpu.VMEM((HASTE, STRIP, D), bf16),
            final=pltpu.VMEM((STRIP, D), f32),
            small=pltpu.VMEM((5, 8, D), f32),
            small_in=pltpu.VMEM((4, 8, D), f32),
            cross_in=pltpu.VMEM((8, D), f32),
            cross_sem=pltpu.SemaphoreType.DMA((2,)),
            v_up=pltpu.VMEM((D, FF), bf16),
            v_down=pltpu.VMEM((FF, D), bf16),
            x_low=pltpu.VMEM((CAPACITY, D), bf16),
            v_part=pltpu.VMEM((CAPACITY, D), f32),
            lse_rows=pltpu.VMEM((16, CAPACITY), f32),
            **shared_scratch(CAPACITY),
            grad=pltpu.VMEM((CAPACITY, D), f32),
            da=pltpu.VMEM((CAPACITY, D), bf16),
            grad_mixed=pltpu.VMEM((CAPACITY, D), bf16),
            grad_qkv=pltpu.VMEM((CAPACITY, 3 * D), bf16),
            sums=pltpu.VMEM((48, D), f32),
            sems=pltpu.SemaphoreType.DMA((18,)),
            load_sem=pltpu.SemaphoreType.DMA((2, 2)),
            core_sem=pltpu.SemaphoreType.DMA((2, STRIPS)),
            side_sem=pltpu.SemaphoreType.DMA((2, LATE)),
            up_sem=pltpu.SemaphoreType.DMA((2, 4, LATE)),
            down_sem=pltpu.SemaphoreType.DMA((2, 4, LATE)),
            early_sem=pltpu.SemaphoreType.DMA((2, 2, 4, HASTE)),
            early_side_sem=pltpu.SemaphoreType.DMA((2, HASTE)),
            small_sem=pltpu.SemaphoreType.DMA((2, 4)),
            free_sem=pltpu.SemaphoreType.REGULAR((RING,)),
        ),
        "gradients",
        20 * 10**9,
        collective_id=0,
    )
    shares = {name: found["g_" + name] for name in ("qkv", "out", "up", "down")}
    return shares, found["small_out"], found["part_rows"]


def summed_by_collectives(ops, sums, count):
    first = lax.axis_index("section") == 0
    used = jnp.where(first, 2 * CAPACITY, 2 * FULL)
    ops = jnp.where(lax.broadcasted_iota(i32, (1, 2 * FULL, 1), 1) < used, ops, 0)

    def gradient(left, lefts, right, rights):
        a = jnp.concatenate([ops[left + k] for k in range(lefts)], axis=1)
        b = jnp.concatenate([ops[right + k] for k in range(rights)], axis=1)
        return lax.psum_scatter(t_mm(a, b), "dp", scatter_dimension=0, tiled=True)

    shares = dict(
        qkv=gradient(SLOT_N1, 1, SLOT_DQKV, 3),
        out=gradient(SLOT_MIXED, 1, SLOT_DA, 1),
        up=gradient(SLOT_N2, 1, SLOT_DU, 4),
        down=gradient(SLOT_ACT, 4, SLOT_GL, 1),
    )
    small = jnp.sum((sums[0] + sums[1]).reshape(6, 8, D), axis=1)
    small = jnp.concatenate([small, jnp.zeros((2, D), f32)])
    small = lax.psum(small, "dp")
    shared = lax.psum(jnp.where(first, small[4:6], 0.0), "section")
    return shares, jnp.concatenate([small[:4], shared, small[6:]])


def solution(mesh):
    return jax.shard_map(
        body,
        mesh=mesh,
        in_specs=(
            P(None, "dp", None, None),
            P(None, "dp", None),
            P(None, "dp", None),
            P(None, "dp", None, None),
            P("section", None, None),
            P("section", None, None),
            P("section", None, None),
            P("section", None, None),
            P("section", None, None),
            P("section", None, None),
            P(),
        ),
        out_specs=(
            P("section", None, "dp", None, None),
            P("section", None, "dp", None, None),
            P("section", "dp", None),
            P("section", "dp", None),
            P("section", "dp", None),
            P("section", "dp", None),
            P("section", None, "dp"),
            P("section", None, "dp"),
            P(),
            P(),
        ),
        check_vma=False,
    )
```
